256 devices in a mesh: grp: 8 (over x, core), dev: 32 (over y, z).
Axes of the slice: x: 4, y: 4, z: 8, core: 2. Of those that a mesh axis runs over, the one named last changes fastest.
Arguments:
- features: bfloat16 [131072, 128], P(('grp', 'dev')), may hold values from -6 to 6
- hub_list: int32 [256, 4], P(('grp', 'dev')), may hold values from 0 to 511
- send_list: int32 [256, 32, 32], P(('grp', 'dev')), may hold values from 0 to 511
- send_count: int32 [256, 32], P(('grp', 'dev')), may hold values from 1 to 32, as said below
- tile_dst: int32 [256, 32], P(('grp', 'dev')), may hold values from 0 to 3
- tile_src: int32 [256, 32], P(('grp', 'dev')), may hold values from 0 to 19
- tile_count: int32 [256], P(('grp', 'dev')), may hold values from 1 to 32, as said below
- tile_adj: bfloat16 [8192, 128, 128], P(('grp', 'dev')), may hold values from 0 to 1, as said below
- sample_ids: int32 [256, 256], P(('grp', 'dev')), may hold values from 0 to 511
- labels: int32 [131072], P(('grp', 'dev')), may hold values from 0 to 171
- first_self: bfloat16 [128, 512], replicated, may hold values from -0.5 to 0.5
- first_mean: bfloat16 [128, 512], replicated, may hold values from -0.5 to 0.5
- second_self: bfloat16 [512, 172], replicated, may hold values from -0.75 to 0.75
- second_mean: bfloat16 [512, 172], replicated, may hold values from -0.75 to 0.75
Outputs:
- hidden: bfloat16 [131072, 512], P(('grp', 'dev'))
- grad_hidden: float32 [131072, 512], P(('grp', 'dev'))
- loss_value: float32 [], replicated
- grad_first_self: float32 [128, 512], replicated
- grad_first_mean: float32 [128, 512], replicated
- grad_second_self: float32 [512, 172], replicated
- grad_second_mean: float32 [512, 172], replicated
The draws below stay inside these ranges and needn't reach their ends.
Inputs may be any that keep to these rules, and one draw needn't show every extreme that they name: `send_count`: each partition sends exactly 32 rows to at least one peer. `tile_count`: some partition uses all 32 tiles. `tile_adj`: entries are 0 or 1.
All inputs are finite; a program needn't handle non-finite values.
Results may differ from the reference program's by a relative error of at most 0.004.
The reference program's roundings to bfloat16 on the way count: a program that leaves them out, or rounds other values in their place, can miss the bound.
Values may be sent and summed in bfloat16 or wider, within the bound.
No kernel may reach another device: no remote copies, remote signals or barrier semaphores. Data moves between devices by JAX's collectives and lax.ppermute only.
A program may use at most 64 MiB of HBM per device.

```python
import jax
import jax.numpy as jnp
from jax import lax

F = 128
H = 512
C = 172
TILE = 128
NODE_DEV = 512
HUB_DEV = 4
BND_CAP = 32
TILES_DEV = 32
SAMPLE_DEV = 256
NODES = 131072
HUBS = 1024
SRC_ROWS = 2560
SAMPLES = 65536
N_DEV = 32
DEVICES = 256


def draw_send_count(key, part):
    key = jax.random.fold_in(key, 3)
    first_key, second_key = jax.random.split(key)
    counts = jax.random.randint(first_key, (DEVICES, N_DEV), 1, BND_CAP + 1)
    chosen = jax.random.randint(second_key, (DEVICES,), 0, N_DEV)
    position = jnp.arange(N_DEV, dtype=jnp.int32)[None, :]
    return jnp.where(position == chosen[:, None], BND_CAP, counts).astype(jnp.int32)


def draw_tile_count(key, part):
    key = jax.random.fold_in(key, 5)
    first_key, second_key = jax.random.split(key)
    counts = jax.random.randint(first_key, (DEVICES,), max(TILES_DEV // 4, 1), TILES_DEV + 1)
    chosen = jax.random.randint(second_key, (), 0, DEVICES)
    position = jnp.arange(DEVICES, dtype=jnp.int32)
    return jnp.where(position == chosen, TILES_DEV, counts).astype(jnp.int32)


def draw_tile_adj(key, part):
    key = jax.random.fold_in(key, 7)
    first_key, second_key = jax.random.split(key)
    level = jax.random.uniform(first_key, (DEVICES * TILES_DEV, TILE, 1), jnp.float32)
    density = 0.3 * level * level * level
    values = jax.random.uniform(second_key, (DEVICES * TILES_DEV, TILE, TILE), jnp.float32)
    return (values < density).astype(jnp.float32).astype(jnp.bfloat16)


def place_ends(values, own_key, least, largest):
    longest = values.shape.index(max(values.shape))
    spots = []
    for shift in (0, 1):
        where = [jax.random.randint(jax.random.fold_in(own_key, axis), (), 0, length) for axis, length in enumerate(values.shape)]
        where[longest] = (where[longest] + shift) % values.shape[longest]
        spots.append(tuple(where))
    return values.at[spots[0]].set(least).at[spots[1]].set(largest)


def block_levels(stream_key, extent, shards, low, largest):
    def one(axis_at, parts):
        heights = jax.random.uniform(jax.random.fold_in(jax.random.fold_in(stream_key, 6), axis_at), (parts,), jnp.float32, low / len(shards), largest / len(shards))
        return jnp.repeat(jnp.exp(heights), extent[axis_at] // parts).reshape((-1,) + (1,) * (len(extent) - axis_at - 1))

    factor_of = one(*shards[0])
    for cut in shards[1:]:
        factor_of = factor_of * one(*cut)
    return factor_of


def centred(own_key, dims, scale, most, cuts=(), held_as=jnp.bfloat16):
    gain = block_levels(own_key, dims, cuts, -0.22, 0.18) if cuts else 1.0
    drawn = jax.random.normal(own_key, dims, jnp.float32) * scale * gain
    return jnp.minimum(jnp.maximum(drawn, -most), most).astype(held_as)


def setup_inputs(seed: int = 0) -> dict:
    key_list = jax.random.split(jax.random.key(seed), 15)
    features = centred(key_list[0], (NODES, F), 1.0, 6.0, ((0, 256),))
    hub_list = place_ends(jax.random.randint(key_list[1], (DEVICES, HUB_DEV), 0, NODE_DEV), jax.random.fold_in(key_list[1], 1), 0, NODE_DEV - 1).astype(jnp.int32)
    send_list = place_ends(jax.random.randint(key_list[2], (DEVICES, N_DEV, BND_CAP), 0, NODE_DEV), jax.random.fold_in(key_list[2], 1), 0, NODE_DEV - 1).astype(jnp.int32)
    send_count = draw_send_count(jax.random.fold_in(key_list[14], 71), 0)
    tile_dst = place_ends(jax.random.randint(key_list[4], (DEVICES, TILES_DEV), 0, NODE_DEV // TILE), jax.random.fold_in(key_list[4], 1), 0, (NODE_DEV // TILE) - 1).astype(jnp.int32)
    tile_src = place_ends(jax.random.randint(key_list[5], (DEVICES, TILES_DEV), 0, SRC_ROWS // TILE), jax.random.fold_in(key_list[5], 1), 0, (SRC_ROWS // TILE) - 1).astype(jnp.int32)
    tile_count = draw_tile_count(jax.random.fold_in(key_list[14], 71), 0)
    tile_adj = draw_tile_adj(jax.random.fold_in(key_list[14], 71), 0)
    sample_ids = place_ends(jax.random.randint(key_list[8], (DEVICES, SAMPLE_DEV), 0, NODE_DEV), jax.random.fold_in(key_list[8], 1), 0, NODE_DEV - 1).astype(jnp.int32)
    labels = place_ends(jax.random.randint(key_list[9], (NODES,), 0, C), jax.random.fold_in(key_list[9], 1), 0, C - 1).astype(jnp.int32)
    first_self = centred(key_list[10], (F, H), F ** -0.5, 0.5)
    first_mean = centred(key_list[11], (F, H), F ** -0.5, 0.5)
    second_self = centred(key_list[12], (H, C), (H // 9) ** -0.5, 0.75)
    second_mean = centred(key_list[13], (H, C), (H // 9) ** -0.5, 0.75)
    return {"features": features, "hub_list": hub_list, "send_list": send_list, "send_count": send_count, "tile_dst": tile_dst, "tile_src": tile_src, "tile_count": tile_count, "tile_adj": tile_adj, "sample_ids": sample_ids, "labels": labels, "first_self": first_self, "first_mean": first_mean, "second_self": second_self, "second_mean": second_mean}


def degree_rows(adjacent, targets, count):
    def step_fn(total, position):
        term = jnp.sum(adjacent[position].astype(jnp.float32), axis=1)
        term = jnp.where(position < count, term, jnp.zeros_like(term))
        start = targets[position] * TILE
        current = lax.dynamic_slice_in_dim(total, start, TILE, 0)
        return lax.dynamic_update_slice_in_dim(total, current + term, start, 0), None
    total, unused = lax.scan(step_fn, jnp.zeros((NODE_DEV,), jnp.float32), jnp.arange(TILES_DEV, dtype=jnp.int32))
    return total


def aggregate(source, adjacent, targets, anchors, count):
    def step_fn(total, position):
        block = lax.dynamic_slice_in_dim(source, anchors[position] * TILE, TILE, 0)
        term = jnp.dot(adjacent[position], block, preferred_element_type=jnp.float32)
        term = jnp.where(position < count, term, jnp.zeros_like(term))
        start = targets[position] * TILE
        current = lax.dynamic_slice_in_dim(total, start, TILE, 0)
        return lax.dynamic_update_slice_in_dim(total, current + term, start, 0), None
    total, unused = lax.scan(step_fn, jnp.zeros((NODE_DEV, source.shape[1]), jnp.float32), jnp.arange(TILES_DEV, dtype=jnp.int32))
    return total


def scatter_back(upstream, adjacent, targets, anchors, count):
    def step_fn(total, position):
        block = lax.dynamic_slice_in_dim(upstream, targets[position] * TILE, TILE, 0)
        term = lax.dot_general(adjacent[position], block, (((0,), (0,)), ((), ())), preferred_element_type=jnp.float32)
        term = jnp.where(position < count, term, jnp.zeros_like(term))
        start = anchors[position] * TILE
        current = lax.dynamic_slice_in_dim(total, start, TILE, 0)
        return lax.dynamic_update_slice_in_dim(total, current + term, start, 0), None
    total, unused = lax.scan(step_fn, jnp.zeros((SRC_ROWS, upstream.shape[1]), jnp.float32), jnp.arange(TILES_DEV, dtype=jnp.int32))
    return total


def gather_source(stacked, device, hub_rows, send_list, send_count):
    group = device // N_DEV
    member = device % N_DEV
    peer_ids = group * N_DEV + jnp.arange(N_DEV, dtype=jnp.int32)
    row_ids = send_list[peer_ids, member]
    live_slots = jnp.arange(BND_CAP, dtype=jnp.int32)[None, :] < send_count[peer_ids, member][:, None]
    arriving = stacked[peer_ids[:, None], row_ids]
    arriving = jnp.where(live_slots[:, :, None], arriving, jnp.zeros_like(arriving))
    arriving = arriving.reshape(N_DEV * BND_CAP, stacked.shape[2])
    return jnp.concatenate([stacked[device], hub_rows, arriving], 0), peer_ids, row_ids, live_slots


def reference(features, hub_list, send_list, send_count, tile_dst, tile_src, tile_count, tile_adj, sample_ids, labels, first_self, first_mean, second_self, second_mean):
    stacked_input = features.reshape(DEVICES, NODE_DEV, F)
    device_ids = jnp.arange(DEVICES, dtype=jnp.int32)
    hub_feature = stacked_input[device_ids[:, None], hub_list].reshape(HUBS, F)
    adjacency = tile_adj.reshape(DEVICES, TILES_DEV, TILE, TILE)
    stacked_labels = labels.reshape(DEVICES, NODE_DEV)

    def first_layer(device):
        source, peer_ids, row_ids, live_slots = gather_source(stacked_input, device, hub_feature, send_list, send_count)
        degree = degree_rows(adjacency[device], tile_dst[device], tile_count[device])
        floor_deg = jnp.maximum(degree, 1.0)
        mean_rows = (aggregate(source, adjacency[device], tile_dst[device], tile_src[device], tile_count[device]) / floor_deg[:, None]).astype(jnp.bfloat16)
        linear = jnp.dot(stacked_input[device], first_self, preferred_element_type=jnp.float32) + jnp.dot(mean_rows, first_mean, preferred_element_type=jnp.float32)
        return jnp.maximum(linear, 0.0).astype(jnp.bfloat16), mean_rows

    hidden_stack, mean_first = lax.map(first_layer, device_ids)
    hub_hidden = hidden_stack[device_ids[:, None], hub_list].reshape(HUBS, H)

    def second_layer(carry, device):
        grad_stack, hub_grad, sum_self, sum_mean, loss_sum = carry
        source, peer_ids, row_ids, live_slots = gather_source(hidden_stack, device, hub_hidden, send_list, send_count)
        degree = degree_rows(adjacency[device], tile_dst[device], tile_count[device])
        floor_deg = jnp.maximum(degree, 1.0)
        mean_rows = (aggregate(source, adjacency[device], tile_dst[device], tile_src[device], tile_count[device]) / floor_deg[:, None]).astype(jnp.bfloat16)
        own_rows = hidden_stack[device]
        logits = jnp.dot(own_rows, second_self, preferred_element_type=jnp.float32) + jnp.dot(mean_rows, second_mean, preferred_element_type=jnp.float32)
        picked = sample_ids[device]
        classes = stacked_labels[device][picked]
        chosen = logits[picked]
        log_total = jnp.log(jnp.sum(jnp.exp(chosen), axis=1))
        loss_sum = loss_sum + jnp.sum(log_total - jnp.take_along_axis(chosen, classes[:, None], 1)[:, 0])
        softmax_rows = jnp.exp(chosen - log_total[:, None])
        onehot = (classes[:, None] == jnp.arange(C, dtype=jnp.int32)[None, :]).astype(softmax_rows.dtype)
        grad_logits = jnp.zeros((NODE_DEV, C), jnp.float32).at[picked].add((softmax_rows - onehot) / SAMPLES).astype(jnp.bfloat16)
        sum_self = sum_self + jnp.dot(own_rows.T, grad_logits, preferred_element_type=jnp.float32)
        sum_mean = sum_mean + jnp.dot(mean_rows.T, grad_logits, preferred_element_type=jnp.float32)
        direct = jnp.dot(grad_logits, second_self.T, preferred_element_type=jnp.float32)
        grad_mean = (jnp.dot(grad_logits, second_mean.T, preferred_element_type=jnp.float32) / floor_deg[:, None]).astype(jnp.bfloat16)
        spread = scatter_back(grad_mean, adjacency[device], tile_dst[device], tile_src[device], tile_count[device])
        grad_stack = grad_stack.at[device].add(direct + spread[:NODE_DEV])
        hub_grad = hub_grad + spread[NODE_DEV:NODE_DEV + HUBS]
        returned = spread[NODE_DEV + HUBS:].reshape(N_DEV, BND_CAP, H)
        returned = jnp.where(live_slots[:, :, None], returned, jnp.zeros_like(returned))
        grad_stack = grad_stack.at[peer_ids[:, None], row_ids].add(returned)
        return (grad_stack, hub_grad, sum_self, sum_mean, loss_sum), None

    start = (jnp.zeros((DEVICES, NODE_DEV, H), jnp.float32), jnp.zeros((HUBS, H), jnp.float32), jnp.zeros((H, C), jnp.float32), jnp.zeros((H, C), jnp.float32), jnp.zeros((), jnp.float32))
    finish, unused = lax.scan(second_layer, start, device_ids)
    grad_stack, hub_grad, sum_self, sum_mean, loss_sum = finish
    grad_stack = grad_stack.at[device_ids[:, None], hub_list].add(hub_grad.reshape(DEVICES, HUB_DEV, H))
    grad_hidden = grad_stack.reshape(NODES, H)
    hidden = hidden_stack.reshape(NODES, H)
    grad_first = jnp.where(hidden > 0, grad_hidden, jnp.zeros_like(grad_hidden)).astype(jnp.bfloat16)
    grad_first_self = jnp.dot(features.T, grad_first, preferred_element_type=jnp.float32)
    grad_first_mean = jnp.dot(mean_first.reshape(NODES, F).T, grad_first, preferred_element_type=jnp.float32)
    return (hidden, grad_hidden, loss_sum / SAMPLES, grad_first_self, grad_first_mean, sum_self, sum_mean)
```

```python
import functools

import jax
import jax.numpy as jnp
from jax import lax
from jax.experimental import pallas as pl
from jax.experimental.pallas import tpu as pltpu
from jax.sharding import PartitionSpec as P

F32 = jnp.float32
BF16 = jnp.bfloat16
MIB = 1 << 20
TILE = 128
SLOTS = 48
HUB_AT = 32
WEIGHT_AT = 36
CLASS_ROWS = 176
STACK_ROWS = 640


def nn(left, right):
    return jnp.dot(left, right, preferred_element_type=F32)


def nt(left, right):
    return lax.dot_general(left, right, (((1,), (1,)), ((), ())), preferred_element_type=F32)


def tn(left, right):
    return lax.dot_general(left, right, (((0,), (0,)), ((), ())), preferred_element_type=F32)


def split(values):
    high = values.astype(BF16)
    low = (values - high.astype(F32)).astype(BF16)
    return high, low


def kernel_call(body, outs, scratch=(), in_specs=None, limit=24, flops=0, moved=0):
    placed = {} if in_specs is None else {"in_specs": in_specs}
    return pl.pallas_call(
        body,
        out_shape=outs,
        **placed,
        scratch_shapes=list(scratch),
        compiler_params=pltpu.CompilerParams(vmem_limit_bytes=limit * MIB),
        cost_estimate=pl.CostEstimate(flops=flops, bytes_accessed=moved, transcendentals=0),
    )


VM = pl.BlockSpec(memory_space=pltpu.VMEM)
SM = pl.BlockSpec(memory_space=pltpu.SMEM)


def pick_matrix(send_ref, count_ref, hub_ref, pick_ref):
    peers = send_ref.shape[0]
    nodes = pick_ref.shape[1]
    send = jnp.transpose(send_ref[...])
    slot = lax.broadcasted_iota(jnp.int32, send.shape, 0)
    send = jnp.where(slot < count_ref[...], send, -1)
    row = lax.broadcasted_iota(jnp.int32, (SLOTS - HUB_AT, 1), 0)
    hubs = jnp.full((SLOTS - HUB_AT, 1), -1, jnp.int32)
    for k in range(hub_ref.shape[1]):
        hubs = jnp.where(row == k, hub_ref[0, k], hubs)
    lane = lax.broadcasted_iota(jnp.int32, (HUB_AT, nodes), 1)
    lane_hub = lax.broadcasted_iota(jnp.int32, (SLOTS - HUB_AT, nodes), 1)
    hub_part = jnp.where(hubs == lane_hub, 1.0, 0.0).astype(BF16)
    for n in range(peers):
        body = jnp.where(send[:, n : n + 1] == lane, 1.0, 0.0).astype(BF16)
        pick_ref[n * SLOTS : n * SLOTS + HUB_AT, :] = body
        pick_ref[n * SLOTS + HUB_AT : (n + 1) * SLOTS, :] = hub_part


def send_features(features_ref, send_ref, count_ref, hub_ref, out_ref, pick_ref):
    pick_matrix(send_ref, count_ref, hub_ref, pick_ref)
    out_ref[...] = nn(pick_ref[...], features_ref[...]).astype(BF16)


def build_dense(adj_ref, dst_ref, src_ref, count_ref, dense_ref, turned_ref, degree_ref):
    dense_ref[...] = jnp.zeros_like(dense_ref)
    turned_ref[...] = jnp.zeros_like(turned_ref)

    def add(t, carry):
        rows = pl.ds(pl.multiple_of(dst_ref[0, t] * TILE, TILE), TILE)
        columns = pl.ds(pl.multiple_of(src_ref[0, t] * TILE, TILE), TILE)
        tile = adj_ref[t]
        dense_ref[rows, columns] += tile
        turned_ref[columns, rows] += jnp.transpose(tile)
        return carry

    lax.fori_loop(0, count_ref[0], add, 0)
    ones = jnp.ones((dense_ref.shape[1], TILE), BF16)
    degree_ref[...] = jnp.maximum(nn(dense_ref[...], ones), 1.0)


def spread_hubs(arrived_ref, out_ref):
    hubs = out_ref.shape[1]
    rows = arrived_ref.shape[0]
    i = lax.broadcasted_iota(jnp.int32, (hubs, rows), 0)
    j = lax.broadcasted_iota(jnp.int32, (hubs, rows), 1)
    pick = jnp.where(j == (i >> 2) * SLOTS + HUB_AT + (i & 3), 1.0, 0.0).astype(BF16)
    found = nn(pick, arrived_ref[...]).astype(BF16)
    for g in range(out_ref.shape[0]):
        out_ref[g] = found


def assemble(table_ref, own_ref, hub_ref, arrived_ref, lanes):
    own = own_ref.shape[0]
    hubs = hub_ref.shape[0]
    table_ref[0:own, lanes] = own_ref[...]
    table_ref[own : own + hubs, lanes] = hub_ref[...]
    for n in range(arrived_ref.shape[0] // SLOTS):
        at = own + hubs + n * HUB_AT
        table_ref[at : at + HUB_AT, lanes] = arrived_ref[n * SLOTS : n * SLOTS + HUB_AT, :]


def first_mean_rows(
    features_ref, hub_ref, arrived_ref, dense_ref, degree_ref, send_ref, count_ref, hub_list_ref,
    mean_ref, out_ref, table_ref, pick_ref,
):
    assemble(table_ref, features_ref, hub_ref, arrived_ref, slice(0, TILE))
    pick_matrix(send_ref, count_ref, hub_list_ref, pick_ref)
    total = nn(dense_ref[...], table_ref[...])
    mean = (total / degree_ref[...]).astype(BF16)
    mean_ref[...] = mean
    out_ref[...] = nn(pick_ref[...], mean).astype(BF16)


def main_part(
    samples_all,
    features_ref, feature_hub_ref, feature_arrived_ref,
    mean_ref, mean_hub_ref, mean_arrived_ref,
    dense_ref, turned_ref, degree_ref, sample_ref, label_ref,
    first_self_ref, first_mean_ref, second_self_ref, second_mean_ref,
    hidden_ref, base_ref, edge_ref, out_ref,
    table_ref, source_ref, first_ref, self_ref, both_ref, scaled_ref, stack_ref,
):
    nodes, width = hidden_ref.shape
    classes = second_self_ref.shape[1]
    padded = self_ref.shape[1]
    chunks = table_ref.shape[0] // nodes
    hub_rows = feature_hub_ref.shape[0]
    assemble(table_ref, features_ref, feature_hub_ref, feature_arrived_ref, slice(0, TILE))
    assemble(table_ref, mean_ref, mean_hub_ref, mean_arrived_ref, slice(TILE, 2 * TILE))
    first_ref[0:TILE, :] = first_self_ref[...]
    first_ref[TILE : 2 * TILE, :] = first_mean_ref[...]
    self_ref[...] = jnp.zeros_like(self_ref)
    both_ref[...] = jnp.zeros_like(both_ref)
    self_ref[:, 0:classes] = second_self_ref[...]
    both_ref[:, 0:classes] = second_mean_ref[...]
    both_ref[:, padded : padded + classes] = second_mean_ref[...]

    def rows_of(i):
        return pl.ds(pl.multiple_of(i * nodes, nodes), nodes)

    def forward(i, carry):
        rows = rows_of(i)
        linear = nn(table_ref[rows, :], first_ref[...])
        source_ref[rows, :] = jnp.maximum(linear, 0.0).astype(BF16)
        return carry

    lax.fori_loop(0, chunks, forward, 0)
    hidden = source_ref[0:nodes, :]
    hidden_ref[...] = hidden
    degree = degree_ref[:, 0:1]
    mean = (nn(dense_ref[...], source_ref[...]) / degree).astype(BF16)
    logits = nn(hidden, self_ref[...]) + nn(mean, both_ref[:, 0:padded])

    lane = lax.broadcasted_iota(jnp.int32, (nodes, padded), 1)
    real = lane < classes
    node = lax.broadcasted_iota(jnp.int32, (nodes, sample_ref.shape[1]), 0)
    hits = jnp.where(node == sample_ref[...], 1.0, 0.0)
    times = jnp.sum(hits, axis=1, keepdims=True)
    label = jnp.transpose(jnp.broadcast_to(label_ref[...], (8, nodes)))[:, 0:1]
    onehot = jnp.where(lane == label, 1.0, 0.0)
    top = jnp.max(jnp.where(real, logits, -jnp.inf), axis=1, keepdims=True)
    shifted = logits - top
    powers = jnp.where(real, jnp.exp(shifted), 0.0)
    total = jnp.sum(powers, axis=1, keepdims=True)
    chosen = jnp.sum(onehot * shifted, axis=1, keepdims=True)
    loss = jnp.sum(times * (jnp.log(total) - chosen), axis=0, keepdims=True)
    upstream = times * ((powers / total - onehot) / samples_all)
    upstream = upstream.astype(BF16)

    stack_ref[2 * TILE : 2 * TILE + CLASS_ROWS, :] = tn(upstream, hidden)[0:CLASS_ROWS]
    stack_ref[2 * TILE + CLASS_ROWS : 2 * TILE + 2 * CLASS_ROWS, :] = tn(upstream, mean)[0:CLASS_ROWS]
    tail = STACK_ROWS - 2 * TILE - 2 * CLASS_ROWS
    loss_high, loss_low = split(loss)
    place = lax.broadcasted_iota(jnp.int32, (tail, width), 0)
    marks = jnp.where(place == 0, loss_high.astype(F32), 0.0)
    stack_ref[2 * TILE + 2 * CLASS_ROWS :, :] = jnp.where(place == 1, loss_low.astype(F32), marks)

    high, low = split(upstream.astype(F32) / degree)
    scaled_ref[:, 0:padded] = high
    scaled_ref[:, padded : 2 * padded] = low

    def back(rows):
        pair = nn(turned_ref[rows, :], scaled_ref[...])
        high, low = split(pair[:, 0:padded] + pair[:, padded : 2 * padded])
        spread = nt(high, both_ref[:, 0:padded]) + nt(low, both_ref[:, 0:padded])
        return high, spread

    def weights(rows, grad):
        masked = jnp.where(source_ref[rows, :] > 0, grad, 0.0).astype(BF16)
        return tn(table_ref[rows, :], masked)

    own = rows_of(0)
    unused, spread = back(own)
    base = nt(upstream, self_ref[...]) + spread
    base_ref[...] = base
    stack_ref[0 : 2 * TILE, :] = weights(own, base)

    def hub_chunk(i, carry):
        rows = rows_of(i + 1)
        high, spread = back(rows)
        stack_ref[0 : 2 * TILE, :] += weights(rows, spread)
        for part in range(nodes // TILE):
            out_ref[i * (nodes // TILE) + part, 0:TILE, :] = high[part * TILE : (part + 1) * TILE]
        return carry

    lax.fori_loop(0, hub_rows // nodes, hub_chunk, 0)

    def edge_chunk(i, carry):
        rows = rows_of(i + 1 + hub_rows // nodes)
        high, spread = back(rows)
        stack_ref[0 : 2 * TILE, :] += weights(rows, spread)
        edge_ref[rows_of(i), :] = high
        return carry

    lax.fori_loop(0, edge_ref.shape[0] // nodes, edge_chunk, 0)
    groups = out_ref.shape[0]
    share = STACK_ROWS // groups
    for g in range(groups):
        part = stack_ref[g * share : (g + 1) * share, :].astype(BF16)
        out_ref[g, TILE : TILE + share, :] = part[:, 0:padded]
        out_ref[g, TILE + share : TILE + 2 * share, :] = part[:, padded : 2 * padded]


def sum_groups(arrived_ref, edge_ref, out_ref, total_ref, block_ref):
    share = STACK_ROWS // arrived_ref.shape[0]
    total = arrived_ref[0].astype(F32)
    for g in range(1, arrived_ref.shape[0]):
        total += arrived_ref[g].astype(F32)
    total_ref[...] = total
    block_ref[...] = jnp.zeros_like(block_ref)
    peers = out_ref.shape[0] // SLOTS
    hubs = TILE // peers
    piece = share // (peers // 4)
    lanes = out_ref.shape[1] // 2
    for n in range(peers):
        i, j = n // 4, n % 4
        at = TILE + (j // 2) * share + piece * i
        block_ref[n, 0:hubs, :] = total_ref[hubs * n : hubs * (n + 1), :]
        part = total_ref[at : at + piece, (j % 2) * lanes : (j % 2 + 1) * lanes]
        high = part.astype(BF16).astype(F32)
        block_ref[n, hubs : hubs + piece, 0:lanes] = high
        block_ref[n, hubs : hubs + piece, lanes : 2 * lanes] = part - high
        out_ref[n * SLOTS : n * SLOTS + HUB_AT, :] = edge_ref[n * HUB_AT : (n + 1) * HUB_AT, :]
        out_ref[n * SLOTS + HUB_AT : (n + 1) * SLOTS, :] = block_ref[n].astype(BF16)


def sum_peers(arrived_ref, out_ref):
    peers = out_ref.shape[0]
    lanes = out_ref.shape[2]
    total = jnp.zeros((SLOTS - HUB_AT, 2 * lanes), F32)
    for n in range(peers):
        total += arrived_ref[n * SLOTS + HUB_AT : (n + 1) * SLOTS, :].astype(F32)
    own = total[:, 0:lanes] + total[:, lanes : 2 * lanes]
    for n in range(peers):
        out_ref[n] = own


def join_pieces(arrived_ref, out_ref, whole_ref):
    peers = arrived_ref.shape[0]
    share = out_ref.shape[1]
    piece = share // (peers // 4)
    lanes = arrived_ref.shape[2]
    at = WEIGHT_AT - HUB_AT
    for n in range(peers):
        i, j = n // 4, n % 4
        whole_ref[piece * i : piece * (i + 1), lanes * j : lanes * (j + 1)] = arrived_ref[n, at : at + piece, :]
    whole = whole_ref[...]
    for g in range(out_ref.shape[0]):
        out_ref[g] = whole


def weight_outputs(samples_all, stack_ref, first_self_ref, first_mean_ref, self_ref, mean_ref, loss_ref):
    classes = self_ref.shape[1]
    first_self_ref[...] = stack_ref[0:TILE, :]
    first_mean_ref[...] = stack_ref[TILE : 2 * TILE, :]
    at = 2 * TILE
    self_ref[...] = jnp.transpose(stack_ref[at : at + CLASS_ROWS, :])[:, 0:classes]
    at += CLASS_ROWS
    mean_ref[...] = jnp.transpose(stack_ref[at : at + CLASS_ROWS, :])[:, 0:classes]
    at += CLASS_ROWS
    loss_ref[...] = (stack_ref[at : at + 1, 0:1] + stack_ref[at + 1 : at + 2, 0:1]) / samples_all


def return_rows(base_ref, arrived_ref, send_ref, count_ref, hub_ref, mean_ref, out_ref, pick_ref, padded_ref):
    pick_matrix(send_ref, count_ref, hub_ref, pick_ref)
    padded_ref[...] = jnp.zeros_like(padded_ref)
    padded_ref[:, 0 : mean_ref.shape[1]] = mean_ref[...]
    high, low = split(tn(pick_ref[...], arrived_ref[...]))
    out_ref[...] = base_ref[...] + nt(high, padded_ref[...]) + nt(low, padded_ref[...])


def shape(dims, dtype):
    return jax.ShapeDtypeStruct(dims, dtype)


def swap(values, axis):
    return lax.all_to_all(values, axis, split_axis=0, concat_axis=0, tiled=True)


def on_device(
    features,
    hub_list,
    send_list,
    send_count,
    tile_dst,
    tile_src,
    tile_count,
    tile_adj,
    sample_ids,
    labels,
    first_self,
    first_mean,
    second_self,
    second_mean,
):
    nodes, inputs = features.shape
    width, classes = second_self.shape
    groups = lax.axis_size("grp")
    peers = lax.axis_size("dev")
    sends = send_list[0]
    capacity = sends.shape[1]
    group_hubs = peers * hub_list.shape[1]
    hubs = groups * group_hubs
    table = nodes + hubs + peers * capacity
    slots = peers * SLOTS
    padded = 2 * TILE
    samples_all = float(sample_ids.shape[1] * groups * peers)
    pick = pltpu.VMEM((slots, nodes), BF16)

    rows = kernel_call(
        send_features, shape((slots, inputs), BF16), [pick], [VM, VM, VM, SM]
    )(features, sends, send_count, hub_list)
    feature_arrived = swap(rows.reshape(peers, SLOTS, inputs), "dev").reshape(slots, inputs)

    dense, turned, degree = kernel_call(
        build_dense,
        (shape((nodes, table), BF16), shape((table, nodes), BF16), shape((nodes, TILE), F32)),
        in_specs=[VM, SM, SM, SM],
        flops=2 * nodes * table * TILE,
        moved=8 * MIB,
    )(tile_adj, tile_dst, tile_src, tile_count)

    gather_hubs = kernel_call(spread_hubs, shape((groups, group_hubs, inputs), BF16))
    feature_hubs = swap(gather_hubs(feature_arrived), "grp").reshape(hubs, inputs)
    mean_rows, rows = kernel_call(
        first_mean_rows,
        (shape((nodes, inputs), BF16), shape((slots, inputs), BF16)),
        [pltpu.VMEM((table, inputs), BF16), pick],
        [VM] * 7 + [SM],
    )(features, feature_hubs, feature_arrived, dense, degree, sends, send_count, hub_list)
    mean_arrived = swap(rows.reshape(peers, SLOTS, inputs), "dev").reshape(slots, inputs)
    mean_hubs = swap(gather_hubs(mean_arrived), "grp").reshape(hubs, inputs)

    share = STACK_ROWS // groups
    hidden, base, edges, partial = kernel_call(
        functools.partial(main_part, samples_all),
        (
            shape((nodes, width), BF16),
            shape((nodes, width), F32),
            shape((peers * capacity, padded), BF16),
            shape((groups, TILE + 2 * share, padded), BF16),
        ),
        [
            pltpu.VMEM((table, 2 * inputs), BF16),
            pltpu.VMEM((table, width), BF16),
            pltpu.VMEM((2 * inputs, width), BF16),
            pltpu.VMEM((width, padded), BF16),
            pltpu.VMEM((width, 2 * padded), BF16),
            pltpu.VMEM((nodes, 2 * padded), BF16),
            pltpu.VMEM((STACK_ROWS, width), F32),
        ],
        limit=48,
    )(
        features, feature_hubs, feature_arrived, mean_rows, mean_hubs, mean_arrived,
        dense, turned, degree, sample_ids, labels.reshape(1, nodes),
        first_self, first_mean, second_self, second_mean,
    )
    partial = swap(partial, "grp")
    rows = kernel_call(
        sum_groups,
        shape((slots, padded), BF16),
        [pltpu.VMEM(partial.shape[1:], F32), pltpu.VMEM((peers, SLOTS - HUB_AT, padded), F32)],
    )(partial, edges)
    arrived = swap(rows.reshape(peers, SLOTS, padded), "dev").reshape(slots, padded)

    pieces = kernel_call(sum_peers, shape((peers, SLOTS - HUB_AT, TILE), F32))(arrived)
    pieces = swap(pieces, "dev")
    grad_hidden = kernel_call(
        return_rows,
        shape((nodes, width), F32),
        [pick, pltpu.VMEM((width, padded), BF16)],
        [VM, VM, VM, VM, SM, VM],
        flops=2 * nodes * (slots * padded + 2 * width * padded),
        moved=6 * MIB,
    )(base, arrived, sends, send_count, hub_list, second_mean)
    stack = kernel_call(
        join_pieces, shape((groups, share, width), F32), [pltpu.VMEM((share, width), F32)]
    )(pieces)
    stack = swap(stack, "grp").reshape(STACK_ROWS, width)
    first_self_sum, first_mean_sum, self_sum, mean_sum, loss = kernel_call(
        functools.partial(weight_outputs, samples_all),
        (
            shape(first_self.shape, F32),
            shape(first_mean.shape, F32),
            shape((width, classes), F32),
            shape((width, classes), F32),
            shape((1, 1), F32),
        ),
    )(stack)
    return hidden, grad_hidden, loss[0, 0], first_self_sum, first_mean_sum, self_sum, mean_sum


def solution(mesh):
    both = ("grp", "dev")
    placed = (
        P(both, None),
        P(both, None),
        P(both, None, None),
        P(both, None),
        P(both, None),
        P(both, None),
        P(both),
        P(both, None, None),
        P(both, None),
        P(both),
        P(),
        P(),
        P(),
        P(),
    )
    return jax.shard_map(
        on_device,
        mesh=mesh,
        in_specs=placed,
        out_specs=(P(both, None), P(both, None), P(), P(), P(), P(), P()),
        check_vma=False,
    )
```

```python
import functools

import jax
import jax.numpy as jnp
from jax import lax
from jax.experimental import pallas as pl
from jax.experimental.pallas import tpu as pltpu
from jax.sharding import PartitionSpec as P

F32 = jnp.float32
BF16 = jnp.bfloat16
I32 = jnp.int32
MIB = 1 << 20
TILE = 128
HALF = 64
PEERS = 32
CHIPS = 4
CORES = 2
HUBS_EACH = 4
CAPACITY = 32
PEER_HUBS = CORES * CHIPS * HUBS_EACH
FORWARD_ROWS = CAPACITY + PEER_HUBS
EDGE_ROWS = CAPACITY + CAPACITY // 2
HUB_ROWS = CHIPS * HUBS_EACH
HUB_PACKED = HUB_ROWS + HUB_ROWS // 2
STACK_ROWS = 640
SELF_AT = 256
LOSS_AT = 440
MEAN_AT = 448
CLASS_ROWS = 176
PIECE = STACK_ROWS // CORES * 4 // PEERS
SUM_ROWS = HUB_PACKED + PIECE
BACK_ROWS = EDGE_ROWS + SUM_ROWS
PIECE_ROWS = PIECE + 8

VM = pl.BlockSpec(memory_space=pltpu.VMEM)
SM = pl.BlockSpec(memory_space=pltpu.SMEM)
ANY = pl.BlockSpec(memory_space=pl.ANY)


def nn(left, right):
    return jnp.dot(left, right, preferred_element_type=F32)


def nt(left, right):
    return lax.dot_general(left, right, (((1,), (1,)), ((), ())), preferred_element_type=F32)


def tn(left, right):
    return lax.dot_general(left, right, (((0,), (0,)), ((), ())), preferred_element_type=F32)


def split(values):
    high = values.astype(BF16)
    low = (values - high.astype(F32)).astype(BF16)
    return high, low


def one_hot(hit):
    return jnp.where(hit, 1.0, 0.0).astype(BF16)


def iota(dims, axis):
    return lax.broadcasted_iota(I32, dims, axis)


def kernel_call(body, outs, scratch=(), in_specs=None, limit=24, flops=0, moved=0):
    placed = {} if in_specs is None else {"in_specs": in_specs}
    return pl.pallas_call(
        body,
        out_shape=outs,
        **placed,
        scratch_shapes=list(scratch),
        compiler_params=pltpu.CompilerParams(vmem_limit_bytes=limit * MIB),
        cost_estimate=pl.CostEstimate(flops=flops, bytes_accessed=moved, transcendentals=0),
    )


def position():
    group = lax.axis_index("grp")
    return group // CORES, group % CORES


def hub_picks(hub_ref, core, nodes):
    row = iota((16, nodes), 0)
    found = jnp.full((16, nodes), -1, I32)
    for k in range(HUBS_EACH):
        found = jnp.where(row == core * HUBS_EACH + k, hub_ref[0, k], found)
    return one_hot(found == iota((16, nodes), 1))


def hub_features(features_ref, hub_ref, out_ref):
    unused, core = position()
    out_ref[...] = nn(hub_picks(hub_ref, core, features_ref.shape[0]), features_ref[...]).astype(BF16)


def edge_picks(send_ref, count_ref, pick_ref):
    nodes = pick_ref.shape[1]
    send = jnp.transpose(send_ref[...])
    send = jnp.where(iota(send.shape, 0) < count_ref[...], send, -1)
    lane = iota((CAPACITY, nodes), 1)
    for n in range(PEERS):
        pick_ref[n * CAPACITY : (n + 1) * CAPACITY, :] = one_hot(send[:, n : n + 1] == lane)


def build_dense(adj_ref, dst_ref, src_ref, count_ref, hub_ref, dense_ref, turned_ref, degree_ref, hub_dense_ref, order_ref):
    nodes = dense_ref.shape[0]
    hubs = order_ref.shape[0]
    dense_ref[...] = jnp.zeros_like(dense_ref)
    turned_ref[...] = jnp.zeros_like(turned_ref)

    def add(t, carry):
        rows = pl.ds(pl.multiple_of(dst_ref[0, t] * TILE, TILE), TILE)
        columns = pl.ds(pl.multiple_of(src_ref[0, t] * TILE, TILE), TILE)
        tile = adj_ref[t]
        dense_ref[rows, columns] += tile
        turned_ref[columns, rows] += jnp.transpose(tile)
        return carry

    lax.fori_loop(0, count_ref[0], add, 0)
    new = iota((hubs, 1), 0)
    member, core, chip, k = new >> 5, (new >> 4) & 1, (new >> 2) & 3, new & 3
    old = (chip * CORES + core) * (PEERS * HUBS_EACH) + member * HUBS_EACH + k
    order_ref[...] = one_hot(old == iota((hubs, hubs), 1))
    spot = slice(nodes, nodes + hubs)
    dense_ref[:, spot] = nt(dense_ref[:, spot], order_ref[...]).astype(BF16)
    turned_ref[spot, :] = nn(order_ref[...], turned_ref[spot, :]).astype(BF16)
    ones = jnp.ones((dense_ref.shape[1], TILE), BF16)
    degree_ref[...] = jnp.maximum(nn(dense_ref[...], ones), 1.0)
    unused, core = position()
    hub_dense_ref[...] = nn(hub_picks(hub_ref, core, nodes), dense_ref[...]).astype(BF16)


def fill(pick_ref, values_ref, *refs):
    *pair_refs, out_ref = refs
    chip, unused = position()
    hubs = jnp.zeros((PEER_HUBS, TILE), F32)
    row = iota((PEER_HUBS, 16), 0)
    i = iota((PEER_HUBS, 16), 1)
    for shift, pair_ref in enumerate(pair_refs):
        other = (chip + CHIPS - shift) % CHIPS
        place = one_hot((i < CORES * HUBS_EACH) & (row == (i >> 2) * HUB_ROWS + other * HUBS_EACH + (i & 3)))
        hubs += nn(place, pair_ref[...])
    hubs = hubs.astype(BF16)
    edges = nn(pick_ref[...], values_ref[...]).astype(BF16)
    for n in range(PEERS):
        at = n * FORWARD_ROWS
        out_ref[at : at + CAPACITY, :] = edges[n * CAPACITY : (n + 1) * CAPACITY]
        out_ref[at + CAPACITY : at + FORWARD_ROWS, :] = hubs


def assemble(table_ref, own_ref, arrived_ref, lanes):
    own = own_ref.shape[0]
    table_ref[0:own, lanes] = own_ref[...]
    for n in range(PEERS):
        at = n * FORWARD_ROWS
        hub_at = own + n * PEER_HUBS
        edge_at = own + PEERS * PEER_HUBS + n * CAPACITY
        table_ref[hub_at : hub_at + PEER_HUBS, lanes] = arrived_ref[at + CAPACITY : at + FORWARD_ROWS, :]
        table_ref[edge_at : edge_at + CAPACITY, lanes] = arrived_ref[at : at + CAPACITY, :]


def hub_means(features_ref, arrived_ref, hub_dense_ref, out_ref, table_ref):
    assemble(table_ref, features_ref, arrived_ref, slice(0, TILE))
    counts = hub_dense_ref[...]
    degree = jnp.maximum(nn(counts, jnp.ones((counts.shape[1], TILE), BF16)), 1.0)
    out_ref[...] = (nn(counts, table_ref[...]) / degree).astype(BF16)


def all_means(table_ref, dense_ref, degree_ref, out_ref):
    out_ref[...] = (nn(dense_ref[...], table_ref[...]) / degree_ref[...]).astype(BF16)


def join_rests(first, second):
    return first + pltpu.roll(second, HALF, 1)


def part_rests(packed):
    low = iota(packed.shape, 1) < HALF
    return jnp.where(low, packed, 0.0), jnp.where(low, pltpu.roll(packed, HALF, 1), 0.0)


def main_part(
    samples_all,
    feature_table_ref, mean_ref, mean_arrived_ref, dense_ref, turned_ref, degree_ref,
    sample_any, label_any, first_self_any, first_mean_any, second_self_any, second_mean_any,
    hidden_ref, base_ref, edge_ref, mine_ref, theirs_ref,
    table_ref, source_ref, scaled_ref, stack_ref, pay_ref,
    sample_ref, label_ref, first_ref, raw_self_ref, raw_mean_ref, self_ref, second_ref, sems,
):
    loads = [
        pltpu.make_async_copy(source, target, sems.at[i])
        for i, (source, target) in enumerate(
            (
                (first_self_any, first_ref.at[pl.ds(0, TILE)]),
                (first_mean_any, first_ref.at[pl.ds(TILE, TILE)]),
                (second_self_any, raw_self_ref),
                (second_mean_any, raw_mean_ref),
                (sample_any, sample_ref),
                (label_any, label_ref),
            )
        )
    ]
    for load in loads:
        load.start()
    nodes, width = hidden_ref.shape
    classes = raw_self_ref.shape[0]
    padded = self_ref.shape[0]
    chunks = table_ref.shape[0] // nodes
    table_ref[:, 0:TILE] = feature_table_ref[...]
    assemble(table_ref, mean_ref, mean_arrived_ref, slice(TILE, 2 * TILE))
    self_ref[...] = jnp.zeros_like(self_ref)
    second_ref[...] = jnp.zeros_like(second_ref)
    for load in loads:
        load.wait()
    self_ref[0:classes, :] = raw_self_ref[...]
    second_ref[0:classes, :] = raw_mean_ref[...]

    def rows_of(i):
        return pl.ds(pl.multiple_of(i * nodes, nodes), nodes)

    def forward(i, carry):
        rows = rows_of(i)
        linear = nn(table_ref[rows, :], first_ref[...])
        source_ref[rows, :] = jnp.maximum(linear, 0.0).astype(BF16)
        return carry

    lax.fori_loop(0, chunks, forward, 0)
    hidden = source_ref[0:nodes, :]
    hidden_ref[...] = hidden
    degree = degree_ref[:, 0:1]
    mean = (nn(dense_ref[...], source_ref[...]) / degree).astype(BF16)
    logits = nt(hidden, self_ref[...]) + nt(mean, second_ref[...])

    lane = iota((nodes, padded), 1)
    real = lane < classes
    node = iota((nodes, sample_ref.shape[1]), 0)
    hits = jnp.where(node == sample_ref[...], 1.0, 0.0)
    times = jnp.sum(hits, axis=1, keepdims=True)
    label = jnp.transpose(jnp.broadcast_to(label_ref[...], (8, nodes)))[:, 0:1]
    onehot = jnp.where(lane == label, 1.0, 0.0)
    top = jnp.max(jnp.where(real, logits, -jnp.inf), axis=1, keepdims=True)
    shifted = logits - top
    powers = jnp.where(real, jnp.exp(shifted), 0.0)
    total = jnp.sum(powers, axis=1, keepdims=True)
    chosen = jnp.sum(onehot * shifted, axis=1, keepdims=True)
    loss = jnp.sum(times * (jnp.log(total) - chosen), axis=0, keepdims=True)
    upstream = times * ((powers / total - onehot) / samples_all)
    upstream = upstream.astype(BF16)
    high, low = split(upstream.astype(F32) / degree)
    scaled_ref[:, 0:padded] = high
    scaled_ref[:, padded : 2 * padded] = low

    stack_ref[SELF_AT:, :] = jnp.zeros((STACK_ROWS - SELF_AT, width), F32)
    stack_ref[SELF_AT : SELF_AT + CLASS_ROWS, :] = tn(upstream, hidden)[0:CLASS_ROWS]
    stack_ref[MEAN_AT : MEAN_AT + CLASS_ROWS, :] = tn(upstream, mean)[0:CLASS_ROWS]
    loss_high = loss.astype(BF16).astype(F32)
    place = iota((8, width), 0)
    marks = jnp.where(place == 0, loss_high, 0.0)
    stack_ref[LOSS_AT : LOSS_AT + 8, :] = jnp.where(place == 1, loss - loss_high, marks)

    def back(rows):
        pair = nn(turned_ref[rows, :], scaled_ref[...])
        found = pair[:, 0:padded] + pair[:, padded : 2 * padded]
        high, low = split(found)
        return found, nn(high, second_ref[...]) + nn(low, second_ref[...])

    def weights(rows, grad):
        masked = jnp.where(source_ref[rows, :] > 0, grad, 0.0).astype(BF16)
        return tn(table_ref[rows, :], masked)

    own = rows_of(0)
    unused, spread = back(own)
    base = nt(upstream, jnp.transpose(self_ref[...])) + spread
    base_ref[...] = base
    stack_ref[0 : 2 * TILE, :] = weights(own, base)
    each = nodes // CAPACITY

    def hub_chunk(i, carry):
        rows = rows_of(i + 1)
        found, spread = back(rows)
        stack_ref[0 : 2 * TILE, :] += weights(rows, spread)
        for p in range(each):
            for core in range(CORES):
                at = p * PEER_HUBS + core * HUB_ROWS
                rest = found[at : at + HUB_ROWS, TILE:]
                pay_ref[core, i * each + p, 0:HUB_ROWS, :] = found[at : at + HUB_ROWS, 0:TILE]
                pay_ref[core, i * each + p, HUB_ROWS:HUB_PACKED, :] = join_rests(
                    rest[0 : HUB_ROWS // 2], rest[HUB_ROWS // 2 :]
                )
        return carry

    lax.fori_loop(0, PEERS // each, hub_chunk, 0)

    def edge_chunk(i, carry):
        rows = rows_of(i + 1 + PEERS // each)
        found, spread = back(rows)
        stack_ref[0 : 2 * TILE, :] += weights(rows, spread)
        for p in range(each):
            at = p * CAPACITY
            rest = found[at : at + CAPACITY, TILE:]
            edge_ref[i * each + p, 0:CAPACITY, :] = found[at : at + CAPACITY, 0:TILE].astype(BF16)
            edge_ref[i * each + p, CAPACITY:EDGE_ROWS, :] = join_rests(
                rest[0 : CAPACITY // 2], rest[CAPACITY // 2 :]
            ).astype(BF16)
        return carry

    lax.fori_loop(0, PEERS // each, edge_chunk, 0)
    for core in range(CORES):
        for n in range(PEERS):
            at = core * (STACK_ROWS // CORES) + PIECE * (n % 8)
            lanes = slice(TILE * (n // 8), TILE * (n // 8 + 1))
            pay_ref[core, n, HUB_PACKED:SUM_ROWS, :] = stack_ref[at : at + PIECE, lanes]
    unused, core = position()
    mine_ref[...] = pay_ref[core].astype(BF16)
    theirs_ref[...] = pay_ref[1 - core].astype(BF16)


def sum_cores(mine_ref, arrived_ref, edge_ref, out_ref):
    out_ref[:, 0:EDGE_ROWS, :] = edge_ref[...]
    total = mine_ref[...].astype(F32) + arrived_ref[...].astype(F32)
    out_ref[:, EDGE_ROWS:BACK_ROWS, :] = total.astype(BF16)


def sum_peers(arrived_ref, out_ref):
    total = jnp.zeros((SUM_ROWS, TILE), F32)
    for n in range(PEERS):
        total += arrived_ref[n, EDGE_ROWS:BACK_ROWS, :].astype(F32)
    out_ref[...] = total


def sum_chips(*refs):
    *sum_refs, out_ref, total_ref = refs
    total = sum_refs[0][...]
    for sum_ref in sum_refs[1:]:
        total += sum_ref[...]
    total_ref[...] = total
    piece = total[HUB_PACKED:SUM_ROWS]
    rest = piece[0:8] - piece[0:8].astype(BF16).astype(F32)
    piece = jnp.concatenate([piece, rest], axis=0).astype(BF16)
    for n in range(PEERS):
        out_ref[n] = piece


def return_rows(base_ref, arrived_ref, total_ref, pick_ref, hub_ref, mean_any, out_ref, found_ref, raw_ref, second_ref, sem):
    load = pltpu.make_async_copy(mean_any, raw_ref, sem)
    load.start()
    nodes = out_ref.shape[0]
    for n in range(PEERS):
        at = n * CAPACITY
        found_ref[at : at + CAPACITY, 0:TILE] = arrived_ref[n, 0:CAPACITY, :]
        first, second = part_rests(arrived_ref[n, CAPACITY:EDGE_ROWS, :].astype(F32))
        found_ref[at : at + CAPACITY // 2, TILE:] = first.astype(BF16)
        found_ref[at + CAPACITY // 2 : at + CAPACITY, TILE:] = second.astype(BF16)
    first, second = part_rests(total_ref[HUB_ROWS:HUB_PACKED, :])
    hubs = jnp.concatenate([total_ref[0:HUB_ROWS, :], jnp.concatenate([first, second], axis=0)], axis=1)
    chip, unused = position()
    lane = iota((nodes, HUB_ROWS), 1)
    owner = jnp.full((nodes, HUB_ROWS), -1, I32)
    for k in range(HUBS_EACH):
        owner = jnp.where(lane == chip * HUBS_EACH + k, hub_ref[0, k], owner)
    owner = one_hot(owner == iota((nodes, HUB_ROWS), 0))
    high, low = split(hubs)
    rows = tn(pick_ref[...], found_ref[...]) + nn(owner, high) + nn(owner, low)
    second_ref[...] = jnp.zeros_like(second_ref)
    load.wait()
    second_ref[0 : raw_ref.shape[0], :] = raw_ref[...]
    high, low = split(rows)
    out_ref[...] = base_ref[...] + nn(high, second_ref[...]) + nn(low, second_ref[...])


def weight_outputs(samples_all, mine_ref, theirs_ref, first_self_ref, first_mean_ref, self_ref, mean_ref, loss_ref, stack_ref):
    unused, core = position()
    half = STACK_ROWS // CORES
    for n in range(PEERS):
        mine = mine_ref[n].astype(F32)
        theirs = theirs_ref[n].astype(F32)
        lanes = slice(TILE * (n // 8), TILE * (n // 8 + 1))
        at = PIECE * (n % 8)
        first = jnp.where(core == 0, mine, theirs)
        second = jnp.where(core == 0, theirs, mine)
        stack_ref[at : at + PIECE, lanes] = first[0:PIECE]
        stack_ref[half + at : half + at + PIECE, lanes] = second[0:PIECE]
        if lanes.start == 0 and half + at == LOSS_AT:
            loss = second[0:1, 0:1] + second[1:2, 0:1] + second[PIECE : PIECE + 1, 0:1]
            loss_ref[...] = loss / samples_all
    classes = self_ref.shape[0]
    first_self_ref[...] = stack_ref[0:TILE, :]
    first_mean_ref[...] = stack_ref[TILE : 2 * TILE, :]
    self_ref[...] = stack_ref[SELF_AT : SELF_AT + classes, :]
    mean_ref[...] = stack_ref[MEAN_AT : MEAN_AT + classes, :]


def shape(dims, dtype):
    return jax.ShapeDtypeStruct(dims, dtype)


def swap(values):
    return lax.all_to_all(values, "dev", split_axis=0, concat_axis=0, tiled=True)


def to_core(values):
    return lax.ppermute(values, "grp", [(i, i ^ 1) for i in range(CHIPS * CORES)])


def to_chips(values):
    every = CHIPS * CORES
    return [
        lax.ppermute(values, "grp", [(i, (i + CORES * shift) % every) for i in range(every)])
        for shift in range(1, CHIPS)
    ]


def on_device(
    features,
    hub_list,
    send_list,
    send_count,
    tile_dst,
    tile_src,
    tile_count,
    tile_adj,
    sample_ids,
    labels,
    first_self,
    first_mean,
    second_self,
    second_mean,
):
    nodes, inputs = features.shape
    width, classes = second_self.shape
    hubs = CHIPS * CORES * PEERS * HUBS_EACH
    edges = PEERS * CAPACITY
    table = nodes + hubs + edges
    padded = 2 * TILE
    samples_all = float(sample_ids.shape[1] * CHIPS * CORES * PEERS)
    second_self = second_self.T
    second_mean = second_mean.T

    def exchange(own, values):
        pair = own + to_core(own)
        rows = kernel_call(fill, shape((PEERS * FORWARD_ROWS, inputs), BF16), moved=2 * MIB)(
            picks, values(), pair, *to_chips(pair)
        )
        return swap(rows.reshape(PEERS, FORWARD_ROWS, inputs)).reshape(PEERS * FORWARD_ROWS, inputs)

    own = kernel_call(hub_features, shape((16, inputs), BF16), in_specs=[VM, SM])(features, hub_list)
    picks = kernel_call(edge_picks, shape((edges, nodes), BF16), moved=2 * MIB)(send_list[0], send_count)
    feature_arrived = exchange(own, lambda: features)
    dense, turned, degree, hub_dense = kernel_call(
        build_dense,
        (
            shape((nodes, table), BF16),
            shape((table, nodes), BF16),
            shape((nodes, TILE), F32),
            shape((16, table), BF16),
        ),
        [pltpu.VMEM((hubs, hubs), BF16)],
        [VM, SM, SM, SM, SM],
        flops=4 * nodes * hubs * hubs,
        moved=16 * MIB,
    )(tile_adj, tile_dst, tile_src, tile_count, hub_list)
    own, feature_table = kernel_call(
        hub_means, (shape((16, inputs), BF16), shape((table, inputs), BF16))
    )(features, feature_arrived, hub_dense)
    mean_rows = kernel_call(
        all_means, shape((nodes, inputs), BF16), flops=2 * nodes * table * inputs, moved=4 * MIB
    )(feature_table, dense, degree)
    mean_arrived = exchange(own, lambda: mean_rows)

    hidden, base, edge_rows, mine, theirs = kernel_call(
        functools.partial(main_part, samples_all),
        (
            shape((nodes, width), BF16),
            shape((nodes, width), F32),
            shape((PEERS, EDGE_ROWS, TILE), BF16),
            shape((PEERS, SUM_ROWS, TILE), BF16),
            shape((PEERS, SUM_ROWS, TILE), BF16),
        ),
        [
            pltpu.VMEM((table, 2 * inputs), BF16),
            pltpu.VMEM((table, width), BF16),
            pltpu.VMEM((nodes, 2 * padded), BF16),
            pltpu.VMEM((STACK_ROWS, width), F32),
            pltpu.VMEM((CORES, PEERS, SUM_ROWS, TILE), F32),
            pltpu.VMEM(sample_ids.shape, I32),
            pltpu.VMEM((1, nodes), I32),
            pltpu.VMEM((2 * inputs, width), BF16),
            pltpu.VMEM((classes, width), BF16),
            pltpu.VMEM((classes, width), BF16),
            pltpu.VMEM((padded, width), BF16),
            pltpu.VMEM((padded, width), BF16),
            pltpu.SemaphoreType.DMA((6,)),
        ],
        [VM] * 6 + [ANY] * 6,
        limit=44,
    )(
        feature_table, mean_rows, mean_arrived, dense, turned, degree,
        sample_ids, labels.reshape(1, nodes), first_self, first_mean, second_self, second_mean,
    )
    rows = kernel_call(sum_cores, shape((PEERS, BACK_ROWS, TILE), BF16))(mine, to_core(theirs), edge_rows)
    arrived = swap(rows)
    sums = kernel_call(sum_peers, shape((SUM_ROWS, TILE), F32))(arrived)
    pieces, total = kernel_call(
        sum_chips, (shape((PEERS, PIECE_ROWS, TILE), BF16), shape((SUM_ROWS, TILE), F32))
    )(sums, *to_chips(sums))
    pieces = swap(pieces)
    grad_hidden = kernel_call(
        return_rows,
        shape((nodes, width), F32),
        [
            pltpu.VMEM((edges, padded), BF16),
            pltpu.VMEM((classes, width), BF16),
            pltpu.VMEM((padded, width), BF16),
            pltpu.SemaphoreType.DMA,
        ],
        [VM, VM, VM, VM, SM, ANY],
        flops=2 * nodes * (edges * padded + 2 * width * padded),
        moved=8 * MIB,
    )(base, arrived, total, picks, hub_list, second_mean)
    first_self_sum, first_mean_sum, self_sum, mean_sum, loss = kernel_call(
        functools.partial(weight_outputs, samples_all),
        (
            shape(first_self.shape, F32),
            shape(first_mean.shape, F32),
            shape((classes, width), F32),
            shape((classes, width), F32),
            shape((1, 1), F32),
        ),
        [pltpu.VMEM((STACK_ROWS, width), F32)],
    )(pieces, to_core(pieces))
    return hidden, grad_hidden, loss[0, 0], first_self_sum, first_mean_sum, self_sum.T, mean_sum.T


def solution(mesh):
    both = ("grp", "dev")
    placed = (
        P(both, None),
        P(both, None),
        P(both, None, None),
        P(both, None),
        P(both, None),
        P(both, None),
        P(both),
        P(both, None, None),
        P(both, None),
        P(both),
        P(),
        P(),
        P(),
        P(),
    )
    return jax.shard_map(
        on_device,
        mesh=mesh,
        in_specs=placed,
        out_specs=(P(both, None), P(both, None), P(), P(), P(), P(), P()),
        check_vma=False,
    )
```

```python
import functools

import jax
import jax.numpy as jnp
from jax import lax
from jax.experimental import pallas as pl
from jax.experimental.pallas import tpu as pltpu
from jax.sharding import PartitionSpec as P

F32 = jnp.float32
BF16 = jnp.bfloat16
I32 = jnp.int32
MIB = 1 << 20
TILE = 128
HALF = 64
PEERS = 32
CHIPS = 4
CORES = 2
HUBS_EACH = 4
CAPACITY = 32
GROUP_HUBS = PEERS * HUBS_EACH
FORWARD_ROWS = CAPACITY + 8
PEER_HUBS = CORES * CHIPS * HUBS_EACH
EDGE_ROWS = CAPACITY + CAPACITY // 2
HUB_ROWS = CHIPS * HUBS_EACH
HUB_PACKED = HUB_ROWS + HUB_ROWS // 2
STACK_ROWS = 640
SELF_AT = 256
LOSS_AT = 440
MEAN_AT = 448
CLASS_ROWS = 176
PIECE = STACK_ROWS // CORES * 4 // PEERS
SUM_ROWS = HUB_PACKED + PIECE
BACK_ROWS = EDGE_ROWS + SUM_ROWS

VM = pl.BlockSpec(memory_space=pltpu.VMEM)
SM = pl.BlockSpec(memory_space=pltpu.SMEM)
ANY = pl.BlockSpec(memory_space=pl.ANY)
HBM = pl.BlockSpec(memory_space=pltpu.HBM)


def nn(left, right):
    return jnp.dot(left, right, preferred_element_type=F32)


def nt(left, right):
    return lax.dot_general(left, right, (((1,), (1,)), ((), ())), preferred_element_type=F32)


def tn(left, right):
    return lax.dot_general(left, right, (((0,), (0,)), ((), ())), preferred_element_type=F32)


def split(values):
    high = values.astype(BF16)
    low = (values - high.astype(F32)).astype(BF16)
    return high, low


def one_hot(hit):
    return jnp.where(hit, 1.0, 0.0).astype(BF16)


def iota(dims, axis):
    return lax.broadcasted_iota(I32, dims, axis)


def kernel_call(body, outs, scratch=(), in_specs=None, limit=5, flops=0, moved=0):
    placed = {} if in_specs is None else {"in_specs": in_specs}
    return pl.pallas_call(
        body,
        out_shape=outs,
        **placed,
        scratch_shapes=list(scratch),
        compiler_params=pltpu.CompilerParams(vmem_limit_bytes=limit * MIB),
        cost_estimate=pl.CostEstimate(flops=flops, bytes_accessed=moved, transcendentals=0),
    )


def position():
    group = lax.axis_index("grp")
    return group // CORES, group % CORES


def fetch(pairs, sems):
    loads = [pltpu.make_async_copy(source, target, sems.at[i]) for i, (source, target) in enumerate(pairs)]
    for load in loads:
        load.start()
    return loads


def wanted_rows(send, counts, hub_ref):
    send = jnp.transpose(send)
    send = jnp.where(iota(send.shape, 0) < counts, send, -1)
    row = iota((FORWARD_ROWS - CAPACITY, PEERS), 0)
    hubs = jnp.full(row.shape, -1, I32)
    for k in range(HUBS_EACH):
        hubs = jnp.where(row == k, hub_ref[0, k], hubs)
    return jnp.concatenate([send, hubs], axis=0)


def pick_matrix(wanted, pick_ref):
    lane = iota((2 * FORWARD_ROWS, pick_ref.shape[1]), 1)
    for n in range(0, PEERS, 2):
        pair = jnp.concatenate([wanted[:, n : n + 1], wanted[:, n + 1 : n + 2]], axis=0)
        pick_ref[n * FORWARD_ROWS : (n + 2) * FORWARD_ROWS, :] = one_hot(pair == lane)


def send_features(
    features_any, send_any, count_any, hub_any, out_ref, pick_ref, features_ref, send_ref, count_ref, hub_ref, sems
):
    loads = fetch(
        (
            (send_any.at[0], send_ref),
            (count_any, count_ref),
            (hub_any, hub_ref),
            (features_any, features_ref),
        ),
        sems,
    )
    for load in loads[:-1]:
        load.wait()
    pick_matrix(wanted_rows(send_ref[...], count_ref[...], hub_ref), pick_ref)
    loads[-1].wait()
    out_ref[...] = nn(pick_ref[...], features_ref[...]).astype(BF16)


def build_dense(*refs):
    count = 13
    sources, refs = refs[:count], refs[count + 1 :]
    dense_ref, numbers_ref, weights_ref, wanted_ref, pick_ref, *places, sems = refs
    (
        adj_ref, dst_ref, src_ref, live_ref, send_ref, count_ref, hub_ref,
        sample_ref, label_ref, raw_self_ref, raw_mean_ref,
    ) = places
    targets = (
        adj_ref, dst_ref, src_ref, live_ref, send_ref, count_ref, hub_ref, sample_ref, label_ref,
        weights_ref.at[pl.ds(0, TILE)], weights_ref.at[pl.ds(TILE, TILE)], raw_self_ref, raw_mean_ref,
    )
    loads = fetch(zip(sources, targets), sems)
    dense_ref[...] = jnp.zeros_like(dense_ref)
    weights_ref[SELF_AT:, :] = jnp.zeros((weights_ref.shape[0] - SELF_AT, weights_ref.shape[1]), BF16)
    for load in loads:
        load.wait()

    def add(t, carry):
        rows = pl.ds(pl.multiple_of(dst_ref[0, t] * TILE, TILE), TILE)
        columns = pl.ds(pl.multiple_of(src_ref[0, t] * TILE, TILE), TILE)
        dense_ref[rows, columns] += adj_ref[t]
        return carry

    lax.fori_loop(0, live_ref[0], add, 0)
    classes = raw_self_ref.shape[0]
    weights_ref[SELF_AT : SELF_AT + classes, :] = raw_self_ref[...]
    weights_ref[2 * SELF_AT : 2 * SELF_AT + classes, :] = raw_mean_ref[...]
    wanted = wanted_rows(send_ref[...], count_ref[...], hub_ref)
    wanted_ref[...] = wanted
    pick_matrix(wanted, pick_ref)
    nodes = dense_ref.shape[0]
    node = iota((nodes, sample_ref.shape[1]), 0)
    times = jnp.sum(jnp.where(node == sample_ref[...], 1.0, 0.0), axis=1, keepdims=True)
    label = jnp.transpose(jnp.broadcast_to(label_ref[...], (8, nodes)))[:, 0:1]
    degree = jnp.maximum(nn(dense_ref[...], jnp.ones((dense_ref.shape[1], TILE), BF16)), 1.0)
    lane = iota(degree.shape, 1)
    numbers_ref[...] = jnp.where(lane == 0, degree, jnp.where(lane == 1, times, label.astype(F32)))


def group_hubs(arrived_ref, out_ref):
    low = iota((8, TILE), 0) < HUBS_EACH
    rows = []
    for n in range(0, PEERS, 2):
        first = arrived_ref[n, CAPACITY:FORWARD_ROWS, :].astype(F32)
        second = arrived_ref[n + 1, CAPACITY:FORWARD_ROWS, :].astype(F32)
        rows.append(jnp.where(low, first, pltpu.roll(second, HUBS_EACH, 0)))
    out_ref[...] = jnp.concatenate(rows, axis=0).astype(BF16)


def join_blocks(*refs):
    out_ref = refs[-1]
    for i in range(CHIPS):
        out_ref[i * GROUP_HUBS : (i + 1) * GROUP_HUBS, :] = refs[i][...]


def place_hubs(table_ref, start, hub_refs, lanes):
    chip, core = position()
    for there, hub_ref in zip((core, 1 - core), hub_refs):
        for i in range(CHIPS):
            other = (chip + CHIPS - i) % CHIPS
            at = start + (other * CORES + there) * GROUP_HUBS
            block = hub_ref[i * GROUP_HUBS : (i + 1) * GROUP_HUBS, :]
            table_ref[pl.ds(pl.multiple_of(at, GROUP_HUBS), GROUP_HUBS), lanes] = block


def first_means(
    features_ref, arrived_ref, dense_ref, numbers_ref, pick_ref, own_hub_ref, other_hub_ref,
    mean_ref, table_ref, out_ref,
):
    nodes = features_ref.shape[0]
    table_ref[0:nodes, :] = features_ref[...]
    place_hubs(table_ref, nodes, (own_hub_ref, other_hub_ref), slice(0, TILE))
    edge_at = nodes + CORES * CHIPS * GROUP_HUBS
    for n in range(PEERS):
        at = edge_at + n * CAPACITY
        table_ref[at : at + CAPACITY, :] = arrived_ref[n, 0:CAPACITY, :]
    mean = (nn(dense_ref[...], table_ref[...]) / numbers_ref[:, 0:1]).astype(BF16)
    mean_ref[...] = mean
    out_ref[...] = nn(pick_ref[...], mean).astype(BF16)


def join_rests(first, second):
    return first + pltpu.roll(second, HALF, 1)


def part_rests(packed):
    low = iota(packed.shape, 1) < HALF
    return jnp.where(low, packed, 0.0), jnp.where(low, pltpu.roll(packed, HALF, 1), 0.0)


def early_part(
    feature_table_ref, mean_ref, arrived_ref, dense_ref, weights_ref,
    hidden_ref, table_ref, source_ref, part_ref, logits_ref,
):
    nodes, width = hidden_ref.shape
    edges = PEERS * CAPACITY
    edge_at = feature_table_ref.shape[0] - edges
    table_ref[0:nodes, 0:TILE] = feature_table_ref[0:nodes, :]
    table_ref[nodes:, 0:TILE] = feature_table_ref[edge_at:, :]
    table_ref[0:nodes, TILE:] = mean_ref[...]
    for n in range(PEERS):
        at = nodes + n * CAPACITY
        table_ref[at : at + CAPACITY, TILE:] = arrived_ref[n, 0:CAPACITY, :]

    def forward(i, carry):
        rows = pl.ds(pl.multiple_of(i * nodes, nodes), nodes)
        source_ref[rows, :] = jnp.maximum(nn(table_ref[rows, :], weights_ref[0:SELF_AT, :]), 0.0).astype(BF16)
        return carry

    lax.fori_loop(0, table_ref.shape[0] // nodes, forward, 0)
    hidden = source_ref[0:nodes, :]
    hidden_ref[...] = hidden
    part_ref[...] = nn(dense_ref[:, 0:nodes], hidden) + nn(dense_ref[:, edge_at:], source_ref[nodes:, :])
    logits_ref[...] = nt(hidden, weights_ref[SELF_AT : 2 * SELF_AT, :])


def main_part(
    samples_all, classes,
    feature_table_ref, early_table_ref, early_source_ref, part_ref, logits_ref,
    dense_ref, numbers_ref, weights_ref, own_hub_ref, other_hub_ref,
    base_ref, edge_ref, mine_ref, theirs_ref,
    table_ref, source_ref, turned_ref, stack_ref, pay_ref,
):
    nodes, width = base_ref.shape
    padded = SELF_AT
    hubs = table_ref.shape[0]
    self_rows = slice(SELF_AT, 2 * SELF_AT)
    mean_rows = slice(2 * SELF_AT, 3 * SELF_AT)
    table_ref[:, 0:TILE] = feature_table_ref[nodes : nodes + hubs, :]
    place_hubs(table_ref, 0, (own_hub_ref, other_hub_ref), slice(TILE, 2 * TILE))

    def rows_of(i):
        return pl.ds(pl.multiple_of(i * nodes, nodes), nodes)

    def forward(i, carry):
        rows = rows_of(i)
        source_ref[rows, :] = jnp.maximum(nn(table_ref[rows, :], weights_ref[0:SELF_AT, :]), 0.0).astype(BF16)
        return carry

    lax.fori_loop(0, hubs // nodes, forward, 0)
    hidden = early_source_ref[0:nodes, :]
    degree = numbers_ref[:, 0:1]
    times = numbers_ref[:, 1:2]
    label = numbers_ref[:, 2:3].astype(I32)
    mean = part_ref[...] + nn(dense_ref[:, nodes : nodes + hubs], source_ref[...])
    mean = (mean / degree).astype(BF16)
    logits = logits_ref[...] + nt(mean, weights_ref[mean_rows, :])

    lane = iota((nodes, padded), 1)
    real = lane < classes
    onehot = jnp.where(lane == label, 1.0, 0.0)
    top = jnp.max(jnp.where(real, logits, -jnp.inf), axis=1, keepdims=True)
    shifted = logits - top
    powers = jnp.where(real, jnp.exp(shifted), 0.0)
    total = jnp.sum(powers, axis=1, keepdims=True)
    chosen = jnp.sum(onehot * shifted, axis=1, keepdims=True)
    loss = jnp.sum(times * (jnp.log(total) - chosen), axis=0, keepdims=True)
    upstream = times * ((powers / total - onehot) / samples_all)
    upstream = upstream.astype(BF16)
    turned_ref[...] = jnp.transpose((upstream.astype(F32) / degree).astype(BF16))

    stack_ref[SELF_AT:, :] = jnp.zeros((STACK_ROWS - SELF_AT, width), F32)
    upstream_turned = jnp.transpose(upstream)
    stack_ref[SELF_AT : SELF_AT + CLASS_ROWS, :] = nn(upstream_turned, hidden)[0:CLASS_ROWS]
    stack_ref[MEAN_AT : MEAN_AT + CLASS_ROWS, :] = nn(upstream_turned, mean)[0:CLASS_ROWS]
    loss_high = loss.astype(BF16).astype(F32)
    place = iota((8, width), 0)
    marks = jnp.where(place == 0, loss_high, 0.0)
    stack_ref[LOSS_AT : LOSS_AT + 8, :] = jnp.where(place == 1, loss - loss_high, marks)

    def back(at):
        found = nn(turned_ref[...], dense_ref[:, pl.ds(pl.multiple_of(at, nodes), nodes)])
        found = jnp.transpose(found.astype(BF16))
        return found, nn(found, weights_ref[mean_rows, :])

    def weights(table, source, grad):
        masked = jnp.where(source > 0, grad, 0.0).astype(BF16)
        return tn(table, masked)

    unused, spread = back(0)
    base = nn(upstream, weights_ref[self_rows, :]) + spread
    base_ref[...] = base
    stack_ref[0 : 2 * TILE, :] = weights(early_table_ref[0:nodes, :], hidden, base)
    each = nodes // CAPACITY

    low = iota((8, padded), 0) < HUBS_EACH
    for i in range(hubs // nodes):
        rows = slice(i * nodes, (i + 1) * nodes)
        found, spread = back(nodes + i * nodes)
        stack_ref[0 : 2 * TILE, :] += weights(table_ref[rows, :], source_ref[rows, :], spread)
        found = found.astype(F32)
        for core in range(CORES):
            for n in range(0, PEERS, 2):
                at = core * GROUP_HUBS + n * HUBS_EACH
                first = found[at : at + 8]
                second = found[at + CORES * GROUP_HUBS : at + CORES * GROUP_HUBS + 8]
                for member, rows_here in (
                    (n, jnp.where(low, first, pltpu.roll(second, HUBS_EACH, 0))),
                    (n + 1, jnp.where(low, pltpu.roll(first, HUBS_EACH, 0), second)),
                ):
                    pay_ref[core, member, 8 * i : 8 * i + 8, :] = rows_here[:, 0:TILE]
                    rest = rows_here[:, TILE:]
                    if i == 0:
                        pay_ref[core, member, HUB_ROWS:HUB_PACKED, :] = rest
                    else:
                        pay_ref[core, member, HUB_ROWS:HUB_PACKED, :] += pltpu.roll(rest, HALF, 1)

    def edge_chunk(i, carry):
        rows = rows_of(i + 1)
        found, spread = back(nodes + hubs + i * nodes)
        stack_ref[0 : 2 * TILE, :] += weights(early_table_ref[rows, :], early_source_ref[rows, :], spread)
        for p in range(each):
            at = p * CAPACITY
            rest = found[at : at + CAPACITY, TILE:].astype(F32)
            edge_ref[i * each + p, 0:CAPACITY, :] = found[at : at + CAPACITY, 0:TILE]
            edge_ref[i * each + p, CAPACITY:EDGE_ROWS, :] = join_rests(
                rest[0 : CAPACITY // 2], rest[CAPACITY // 2 :]
            ).astype(BF16)
        return carry

    lax.fori_loop(0, PEERS // each, edge_chunk, 0)
    for core in range(CORES):
        for n in range(PEERS):
            at = core * (STACK_ROWS // CORES) + PIECE * (n % 8)
            lanes = slice(TILE * (n // 8), TILE * (n // 8 + 1))
            pay_ref[core, n, HUB_PACKED:SUM_ROWS, :] = stack_ref[at : at + PIECE, lanes]
    unused, core = position()
    mine_ref[...] = pay_ref[core].astype(BF16)
    theirs_ref[...] = pay_ref[1 - core].astype(BF16)


def sum_cores(mine_ref, arrived_ref, edge_ref, out_ref):
    out_ref[:, 0:EDGE_ROWS, :] = edge_ref[...]
    total = mine_ref[...].astype(F32) + arrived_ref[...].astype(F32)
    out_ref[:, EDGE_ROWS:BACK_ROWS, :] = total.astype(BF16)


def sum_peers(arrived_ref, out_ref):
    total = arrived_ref[0, EDGE_ROWS:BACK_ROWS, :].astype(F32)
    for n in range(1, PEERS):
        total += arrived_ref[n, EDGE_ROWS:BACK_ROWS, :].astype(F32)
    out_ref[...] = total


def return_edges(base_ref, arrived_ref, wanted_ref, weights_ref, out_ref, found_ref, pick_ref):
    pick_matrix(wanted_ref[...], pick_ref)
    found_ref[...] = jnp.zeros_like(found_ref)
    for n in range(PEERS):
        at = n * FORWARD_ROWS
        first, second = part_rests(arrived_ref[n, CAPACITY:EDGE_ROWS, :].astype(F32))
        rest = jnp.concatenate([first, second], axis=0).astype(BF16)
        found_ref[at : at + CAPACITY, 0:TILE] = arrived_ref[n, 0:CAPACITY, :]
        found_ref[at : at + CAPACITY, TILE:] = rest
    rows = tn(pick_ref[...], found_ref[...])
    out_ref[...] = base_ref[...] + nn(rows.astype(BF16), weights_ref[2 * SELF_AT :, :])


def sum_chips(*refs):
    sum_refs, out_ref, total_ref = refs[:CHIPS], refs[-2], refs[-1]
    total = sum_refs[0][...]
    for sum_ref in sum_refs[1:]:
        total += sum_ref[...]
    total_ref[...] = total
    piece = total[HUB_PACKED:SUM_ROWS]
    unused, core = position()
    holder = (core == LOSS_AT * CORES // STACK_ROWS) & (lax.axis_index("dev") == LOSS_AT % (STACK_ROWS // CORES) // PIECE)
    rest = piece[0:1] - piece[0:1].astype(BF16).astype(F32)
    row = iota(piece.shape, 0)
    piece = jnp.where((row == 2) & holder, rest, piece).astype(BF16)
    for n in range(PEERS):
        out_ref[n] = piece


def return_hubs(base_ref, total_ref, wanted_ref, weights_ref, out_ref):
    nodes = out_ref.shape[0]
    chip, unused = position()
    mains = (total_ref[0:8, :], total_ref[8:16, :])
    rests = part_rests(total_ref[HUB_ROWS:HUB_PACKED, :])
    own = jnp.zeros((8, 2 * TILE), F32)
    for other in range(CHIPS):
        rows = jnp.concatenate([mains[other // 2], rests[other // 2]], axis=1)
        if other % 2:
            rows = pltpu.roll(rows, HUBS_EACH, 0)
        own += jnp.where(chip == other, rows, 0.0)
    high, low = split(nn(own.astype(BF16), weights_ref[2 * SELF_AT :, :]))
    owner = one_hot(wanted_ref[CAPACITY:FORWARD_ROWS, 0:1] == iota((8, nodes), 1))
    out_ref[...] = base_ref[...] + tn(owner, high) + tn(owner, low)


def weight_outputs(samples_all, mine_ref, theirs_ref, first_self_ref, first_mean_ref, self_ref, mean_ref, loss_ref, stack_ref):
    unused, core = position()
    half = STACK_ROWS // CORES
    for n in range(PEERS):
        mine = mine_ref[n].astype(F32)
        theirs = theirs_ref[n].astype(F32)
        lanes = slice(TILE * (n // 8), TILE * (n // 8 + 1))
        at = PIECE * (n % 8)
        stack_ref[at : at + PIECE, lanes] = jnp.where(core == 0, mine, theirs)
        stack_ref[half + at : half + at + PIECE, lanes] = jnp.where(core == 0, theirs, mine)
    classes = self_ref.shape[0]
    first_self_ref[...] = stack_ref[0:TILE, :]
    first_mean_ref[...] = stack_ref[TILE : 2 * TILE, :]
    self_ref[...] = stack_ref[SELF_AT : SELF_AT + classes, :]
    mean_ref[...] = stack_ref[MEAN_AT : MEAN_AT + classes, :]
    parts = stack_ref[LOSS_AT : LOSS_AT + 8, 0:1]
    loss_ref[...] = (parts[0:1] + parts[1:2] + parts[2:3]) / samples_all


def shape(dims, dtype):
    return jax.ShapeDtypeStruct(dims, dtype)


def swap(values):
    return lax.all_to_all(values, "dev", split_axis=0, concat_axis=0, tiled=True)


def to_core(values):
    return lax.ppermute(values, "grp", [(i, i ^ 1) for i in range(CHIPS * CORES)])


def to_chips(values):
    every = CHIPS * CORES
    return [
        lax.ppermute(values, "grp", [(i, (i + CORES * shift) % every) for i in range(every)])
        for shift in range(1, CHIPS)
    ]


def on_device(
    features,
    hub_list,
    send_list,
    send_count,
    tile_dst,
    tile_src,
    tile_count,
    tile_adj,
    sample_ids,
    labels,
    first_self,
    first_mean,
    second_self,
    second_mean,
):
    nodes, inputs = features.shape
    width, classes = second_self.shape
    hubs = CHIPS * CORES * PEERS * HUBS_EACH
    edges = PEERS * CAPACITY
    table = nodes + hubs + edges
    padded = 2 * TILE
    samples_all = float(sample_ids.shape[1] * CHIPS * CORES * PEERS)

    slots = PEERS * FORWARD_ROWS

    def gather_hubs(arrived, beside):
        own = kernel_call(group_hubs, shape((GROUP_HUBS, inputs), BF16))(arrived)
        blocks = kernel_call(
            join_blocks,
            shape((CHIPS * GROUP_HUBS, inputs), BF16),
            in_specs=[VM] * CHIPS + [ANY] * len(beside),
        )(own, *to_chips(own), *beside)
        return blocks, to_core(blocks)

    rows = kernel_call(
        send_features,
        shape((slots, inputs), BF16),
        [
            pltpu.VMEM((slots, nodes), BF16),
            pltpu.VMEM((nodes, inputs), BF16),
            pltpu.VMEM(send_list.shape[1:], I32),
            pltpu.VMEM(send_count.shape, I32),
            pltpu.SMEM(hub_list.shape, I32),
            pltpu.SemaphoreType.DMA((4,)),
        ],
        [HBM] * 4,
        limit=60,
    )(features, send_list, send_count, hub_list)
    feature_arrived = swap(rows.reshape(PEERS, FORWARD_ROWS, inputs))
    raw = (second_self.T, second_mean.T)
    operands = (
        tile_adj, tile_dst, tile_src, tile_count, send_list[0], send_count, hub_list,
        sample_ids, labels.reshape(1, nodes), first_self, first_mean, *raw,
    )
    dense, numbers, weights, wanted, picks = kernel_call(
        build_dense,
        (
            shape((nodes, table), BF16),
            shape((nodes, TILE), F32),
            shape((3 * padded, width), BF16),
            shape((FORWARD_ROWS, PEERS), I32),
            shape((slots, nodes), BF16),
        ),
        [
            pltpu.VMEM(tile_adj.shape, BF16),
            pltpu.SMEM(tile_dst.shape, I32),
            pltpu.SMEM(tile_src.shape, I32),
            pltpu.SMEM(tile_count.shape, I32),
            pltpu.VMEM(send_list.shape[1:], I32),
            pltpu.VMEM(send_count.shape, I32),
            pltpu.SMEM(hub_list.shape, I32),
            pltpu.VMEM(sample_ids.shape, I32),
            pltpu.VMEM((1, nodes), I32),
            pltpu.VMEM(raw[0].shape, BF16),
            pltpu.VMEM(raw[1].shape, BF16),
            pltpu.SemaphoreType.DMA((len(operands),)),
        ],
        [HBM] * len(operands) + [ANY],
        flops=2 * nodes * table * TILE,
        moved=8 * MIB,
    )(
        *(
            operand if operand is tile_count else pltpu.with_memory_space_constraint(operand, pltpu.HBM)
            for operand in operands
        ),
        feature_arrived,
    )
    feature_hubs = gather_hubs(feature_arrived, [numbers])
    mean_rows, feature_table, rows = kernel_call(
        first_means,
        (shape((nodes, inputs), BF16), shape((table, inputs), BF16), shape((slots, inputs), BF16)),
    )(features, feature_arrived, dense, numbers, picks, *feature_hubs)
    mean_arrived = swap(rows.reshape(PEERS, FORWARD_ROWS, inputs))

    hidden, early_table, early_source, part, own_logits = kernel_call(
        early_part,
        (
            shape((nodes, width), BF16),
            shape((nodes + edges, 2 * inputs), BF16),
            shape((nodes + edges, width), BF16),
            shape((nodes, width), F32),
            shape((nodes, padded), F32),
        ),
        limit=8,
        flops=6 * nodes * edges * width,
        moved=8 * MIB,
    )(feature_table, mean_rows, mean_arrived, dense, weights)
    mean_hubs = gather_hubs(mean_arrived, [own_logits])
    base, edge_rows, mine, theirs = kernel_call(
        functools.partial(main_part, samples_all, classes),
        (
            shape((nodes, width), F32),
            shape((PEERS, EDGE_ROWS, TILE), BF16),
            shape((PEERS, SUM_ROWS, TILE), BF16),
            shape((PEERS, SUM_ROWS, TILE), BF16),
        ),
        [
            pltpu.VMEM((hubs, 2 * inputs), BF16),
            pltpu.VMEM((hubs, width), BF16),
            pltpu.VMEM((padded, nodes), BF16),
            pltpu.VMEM((STACK_ROWS, width), F32),
            pltpu.VMEM((CORES, PEERS, SUM_ROWS, TILE), F32),
        ],
        limit=16,
    )(
        feature_table, early_table, early_source, part, own_logits, dense, numbers, weights, *mean_hubs,
    )
    rows = kernel_call(sum_cores, shape((PEERS, BACK_ROWS, TILE), BF16))(mine, to_core(theirs), edge_rows)
    arrived = swap(rows)
    sums = kernel_call(sum_peers, shape((SUM_ROWS, TILE), F32))(arrived)
    base = kernel_call(
        return_edges,
        shape((nodes, width), F32),
        [pltpu.VMEM((slots, padded), BF16), pltpu.VMEM((slots, nodes), BF16)],
        limit=6,
        flops=2 * nodes * (edges * padded + width * padded),
        moved=4 * MIB,
    )(base, arrived, wanted, weights)
    pieces, total = kernel_call(
        sum_chips,
        (shape((PEERS, PIECE, TILE), BF16), shape((SUM_ROWS, TILE), F32)),
        in_specs=[VM] * CHIPS + [ANY],
    )(sums, *to_chips(sums), base)
    pieces = swap(pieces)
    grad_hidden = kernel_call(
        return_hubs,
        shape((nodes, width), F32),
        flops=4 * nodes * padded * width,
        moved=4 * MIB,
    )(base, total, wanted, weights)
    first_self_sum, first_mean_sum, self_sum, mean_sum, loss = kernel_call(
        functools.partial(weight_outputs, samples_all),
        (
            shape(first_self.shape, F32),
            shape(first_mean.shape, F32),
            shape((classes, width), F32),
            shape((classes, width), F32),
            shape((1, 1), F32),
        ),
        [pltpu.VMEM((STACK_ROWS, width), F32)],
    )(pieces, to_core(pieces))
    return hidden, grad_hidden, loss[0, 0], first_self_sum, first_mean_sum, self_sum.T, mean_sum.T


def solution(mesh):
    both = ("grp", "dev")
    placed = (
        P(both, None),
        P(both, None),
        P(both, None, None),
        P(both, None),
        P(both, None),
        P(both, None),
        P(both),
        P(both, None, None),
        P(both, None),
        P(both),
        P(),
        P(),
        P(),
        P(),
    )
    return jax.shard_map(
        on_device,
        mesh=mesh,
        in_specs=placed,
        out_specs=(P(both, None), P(both, None), P(), P(), P(), P(), P()),
        check_vma=False,
    )
```

```python
import functools

import jax
import jax.numpy as jnp
from jax import lax
from jax.experimental import pallas as pl
from jax.experimental.pallas import tpu as pltpu
from jax.sharding import PartitionSpec as P

F32 = jnp.float32
BF16 = jnp.bfloat16
I32 = jnp.int32
MIB = 1 << 20
TILE = 128
HALF = 64
PEERS = 32
CHIPS = 4
CORES = 2
HUBS_EACH = 4
CAPACITY = 32
GROUP_HUBS = PEERS * HUBS_EACH
FORWARD_ROWS = CAPACITY + 8
PEER_HUBS = CORES * CHIPS * HUBS_EACH
EDGE_ROWS = CAPACITY + CAPACITY // 2
HUB_ROWS = CHIPS * HUBS_EACH
HUB_PACKED = HUB_ROWS + HUB_ROWS // 2
STACK_ROWS = 640
SELF_AT = 256
LOSS_AT = 440
MEAN_AT = 448
CLASS_ROWS = 176
PIECE = STACK_ROWS // CORES * 4 // PEERS
SUM_ROWS = HUB_PACKED + PIECE
BACK_ROWS = EDGE_ROWS + SUM_ROWS

VM = pl.BlockSpec(memory_space=pltpu.VMEM)
SM = pl.BlockSpec(memory_space=pltpu.SMEM)
ANY = pl.BlockSpec(memory_space=pl.ANY)
HBM = pl.BlockSpec(memory_space=pltpu.HBM)


def nn(left, right):
    return jnp.dot(left, right, preferred_element_type=F32)


def nt(left, right):
    return lax.dot_general(left, right, (((1,), (1,)), ((), ())), preferred_element_type=F32)


def tn(left, right):
    return lax.dot_general(left, right, (((0,), (0,)), ((), ())), preferred_element_type=F32)


def split(values):
    high = values.astype(BF16)
    low = (values - high.astype(F32)).astype(BF16)
    return high, low


def one_hot(hit):
    return jnp.where(hit, 1.0, 0.0).astype(BF16)


def iota(dims, axis):
    return lax.broadcasted_iota(I32, dims, axis)


def kernel_call(body, outs, scratch=(), in_specs=None, limit=5, flops=0, moved=0):
    placed = {} if in_specs is None else {"in_specs": in_specs}
    return pl.pallas_call(
        body,
        out_shape=outs,
        **placed,
        scratch_shapes=list(scratch),
        compiler_params=pltpu.CompilerParams(vmem_limit_bytes=limit * MIB),
        cost_estimate=pl.CostEstimate(flops=flops, bytes_accessed=moved, transcendentals=0),
    )


def position():
    group = lax.axis_index("grp")
    return group // CORES, group % CORES


def fetch(pairs, sems):
    loads = [pltpu.make_async_copy(source, target, sems.at[i]) for i, (source, target) in enumerate(pairs)]
    for load in loads:
        load.start()
    return loads


def wanted_rows(send, counts, hub_ref):
    send = jnp.transpose(send)
    send = jnp.where(iota(send.shape, 0) < counts, send, -1)
    row = iota((FORWARD_ROWS - CAPACITY, PEERS), 0)
    hubs = jnp.full(row.shape, -1, I32)
    for k in range(HUBS_EACH):
        hubs = jnp.where(row == k, hub_ref[0, k], hubs)
    return jnp.concatenate([send, hubs], axis=0)


def pick_matrix(wanted, pick_ref):
    lane = iota((2 * FORWARD_ROWS, pick_ref.shape[1]), 1)
    for n in range(0, PEERS, 2):
        pair = jnp.concatenate([wanted[:, n : n + 1], wanted[:, n + 1 : n + 2]], axis=0)
        pick_ref[n * FORWARD_ROWS : (n + 2) * FORWARD_ROWS, :] = one_hot(pair == lane)


def send_features(
    features_any, send_any, count_any, hub_any, out_ref, pick_ref, features_ref, send_ref, count_ref, hub_ref, sems
):
    loads = fetch(
        (
            (send_any.at[0], send_ref),
            (count_any, count_ref),
            (hub_any, hub_ref),
            (features_any, features_ref),
        ),
        sems,
    )
    for load in loads[:-1]:
        load.wait()
    pick_matrix(wanted_rows(send_ref[...], count_ref[...], hub_ref), pick_ref)
    loads[-1].wait()
    out_ref[...] = nn(pick_ref[...], features_ref[...]).astype(BF16)


def build_dense(*refs):
    count = 13
    sources, refs = refs[:count], refs[count + 1 :]
    dense_ref, numbers_ref, weights_ref, wanted_ref, pick_ref, *places, sems = refs
    (
        adj_ref, dst_ref, src_ref, live_ref, send_ref, count_ref, hub_ref,
        sample_ref, label_ref, raw_self_ref, raw_mean_ref,
    ) = places
    targets = (
        adj_ref, dst_ref, src_ref, live_ref, send_ref, count_ref, hub_ref, sample_ref, label_ref,
        weights_ref.at[pl.ds(0, TILE)], weights_ref.at[pl.ds(TILE, TILE)], raw_self_ref, raw_mean_ref,
    )
    loads = fetch(zip(sources, targets), sems)
    dense_ref[...] = jnp.zeros_like(dense_ref)
    weights_ref[SELF_AT:, :] = jnp.zeros((weights_ref.shape[0] - SELF_AT, weights_ref.shape[1]), BF16)
    for load in loads:
        load.wait()

    def add(t, carry):
        rows = pl.ds(pl.multiple_of(dst_ref[0, t] * TILE, TILE), TILE)
        columns = pl.ds(pl.multiple_of(src_ref[0, t] * TILE, TILE), TILE)
        dense_ref[rows, columns] += adj_ref[t]
        return carry

    lax.fori_loop(0, live_ref[0], add, 0)
    classes = raw_self_ref.shape[0]
    weights_ref[SELF_AT : SELF_AT + classes, :] = raw_self_ref[...]
    weights_ref[2 * SELF_AT : 2 * SELF_AT + classes, :] = raw_mean_ref[...]
    wanted = wanted_rows(send_ref[...], count_ref[...], hub_ref)
    wanted_ref[...] = wanted
    pick_matrix(wanted, pick_ref)
    nodes = dense_ref.shape[0]
    node = iota((nodes, sample_ref.shape[1]), 0)
    times = jnp.sum(jnp.where(node == sample_ref[...], 1.0, 0.0), axis=1, keepdims=True)
    label = jnp.transpose(jnp.broadcast_to(label_ref[...], (8, nodes)))[:, 0:1]
    degree = jnp.maximum(nn(dense_ref[...], jnp.ones((dense_ref.shape[1], TILE), BF16)), 1.0)
    lane = iota(degree.shape, 1)
    numbers_ref[...] = jnp.where(lane == 0, degree, jnp.where(lane == 1, times, label.astype(F32)))


def group_hubs(arrived_ref, out_ref):
    low = iota((8, TILE), 0) < HUBS_EACH
    rows = []
    for n in range(0, PEERS, 2):
        first = arrived_ref[n, CAPACITY:FORWARD_ROWS, :].astype(F32)
        second = arrived_ref[n + 1, CAPACITY:FORWARD_ROWS, :].astype(F32)
        rows.append(jnp.where(low, first, pltpu.roll(second, HUBS_EACH, 0)))
    out_ref[...] = jnp.concatenate(rows, axis=0).astype(BF16)


def join_blocks(*refs):
    out_ref = refs[-1]
    for i in range(CHIPS):
        out_ref[i * GROUP_HUBS : (i + 1) * GROUP_HUBS, :] = refs[i][...]


def place_hubs(table_ref, start, hub_refs, lanes):
    chip, core = position()
    for there, hub_ref in zip((core, 1 - core), hub_refs):
        for i in range(CHIPS):
            other = (chip + CHIPS - i) % CHIPS
            at = start + (other * CORES + there) * GROUP_HUBS
            block = hub_ref[i * GROUP_HUBS : (i + 1) * GROUP_HUBS, :]
            table_ref[pl.ds(pl.multiple_of(at, GROUP_HUBS), GROUP_HUBS), lanes] = block


def early_means(features_ref, arrived_ref, dense_ref, own_hub_ref, part_ref, table_ref):
    nodes = features_ref.shape[0]
    edge_at = nodes + CORES * CHIPS * GROUP_HUBS
    table_ref[0:nodes, :] = features_ref[...]
    table_ref[nodes:edge_at, :] = jnp.zeros((edge_at - nodes, TILE), BF16)
    place_hubs(table_ref, nodes, (own_hub_ref,), slice(0, TILE))
    for n in range(PEERS):
        at = edge_at + n * CAPACITY
        table_ref[at : at + CAPACITY, :] = arrived_ref[n, 0:CAPACITY, :]
    part_ref[...] = nn(dense_ref[...], table_ref[...])


def first_means(part_ref, dense_ref, numbers_ref, pick_ref, other_hub_ref, mean_ref, out_ref):
    nodes = part_ref.shape[0]
    chip, core = position()
    total = part_ref[...]
    for i in range(CHIPS):
        other = (chip + CHIPS - i) % CHIPS
        at = nodes + (other * CORES + 1 - core) * GROUP_HUBS
        columns = dense_ref[:, pl.ds(pl.multiple_of(at, GROUP_HUBS), GROUP_HUBS)]
        total += nn(columns, other_hub_ref[i * GROUP_HUBS : (i + 1) * GROUP_HUBS, :])
    mean = (total / numbers_ref[:, 0:1]).astype(BF16)
    mean_ref[...] = mean
    out_ref[...] = nn(pick_ref[...], mean).astype(BF16)


def join_rests(first, second):
    return first + pltpu.roll(second, HALF, 1)


def part_rests(packed):
    low = iota(packed.shape, 1) < HALF
    return jnp.where(low, packed, 0.0), jnp.where(low, pltpu.roll(packed, HALF, 1), 0.0)


def early_part(
    features_ref, feature_arrived_ref, mean_ref, arrived_ref, dense_ref, weights_ref,
    hidden_ref, turned_ref, source_ref, part_ref, logits_ref, table_ref,
):
    nodes, width = hidden_ref.shape
    edges = PEERS * CAPACITY
    edge_at = dense_ref.shape[1] - edges
    table_ref[0:nodes, 0:TILE] = features_ref[...]
    table_ref[0:nodes, TILE:] = mean_ref[...]
    for n in range(PEERS):
        at = nodes + n * CAPACITY
        table_ref[at : at + CAPACITY, 0:TILE] = feature_arrived_ref[n, 0:CAPACITY, :]
        table_ref[at : at + CAPACITY, TILE:] = arrived_ref[n, 0:CAPACITY, :]
    for at in range(0, nodes + edges, nodes):
        rows = slice(at, at + nodes)
        linear = nn(table_ref[rows, :], weights_ref[0:SELF_AT, :])
        source_ref[rows, :] = jnp.maximum(linear, 0.0).astype(BF16)
        turned_ref[:, rows] = jnp.transpose(table_ref[rows, :])
    hidden = source_ref[0:nodes, :]
    hidden_ref[...] = hidden
    part_ref[...] = nn(dense_ref[:, 0:nodes], hidden) + nn(dense_ref[:, edge_at:], source_ref[nodes:, :])
    logits_ref[...] = nt(hidden, weights_ref[SELF_AT : 2 * SELF_AT, :])


def hub_part(
    dense_ref, weights_ref, features, means, others, turned_ref, source_ref, columns_ref
):
    nodes = dense_ref.shape[0]
    chip, core = position()
    there = 1 - core if others else core
    table = jnp.concatenate([features, means], axis=1)
    turned_ref[...] = jnp.transpose(table)
    source_ref[...] = jnp.maximum(nn(table, weights_ref[0:SELF_AT, :]), 0.0).astype(BF16)
    for i in range(CHIPS):
        other = (chip + CHIPS - i) % CHIPS
        at = pl.multiple_of(nodes + (other * CORES + there) * GROUP_HUBS, GROUP_HUBS)
        columns_ref[:, i * GROUP_HUBS : (i + 1) * GROUP_HUBS] = dense_ref[:, pl.ds(at, GROUP_HUBS)]
    return nn(columns_ref[...], source_ref[...])


def own_hub_part(
    dense_ref, weights_ref, part_ref, feature_ref, mean_ref, turned_ref, source_ref, columns_ref, out_ref
):
    total = hub_part(
        dense_ref, weights_ref, feature_ref[...], mean_ref[...], False, turned_ref, source_ref, columns_ref
    )
    out_ref[...] = part_ref[...] + total


def main_part(
    samples_all, classes,
    early_turned_ref, early_source_ref, logits_ref, own_turned_ref, own_source_ref, own_columns_ref, part_ref,
    dense_ref, numbers_ref, weights_ref, feature_ref, mean_ref,
    base_ref, edge_ref, mine_ref, theirs_ref,
    other_turned_ref, other_source_ref, other_columns_ref, scaled_ref, masked_ref, stack_ref, rest_ref,
):
    nodes, width = base_ref.shape
    padded = SELF_AT
    self_rows = slice(SELF_AT, 2 * SELF_AT)
    mean_rows = slice(2 * SELF_AT, 3 * SELF_AT)
    edge_at = dense_ref.shape[1] - PEERS * CAPACITY
    total = hub_part(
        dense_ref, weights_ref, feature_ref[...], mean_ref[...], True,
        other_turned_ref, other_source_ref, other_columns_ref,
    )
    hidden = early_source_ref[0:nodes, :]
    degree = numbers_ref[:, 0:1]
    times = numbers_ref[:, 1:2]
    label = numbers_ref[:, 2:3].astype(I32)
    mean = ((part_ref[...] + total) / degree).astype(BF16)
    logits = logits_ref[...] + nt(mean, weights_ref[mean_rows, :])

    lane = iota((nodes, padded), 1)
    real = lane < classes
    onehot = jnp.where(lane == label, 1.0, 0.0)
    top = jnp.max(jnp.where(real, logits, -jnp.inf), axis=1, keepdims=True)
    shifted = logits - top
    powers = jnp.where(real, jnp.exp(shifted), 0.0)
    total = jnp.sum(powers, axis=1, keepdims=True)
    chosen = jnp.sum(onehot * shifted, axis=1, keepdims=True)
    loss = jnp.sum(times * (jnp.log(total) - chosen), axis=0, keepdims=True)
    upstream = times * ((powers / total - onehot) / samples_all)
    upstream = upstream.astype(BF16)
    scaled_ref[...] = jnp.transpose((upstream.astype(F32) / degree).astype(BF16))

    def back(columns):
        found = nn(scaled_ref[...], columns)
        found = jnp.transpose(found.astype(BF16))
        return found, nn(found, weights_ref[mean_rows, :])

    def mask(at, source, grad):
        masked_ref[at : at + nodes, :] = jnp.where(source > 0, grad, 0.0).astype(BF16)

    low = iota((8, padded), 0) < HUBS_EACH
    hub_at = nodes + PEERS * CAPACITY
    for i, (columns_ref, source_ref, out_ref) in enumerate(
        ((own_columns_ref, own_source_ref, mine_ref), (other_columns_ref, other_source_ref, theirs_ref))
    ):
        found, spread = back(columns_ref[...])
        mask(hub_at + i * nodes, source_ref[...], spread)
        found = found.astype(F32)
        for n in range(0, PEERS, 2):
            first, second = [], []
            for pair in range(CHIPS // 2):
                at = 2 * pair * GROUP_HUBS + n * HUBS_EACH
                even = found[at : at + 8]
                odd = found[at + GROUP_HUBS : at + GROUP_HUBS + 8]
                first.append(jnp.where(low, even, pltpu.roll(odd, HUBS_EACH, 0)))
                second.append(jnp.where(low, pltpu.roll(even, HUBS_EACH, 0), odd))
            for member, blocks in ((n, first), (n + 1, second)):
                rows = jnp.concatenate([block[:, 0:TILE] for block in blocks], axis=0)
                out_ref[member, 0:HUB_ROWS, :] = rows.astype(BF16)
                rest_ref[i, member] = join_rests(blocks[0][:, TILE:], blocks[1][:, TILE:])

    unused, spread = back(dense_ref[:, 0:nodes])
    base = nn(upstream, weights_ref[self_rows, :]) + spread
    base_ref[...] = base
    mask(0, hidden, base)
    each = nodes // CAPACITY
    for i in range(PEERS // each):
        found, spread = back(dense_ref[:, edge_at + i * nodes : edge_at + (i + 1) * nodes])
        at = (i + 1) * nodes
        mask(at, early_source_ref[at : at + nodes, :], spread)
        for p in range(each):
            at = p * CAPACITY
            rest = found[at : at + CAPACITY, TILE:].astype(F32)
            edge_ref[i * each + p, 0:CAPACITY, :] = found[at : at + CAPACITY, 0:TILE]
            edge_ref[i * each + p, CAPACITY:EDGE_ROWS, :] = join_rests(
                rest[0 : CAPACITY // 2], rest[CAPACITY // 2 :]
            ).astype(BF16)

    stack_ref[SELF_AT:, :] = jnp.zeros((STACK_ROWS - SELF_AT, width), F32)
    upstream_turned = jnp.transpose(upstream)
    stack_ref[SELF_AT : SELF_AT + CLASS_ROWS, :] = nn(upstream_turned, hidden)[0:CLASS_ROWS]
    stack_ref[MEAN_AT : MEAN_AT + CLASS_ROWS, :] = nn(upstream_turned, mean)[0:CLASS_ROWS]
    loss_high = loss.astype(BF16).astype(F32)
    place = iota((8, width), 0)
    marks = jnp.where(place == 0, loss_high, 0.0)
    stack_ref[LOSS_AT : LOSS_AT + 8, :] = jnp.where(place == 1, loss - loss_high, marks)
    stack_ref[0:SELF_AT, :] = (
        nn(early_turned_ref[...], masked_ref[0:hub_at, :])
        + nn(own_turned_ref[...], masked_ref[hub_at : hub_at + nodes, :])
        + nn(other_turned_ref[...], masked_ref[hub_at + nodes :, :])
    )
    unused, core = position()
    for i, (there, out_ref) in enumerate(((core, mine_ref), (1 - core, theirs_ref))):
        for n in range(PEERS):
            at = there * (STACK_ROWS // CORES) + PIECE * (n % 8)
            lanes = slice(TILE * (n // 8), TILE * (n // 8 + 1))
            piece = stack_ref[pl.ds(pl.multiple_of(at, 8), PIECE), lanes]
            rows = jnp.concatenate([rest_ref[i, n], piece], axis=0)
            out_ref[n, HUB_ROWS:SUM_ROWS, :] = rows.astype(BF16)


def sum_cores(mine_ref, arrived_ref, edge_ref, out_ref):
    out_ref[:, 0:EDGE_ROWS, :] = edge_ref[...]
    total = mine_ref[...].astype(F32) + arrived_ref[...].astype(F32)
    out_ref[:, EDGE_ROWS:BACK_ROWS, :] = total.astype(BF16)


def sum_peers(arrived_ref, out_ref):
    total = arrived_ref[0, EDGE_ROWS:BACK_ROWS, :].astype(F32)
    for n in range(1, PEERS):
        total += arrived_ref[n, EDGE_ROWS:BACK_ROWS, :].astype(F32)
    out_ref[...] = total


def return_edges(base_ref, arrived_ref, wanted_ref, weights_ref, out_ref, found_ref, pick_ref):
    pick_matrix(wanted_ref[...], pick_ref)
    found_ref[...] = jnp.zeros_like(found_ref)
    for n in range(PEERS):
        at = n * FORWARD_ROWS
        first, second = part_rests(arrived_ref[n, CAPACITY:EDGE_ROWS, :].astype(F32))
        rest = jnp.concatenate([first, second], axis=0).astype(BF16)
        found_ref[at : at + CAPACITY, 0:TILE] = arrived_ref[n, 0:CAPACITY, :]
        found_ref[at : at + CAPACITY, TILE:] = rest
    rows = tn(pick_ref[...], found_ref[...])
    out_ref[...] = base_ref[...] + nn(rows.astype(BF16), weights_ref[2 * SELF_AT :, :])


def sum_chips(*refs):
    sum_refs, out_ref, hub_ref = refs[:CHIPS], refs[-2], refs[-1]
    piece = sum_refs[0][HUB_PACKED:SUM_ROWS, :]
    for sum_ref in sum_refs[1:]:
        piece += sum_ref[HUB_PACKED:SUM_ROWS, :]
    hubs = jnp.zeros((8, 2 * TILE), F32)
    for shift, sum_ref in enumerate(sum_refs):
        i = (CHIPS - shift) % CHIPS
        main = sum_ref[8 * (i // 2) : 8 * (i // 2) + 8, :]
        rest = part_rests(sum_ref[HUB_ROWS:HUB_PACKED, :])[i // 2]
        rows = jnp.concatenate([main, rest], axis=1)
        hubs += pltpu.roll(rows, HUBS_EACH, 0) if i % 2 else rows
    hub_ref[...] = hubs
    unused, core = position()
    holder = (core == LOSS_AT * CORES // STACK_ROWS) & (lax.axis_index("dev") == LOSS_AT % (STACK_ROWS // CORES) // PIECE)
    rest = piece[0:1] - piece[0:1].astype(BF16).astype(F32)
    row = iota(piece.shape, 0)
    piece = jnp.where((row == 2) & holder, rest, piece).astype(BF16)
    for n in range(PEERS):
        out_ref[n] = piece


def return_hubs(base_ref, hub_ref, wanted_ref, weights_ref, out_ref):
    nodes = out_ref.shape[0]
    high, low = split(nn(hub_ref[...].astype(BF16), weights_ref[2 * SELF_AT :, :]))
    owner = one_hot(wanted_ref[CAPACITY:FORWARD_ROWS, 0:1] == iota((8, nodes), 1))
    out_ref[...] = base_ref[...] + tn(owner, high) + tn(owner, low)


def weight_outputs(samples_all, mine_ref, theirs_ref, first_self_ref, first_mean_ref, self_ref, mean_ref, loss_ref, stack_ref):
    unused, core = position()
    half = STACK_ROWS // CORES
    for n in range(PEERS):
        mine = mine_ref[n].astype(F32)
        theirs = theirs_ref[n].astype(F32)
        lanes = slice(TILE * (n // 8), TILE * (n // 8 + 1))
        at = PIECE * (n % 8)
        stack_ref[at : at + PIECE, lanes] = jnp.where(core == 0, mine, theirs)
        stack_ref[half + at : half + at + PIECE, lanes] = jnp.where(core == 0, theirs, mine)
    classes = self_ref.shape[0]
    first_self_ref[...] = stack_ref[0:TILE, :]
    first_mean_ref[...] = stack_ref[TILE : 2 * TILE, :]
    self_ref[...] = stack_ref[SELF_AT : SELF_AT + classes, :]
    mean_ref[...] = stack_ref[MEAN_AT : MEAN_AT + classes, :]
    parts = stack_ref[LOSS_AT : LOSS_AT + 8, 0:1]
    loss_ref[...] = (parts[0:1] + parts[1:2] + parts[2:3]) / samples_all


def shape(dims, dtype):
    return jax.ShapeDtypeStruct(dims, dtype)


def swap(values):
    return lax.all_to_all(values, "dev", split_axis=0, concat_axis=0, tiled=True)


def to_core(values):
    return lax.ppermute(values, "grp", [(i, i ^ 1) for i in range(CHIPS * CORES)])


def to_chips(values):
    every = CHIPS * CORES
    return [
        lax.ppermute(values, "grp", [(i, (i + CORES * shift) % every) for i in range(every)])
        for shift in range(1, CHIPS)
    ]


def on_device(
    features,
    hub_list,
    send_list,
    send_count,
    tile_dst,
    tile_src,
    tile_count,
    tile_adj,
    sample_ids,
    labels,
    first_self,
    first_mean,
    second_self,
    second_mean,
):
    nodes, inputs = features.shape
    width, classes = second_self.shape
    hubs = CHIPS * CORES * PEERS * HUBS_EACH
    edges = PEERS * CAPACITY
    table = nodes + hubs + edges
    padded = 2 * TILE
    samples_all = float(sample_ids.shape[1] * CHIPS * CORES * PEERS)

    slots = PEERS * FORWARD_ROWS

    def gather_hubs(arrived, beside):
        own = kernel_call(group_hubs, shape((GROUP_HUBS, inputs), BF16))(arrived)
        blocks = kernel_call(
            join_blocks,
            shape((CHIPS * GROUP_HUBS, inputs), BF16),
            in_specs=[VM] * CHIPS + [ANY] * len(beside),
        )(own, *to_chips(own), *beside)
        return blocks, to_core(blocks)

    rows = kernel_call(
        send_features,
        shape((slots, inputs), BF16),
        [
            pltpu.VMEM((slots, nodes), BF16),
            pltpu.VMEM((nodes, inputs), BF16),
            pltpu.VMEM(send_list.shape[1:], I32),
            pltpu.VMEM(send_count.shape, I32),
            pltpu.SMEM(hub_list.shape, I32),
            pltpu.SemaphoreType.DMA((4,)),
        ],
        [HBM] * 4,
    )(*(pltpu.with_memory_space_constraint(operand, pltpu.HBM) for operand in (features, send_list, send_count, hub_list)))
    feature_arrived = swap(rows.reshape(PEERS, FORWARD_ROWS, inputs))
    raw = (second_self.T, second_mean.T)
    operands = (
        tile_adj, tile_dst, tile_src, tile_count, send_list[0], send_count, hub_list,
        sample_ids, labels.reshape(1, nodes), first_self, first_mean, *raw,
    )
    dense, numbers, weights, wanted, picks = kernel_call(
        build_dense,
        (
            shape((nodes, table), BF16),
            shape((nodes, TILE), F32),
            shape((3 * padded, width), BF16),
            shape((FORWARD_ROWS, PEERS), I32),
            shape((slots, nodes), BF16),
        ),
        [
            pltpu.VMEM(tile_adj.shape, BF16),
            pltpu.SMEM(tile_dst.shape, I32),
            pltpu.SMEM(tile_src.shape, I32),
            pltpu.SMEM(tile_count.shape, I32),
            pltpu.VMEM(send_list.shape[1:], I32),
            pltpu.VMEM(send_count.shape, I32),
            pltpu.SMEM(hub_list.shape, I32),
            pltpu.VMEM(sample_ids.shape, I32),
            pltpu.VMEM((1, nodes), I32),
            pltpu.VMEM(raw[0].shape, BF16),
            pltpu.VMEM(raw[1].shape, BF16),
            pltpu.SemaphoreType.DMA((len(operands),)),
        ],
        [HBM] * len(operands) + [ANY],
        flops=2 * nodes * table * TILE,
        moved=8 * MIB,
    )(
        *(
            operand if operand is tile_count else pltpu.with_memory_space_constraint(operand, pltpu.HBM)
            for operand in operands
        ),
        feature_arrived,
    )
    feature_hubs = gather_hubs(feature_arrived, [numbers])
    part = kernel_call(
        early_means,
        shape((nodes, inputs), F32),
        [pltpu.VMEM((table, inputs), BF16)],
        flops=2 * nodes * table * inputs,
        moved=4 * MIB,
    )(features, feature_arrived, dense, feature_hubs[0])
    mean_rows, rows = kernel_call(
        first_means, (shape((nodes, inputs), BF16), shape((slots, inputs), BF16))
    )(part, dense, numbers, picks, feature_hubs[1])
    mean_arrived = swap(rows.reshape(PEERS, FORWARD_ROWS, inputs))

    hidden, early_turned, early_source, part, own_logits = kernel_call(
        early_part,
        (
            shape((nodes, width), BF16),
            shape((2 * inputs, nodes + edges), BF16),
            shape((nodes + edges, width), BF16),
            shape((nodes, width), F32),
            shape((nodes, padded), F32),
        ),
        [pltpu.VMEM((nodes + edges, 2 * inputs), BF16)],
        limit=8,
        flops=6 * nodes * edges * width,
        moved=8 * MIB,
    )(features, feature_arrived, mean_rows, mean_arrived, dense, weights)
    mean_hubs = gather_hubs(mean_arrived, [own_logits])
    half = CHIPS * GROUP_HUBS
    own_turned, own_source, own_columns, part = kernel_call(
        own_hub_part,
        (
            shape((2 * inputs, half), BF16),
            shape((half, width), BF16),
            shape((nodes, half), BF16),
            shape((nodes, width), F32),
        ),
        limit=6,
        flops=4 * nodes * half * width,
        moved=4 * MIB,
    )(dense, weights, part, feature_hubs[0], mean_hubs[0])
    base, edge_rows, mine, theirs = kernel_call(
        functools.partial(main_part, samples_all, classes),
        (
            shape((nodes, width), F32),
            shape((PEERS, EDGE_ROWS, TILE), BF16),
            shape((PEERS, SUM_ROWS, TILE), BF16),
            shape((PEERS, SUM_ROWS, TILE), BF16),
        ),
        [
            pltpu.VMEM((2 * inputs, half), BF16),
            pltpu.VMEM((half, width), BF16),
            pltpu.VMEM((nodes, half), BF16),
            pltpu.VMEM((padded, nodes), BF16),
            pltpu.VMEM((table, width), BF16),
            pltpu.VMEM((STACK_ROWS, width), F32),
            pltpu.VMEM((CORES, PEERS, HUB_PACKED - HUB_ROWS, TILE), F32),
        ],
        limit=20,
    )(
        early_turned, early_source, own_logits, own_turned, own_source, own_columns, part,
        dense, numbers, weights, feature_hubs[1], mean_hubs[1],
    )
    rows = kernel_call(sum_cores, shape((PEERS, BACK_ROWS, TILE), BF16))(mine, to_core(theirs), edge_rows)
    arrived = swap(rows)
    sums = kernel_call(sum_peers, shape((SUM_ROWS, TILE), F32))(arrived)
    base = kernel_call(
        return_edges,
        shape((nodes, width), F32),
        [pltpu.VMEM((slots, padded), BF16), pltpu.VMEM((slots, nodes), BF16)],
        limit=6,
        flops=2 * nodes * (edges * padded + width * padded),
        moved=4 * MIB,
    )(base, arrived, wanted, weights)
    pieces, own_hubs = kernel_call(
        sum_chips,
        (shape((PEERS, PIECE, TILE), BF16), shape((8, padded), F32)),
        in_specs=[VM] * CHIPS + [ANY],
    )(sums, *to_chips(sums), base)
    pieces = swap(pieces)
    grad_hidden = kernel_call(
        return_hubs,
        shape((nodes, width), F32),
        flops=4 * nodes * padded * width,
        moved=4 * MIB,
    )(base, own_hubs, wanted, weights)
    first_self_sum, first_mean_sum, self_sum, mean_sum, loss = kernel_call(
        functools.partial(weight_outputs, samples_all),
        (
            shape(first_self.shape, F32),
            shape(first_mean.shape, F32),
            shape((classes, width), F32),
            shape((classes, width), F32),
            shape((1, 1), F32),
        ),
        [pltpu.VMEM((STACK_ROWS, width), F32)],
    )(pieces, to_core(pieces))
    return hidden, grad_hidden, loss[0, 0], first_self_sum, first_mean_sum, self_sum.T, mean_sum.T


def solution(mesh):
    both = ("grp", "dev")
    placed = (
        P(both, None),
        P(both, None),
        P(both, None, None),
        P(both, None),
        P(both, None),
        P(both, None),
        P(both),
        P(both, None, None),
        P(both, None),
        P(both),
        P(),
        P(),
        P(),
        P(),
    )
    return jax.shard_map(
        on_device,
        mesh=mesh,
        in_specs=placed,
        out_specs=(P(both, None), P(both, None), P(), P(), P(), P(), P()),
        check_vma=False,
    )
```

```python
import functools

import jax
import jax.numpy as jnp
from jax import lax
from jax.experimental import pallas as pl
from jax.experimental.pallas import tpu as pltpu
from jax.sharding import PartitionSpec as P

F32 = jnp.float32
BF16 = jnp.bfloat16
I32 = jnp.int32
MIB = 1 << 20
TILE = 128
HALF = 64
PEERS = 32
CHIPS = 4
CORES = 2
HUBS_EACH = 4
CAPACITY = 32
GROUP_HUBS = PEERS * HUBS_EACH
FORWARD_ROWS = CAPACITY + 8
PEER_HUBS = CORES * CHIPS * HUBS_EACH
EDGE_ROWS = CAPACITY + CAPACITY // 2
HUB_ROWS = CHIPS * HUBS_EACH
HUB_PACKED = HUB_ROWS + HUB_ROWS // 2
STACK_ROWS = 640
SELF_AT = 256
LOSS_AT = 440
MEAN_AT = 448
CLASS_ROWS = 176
PIECE = STACK_ROWS // CORES * 4 // PEERS
SUM_ROWS = HUB_PACKED + PIECE
BACK_ROWS = EDGE_ROWS + SUM_ROWS

VM = pl.BlockSpec(memory_space=pltpu.VMEM)
SM = pl.BlockSpec(memory_space=pltpu.SMEM)
ANY = pl.BlockSpec(memory_space=pl.ANY)
HBM = pl.BlockSpec(memory_space=pltpu.HBM)


def nn(left, right):
    return jnp.dot(left, right, preferred_element_type=F32)


def nt(left, right):
    return lax.dot_general(left, right, (((1,), (1,)), ((), ())), preferred_element_type=F32)


def tn(left, right):
    return lax.dot_general(left, right, (((0,), (0,)), ((), ())), preferred_element_type=F32)


def split(values):
    high = values.astype(BF16)
    low = (values - high.astype(F32)).astype(BF16)
    return high, low


def one_hot(hit):
    return jnp.where(hit, 1.0, 0.0).astype(BF16)


def iota(dims, axis):
    return lax.broadcasted_iota(I32, dims, axis)


def kernel_call(body, outs, scratch=(), in_specs=None, limit=5, flops=0, moved=0):
    placed = {} if in_specs is None else {"in_specs": in_specs}
    return pl.pallas_call(
        body,
        out_shape=outs,
        **placed,
        scratch_shapes=list(scratch),
        compiler_params=pltpu.CompilerParams(vmem_limit_bytes=limit * MIB),
        cost_estimate=pl.CostEstimate(flops=flops, bytes_accessed=moved, transcendentals=0),
    )


def position():
    group = lax.axis_index("grp")
    return group // CORES, group % CORES


def before(place, step, size):
    return (place + size - step) % size


def fetch(pairs, sems):
    loads = [pltpu.make_async_copy(source, target, sems.at[i]) for i, (source, target) in enumerate(pairs)]
    for load in loads:
        load.start()
    return loads


def wanted_rows(send, counts, hub_ref):
    send = jnp.transpose(send)
    send = jnp.where(iota(send.shape, 0) < counts, send, -1)
    row = iota((FORWARD_ROWS - CAPACITY, PEERS), 0)
    hubs = jnp.full(row.shape, -1, I32)
    for k in range(HUBS_EACH):
        hubs = jnp.where(row == k, hub_ref[0, k], hubs)
    return jnp.concatenate([send, hubs], axis=0)


def pick_matrix(wanted, pick_ref):
    lane = iota((2 * FORWARD_ROWS, pick_ref.shape[1]), 1)
    for n in range(0, PEERS, 2):
        pair = jnp.concatenate([wanted[:, n : n + 1], wanted[:, n + 1 : n + 2]], axis=0)
        pick_ref[n * FORWARD_ROWS : (n + 2) * FORWARD_ROWS, :] = one_hot(pair == lane)


def send_features(
    features_any, send_any, count_any, hub_any, out_ref, pick_ref, features_ref, send_ref, count_ref, hub_ref, sems
):
    loads = fetch(
        (
            (send_any.at[0], send_ref),
            (count_any, count_ref),
            (hub_any, hub_ref),
            (features_any, features_ref),
        ),
        sems,
    )
    for load in loads[:-1]:
        load.wait()
    pick_matrix(wanted_rows(send_ref[...], count_ref[...], hub_ref), pick_ref)
    loads[-1].wait()
    out_ref[...] = nn(pick_ref[...], features_ref[...]).astype(BF16)


def build_dense(*refs):
    count = 13
    sources, refs = refs[:count], refs[count + 1 :]
    dense_ref, numbers_ref, weights_ref, wanted_ref, pick_ref, *places, sems = refs
    (
        adj_ref, dst_ref, src_ref, live_ref, send_ref, count_ref, hub_ref,
        sample_ref, label_ref, raw_self_ref, raw_mean_ref,
    ) = places
    targets = (
        adj_ref, dst_ref, src_ref, live_ref, send_ref, count_ref, hub_ref, sample_ref, label_ref,
        weights_ref.at[pl.ds(0, TILE)], weights_ref.at[pl.ds(TILE, TILE)], raw_self_ref, raw_mean_ref,
    )
    loads = fetch(zip(sources, targets), sems)
    dense_ref[...] = jnp.zeros_like(dense_ref)
    weights_ref[SELF_AT:, :] = jnp.zeros((weights_ref.shape[0] - SELF_AT, weights_ref.shape[1]), BF16)
    for load in loads:
        load.wait()

    def add(t, carry):
        rows = pl.ds(pl.multiple_of(dst_ref[0, t] * TILE, TILE), TILE)
        columns = pl.ds(pl.multiple_of(src_ref[0, t] * TILE, TILE), TILE)
        dense_ref[rows, columns] += adj_ref[t]
        return carry

    lax.fori_loop(0, live_ref[0], add, 0)
    classes = raw_self_ref.shape[0]
    weights_ref[SELF_AT : SELF_AT + classes, :] = raw_self_ref[...]
    weights_ref[2 * SELF_AT : 2 * SELF_AT + classes, :] = raw_mean_ref[...]
    wanted = wanted_rows(send_ref[...], count_ref[...], hub_ref)
    wanted_ref[...] = wanted
    pick_matrix(wanted, pick_ref)
    nodes = dense_ref.shape[0]
    node = iota((nodes, sample_ref.shape[1]), 0)
    times = jnp.sum(jnp.where(node == sample_ref[...], 1.0, 0.0), axis=1, keepdims=True)
    label = jnp.transpose(jnp.broadcast_to(label_ref[...], (8, nodes)))[:, 0:1]
    degree = jnp.maximum(nn(dense_ref[...], jnp.ones((dense_ref.shape[1], TILE), BF16)), 1.0)
    lane = iota(degree.shape, 1)
    numbers_ref[...] = jnp.where(lane == 0, degree, jnp.where(lane == 1, times, label.astype(F32)))


def build_turned(adj_any, dst_any, src_any, live_ref, unused, turned_ref, adj_ref, dst_ref, src_ref, sems):
    loads = fetch(((dst_any, dst_ref), (src_any, src_ref), (adj_any, adj_ref)), sems)
    turned_ref[...] = jnp.zeros_like(turned_ref)
    for load in loads:
        load.wait()

    def add(t, carry):
        rows = pl.ds(pl.multiple_of(src_ref[0, t] * TILE, TILE), TILE)
        columns = pl.ds(pl.multiple_of(dst_ref[0, t] * TILE, TILE), TILE)
        turned_ref[rows, columns] += jnp.transpose(adj_ref[t])
        return carry

    lax.fori_loop(0, live_ref[0], add, 0)


def group_hubs(arrived_ref, out_ref):
    low = iota((8, TILE), 0) < HUBS_EACH
    rows = []
    for n in range(0, PEERS, 2):
        first = arrived_ref[n, CAPACITY:FORWARD_ROWS, :].astype(F32)
        second = arrived_ref[n + 1, CAPACITY:FORWARD_ROWS, :].astype(F32)
        rows.append(jnp.where(low, first, pltpu.roll(second, HUBS_EACH, 0)))
    out_ref[...] = jnp.concatenate(rows, axis=0).astype(BF16)


def join_blocks(*refs):
    out_ref = refs[-1]
    for i in range(CHIPS):
        out_ref[i * GROUP_HUBS : (i + 1) * GROUP_HUBS, :] = refs[i][...]


def place_hubs(table_ref, start, hub_refs, lanes):
    chip, core = position()
    for there, hub_ref in zip((core, 1 - core), hub_refs):
        for i in range(CHIPS):
            other = (chip + CHIPS - i) % CHIPS
            at = start + (other * CORES + there) * GROUP_HUBS
            block = hub_ref[i * GROUP_HUBS : (i + 1) * GROUP_HUBS, :]
            table_ref[pl.ds(pl.multiple_of(at, GROUP_HUBS), GROUP_HUBS), lanes] = block


def early_means(features_ref, arrived_ref, dense_ref, own_hub_ref, part_ref, table_ref):
    nodes = features_ref.shape[0]
    edge_at = nodes + CORES * CHIPS * GROUP_HUBS
    table_ref[0:nodes, :] = features_ref[...]
    table_ref[nodes:edge_at, :] = jnp.zeros((edge_at - nodes, TILE), BF16)
    place_hubs(table_ref, nodes, (own_hub_ref,), slice(0, TILE))
    for n in range(PEERS):
        at = edge_at + n * CAPACITY
        table_ref[at : at + CAPACITY, :] = arrived_ref[n, 0:CAPACITY, :]
    part_ref[...] = nn(dense_ref[...], table_ref[...])


def first_means(part_ref, dense_ref, numbers_ref, pick_ref, other_hub_ref, mean_ref, out_ref):
    nodes = part_ref.shape[0]
    chip, core = position()
    total = part_ref[...]
    for i in range(CHIPS):
        other = (chip + CHIPS - i) % CHIPS
        at = nodes + (other * CORES + 1 - core) * GROUP_HUBS
        columns = dense_ref[:, pl.ds(pl.multiple_of(at, GROUP_HUBS), GROUP_HUBS)]
        total += nn(columns, other_hub_ref[i * GROUP_HUBS : (i + 1) * GROUP_HUBS, :])
    mean = (total / numbers_ref[:, 0:1]).astype(BF16)
    mean_ref[...] = mean
    out_ref[...] = nn(pick_ref[...], mean).astype(BF16)


def join_rests(first, second):
    return first + pltpu.roll(second, HALF, 1)


def part_rests(packed):
    low = iota(packed.shape, 1) < HALF
    return jnp.where(low, packed, 0.0), jnp.where(low, pltpu.roll(packed, HALF, 1), 0.0)


def early_part(
    features_ref, feature_arrived_ref, mean_ref, arrived_ref, dense_ref, weights_ref,
    hidden_ref, turned_ref, source_ref, part_ref, logits_ref, table_ref,
):
    nodes, width = hidden_ref.shape
    edges = PEERS * CAPACITY
    edge_at = dense_ref.shape[1] - edges
    table_ref[0:nodes, 0:TILE] = features_ref[...]
    table_ref[0:nodes, TILE:] = mean_ref[...]
    for n in range(PEERS):
        at = nodes + n * CAPACITY
        table_ref[at : at + CAPACITY, 0:TILE] = feature_arrived_ref[n, 0:CAPACITY, :]
        table_ref[at : at + CAPACITY, TILE:] = arrived_ref[n, 0:CAPACITY, :]
    for at in range(0, nodes + edges, nodes):
        rows = slice(at, at + nodes)
        linear = nn(table_ref[rows, :], weights_ref[0:SELF_AT, :])
        source_ref[rows, :] = jnp.maximum(linear, 0.0).astype(BF16)
        turned_ref[:, rows] = jnp.transpose(table_ref[rows, :])
    hidden = source_ref[0:nodes, :]
    hidden_ref[...] = hidden
    part_ref[...] = nn(dense_ref[:, 0:nodes], hidden) + nn(dense_ref[:, edge_at:], source_ref[nodes:, :])
    logits_ref[...] = nt(hidden, weights_ref[SELF_AT : 2 * SELF_AT, :])


def hub_part(
    dense_ref, weights_ref, features, means, others, turned_ref, source_ref, columns_ref
):
    nodes = dense_ref.shape[0]
    chip, core = position()
    there = 1 - core if others else core
    table = jnp.concatenate([features, means], axis=1)
    turned_ref[...] = jnp.transpose(table)
    source_ref[...] = jnp.maximum(nn(table, weights_ref[0:SELF_AT, :]), 0.0).astype(BF16)
    for i in range(CHIPS):
        other = (chip + CHIPS - i) % CHIPS
        at = pl.multiple_of(nodes + (other * CORES + there) * GROUP_HUBS, GROUP_HUBS)
        columns_ref[:, i * GROUP_HUBS : (i + 1) * GROUP_HUBS] = dense_ref[:, pl.ds(at, GROUP_HUBS)]
    return nn(columns_ref[...], source_ref[...])


def own_hub_part(
    dense_ref, weights_ref, part_ref, feature_ref, mean_ref, turned_ref, source_ref, out_ref, columns_ref
):
    total = hub_part(
        dense_ref, weights_ref, feature_ref[...], mean_ref[...], False, turned_ref, source_ref, columns_ref
    )
    out_ref[...] = part_ref[...] + total


def main_part(
    samples_all, classes,
    early_turned_ref, early_source_ref, logits_ref, own_turned_ref, own_source_ref, part_ref,
    dense_ref, adjoint_ref, numbers_ref, weights_ref, feature_ref, mean_ref,
    base_ref, edge_ref, mine_ref, theirs_ref,
    other_turned_ref, other_source_ref, other_columns_ref, order_ref, scaled_ref, masked_ref, stack_ref, rest_ref,
):
    nodes, width = base_ref.shape
    padded = SELF_AT
    self_rows = slice(SELF_AT, 2 * SELF_AT)
    mean_rows = slice(2 * SELF_AT, 3 * SELF_AT)
    edge_at = dense_ref.shape[1] - PEERS * CAPACITY
    total = hub_part(
        dense_ref, weights_ref, feature_ref[...], mean_ref[...], True,
        other_turned_ref, other_source_ref, other_columns_ref,
    )
    hidden = early_source_ref[0:nodes, :]
    degree = numbers_ref[:, 0:1]
    times = numbers_ref[:, 1:2]
    label = numbers_ref[:, 2:3].astype(I32)
    mean = ((part_ref[...] + total) / degree).astype(BF16)
    logits = logits_ref[...] + nt(mean, weights_ref[mean_rows, :])

    lane = iota((nodes, padded), 1)
    real = lane < classes
    onehot = jnp.where(lane == label, 1.0, 0.0)
    top = jnp.max(jnp.where(real, logits, -jnp.inf), axis=1, keepdims=True)
    shifted = logits - top
    powers = jnp.where(real, jnp.exp(shifted), 0.0)
    total = jnp.sum(powers, axis=1, keepdims=True)
    chosen = jnp.sum(onehot * shifted, axis=1, keepdims=True)
    loss = jnp.sum(times * (jnp.log(total) - chosen), axis=0, keepdims=True)
    upstream = times * ((powers / total - onehot) / samples_all)
    upstream = upstream.astype(BF16)
    scaled_ref[...] = (upstream.astype(F32) / degree).astype(BF16)

    def back(rows):
        found = nn(rows, scaled_ref[...])
        return found, nn(found.astype(BF16), weights_ref[mean_rows, :])

    def mask(at, source, grad):
        masked_ref[at : at + nodes, :] = jnp.where(source > 0, grad, 0.0).astype(BF16)

    low = iota((8, padded), 0) < HUBS_EACH
    hub_at = nodes + PEERS * CAPACITY
    chip, core = position()
    for i, (there, source_ref, out_ref) in enumerate(
        ((core, own_source_ref, mine_ref), (1 - core, other_source_ref, theirs_ref))
    ):
        for block in range(CHIPS):
            at = nodes + (before(chip, block, CHIPS) * CORES + there) * GROUP_HUBS
            rows = adjoint_ref[pl.ds(pl.multiple_of(at, GROUP_HUBS), GROUP_HUBS), :]
            order_ref[block * GROUP_HUBS : (block + 1) * GROUP_HUBS, :] = rows
        found, spread = back(order_ref[...])
        mask(hub_at + i * nodes, source_ref[...], spread)
        for n in range(0, PEERS, 2):
            first, second = [], []
            for pair in range(CHIPS // 2):
                at = 2 * pair * GROUP_HUBS + n * HUBS_EACH
                even = found[at : at + 8]
                odd = found[at + GROUP_HUBS : at + GROUP_HUBS + 8]
                first.append(jnp.where(low, even, pltpu.roll(odd, HUBS_EACH, 0)))
                second.append(jnp.where(low, pltpu.roll(even, HUBS_EACH, 0), odd))
            for member, blocks in ((n, first), (n + 1, second)):
                rows = jnp.concatenate([block[:, 0:TILE] for block in blocks], axis=0)
                out_ref[member, 0:HUB_ROWS, :] = rows.astype(BF16)
                rest_ref[i, member] = join_rests(blocks[0][:, TILE:], blocks[1][:, TILE:])

    unused, spread = back(adjoint_ref[0:nodes, :])
    base = nn(upstream, weights_ref[self_rows, :]) + spread
    base_ref[...] = base
    mask(0, hidden, base)
    each = nodes // CAPACITY
    for i in range(PEERS // each):
        found, spread = back(adjoint_ref[edge_at + i * nodes : edge_at + (i + 1) * nodes, :])
        at = (i + 1) * nodes
        mask(at, early_source_ref[at : at + nodes, :], spread)
        for p in range(each):
            at = p * CAPACITY
            rest = found[at : at + CAPACITY, TILE:]
            edge_ref[i * each + p, 0:CAPACITY, :] = found[at : at + CAPACITY, 0:TILE].astype(BF16)
            edge_ref[i * each + p, CAPACITY:EDGE_ROWS, :] = join_rests(
                rest[0 : CAPACITY // 2], rest[CAPACITY // 2 :]
            ).astype(BF16)

    stack_ref[SELF_AT:, :] = jnp.zeros((STACK_ROWS - SELF_AT, width), F32)
    upstream_turned = jnp.transpose(upstream)
    stack_ref[SELF_AT : SELF_AT + CLASS_ROWS, :] = nn(upstream_turned, hidden)[0:CLASS_ROWS]
    stack_ref[MEAN_AT : MEAN_AT + CLASS_ROWS, :] = nn(upstream_turned, mean)[0:CLASS_ROWS]
    loss_high = loss.astype(BF16).astype(F32)
    place = iota((8, width), 0)
    marks = jnp.where(place == 0, loss_high, 0.0)
    stack_ref[LOSS_AT : LOSS_AT + 8, :] = jnp.where(place == 1, loss - loss_high, marks)
    stack_ref[0:SELF_AT, :] = (
        nn(early_turned_ref[...], masked_ref[0:hub_at, :])
        + nn(own_turned_ref[...], masked_ref[hub_at : hub_at + nodes, :])
        + nn(other_turned_ref[...], masked_ref[hub_at + nodes :, :])
    )
    for i, (there, out_ref) in enumerate(((core, mine_ref), (1 - core, theirs_ref))):
        for n in range(PEERS):
            at = there * (STACK_ROWS // CORES) + PIECE * (n % 8)
            lanes = slice(TILE * (n // 8), TILE * (n // 8 + 1))
            piece = stack_ref[pl.ds(pl.multiple_of(at, 8), PIECE), lanes]
            rows = jnp.concatenate([rest_ref[i, n], piece], axis=0)
            out_ref[n, HUB_ROWS:SUM_ROWS, :] = rows.astype(BF16)


def sum_cores(mine_ref, arrived_ref, edge_ref, out_ref):
    out_ref[:, 0:EDGE_ROWS, :] = edge_ref[...]
    total = mine_ref[...].astype(F32) + arrived_ref[...].astype(F32)
    out_ref[:, EDGE_ROWS:BACK_ROWS, :] = total.astype(BF16)


def sum_peers(arrived_ref, out_ref):
    total = arrived_ref[0, EDGE_ROWS:BACK_ROWS, :].astype(F32)
    for n in range(1, PEERS):
        total += arrived_ref[n, EDGE_ROWS:BACK_ROWS, :].astype(F32)
    out_ref[...] = total


def return_edges(base_ref, arrived_ref, wanted_ref, weights_ref, out_ref, found_ref, pick_ref):
    pick_matrix(wanted_ref[...], pick_ref)
    found_ref[...] = jnp.zeros_like(found_ref)
    for n in range(PEERS):
        at = n * FORWARD_ROWS
        first, second = part_rests(arrived_ref[n, CAPACITY:EDGE_ROWS, :].astype(F32))
        rest = jnp.concatenate([first, second], axis=0).astype(BF16)
        found_ref[at : at + CAPACITY, 0:TILE] = arrived_ref[n, 0:CAPACITY, :]
        found_ref[at : at + CAPACITY, TILE:] = rest
    rows = tn(pick_ref[...], found_ref[...])
    out_ref[...] = base_ref[...] + nn(rows.astype(BF16), weights_ref[2 * SELF_AT :, :])


def sum_chips(*refs):
    sum_refs, out_ref, hub_ref = refs[:CHIPS], refs[-2], refs[-1]
    piece = sum_refs[0][HUB_PACKED:SUM_ROWS, :]
    for sum_ref in sum_refs[1:]:
        piece += sum_ref[HUB_PACKED:SUM_ROWS, :]
    hubs = jnp.zeros((8, 2 * TILE), F32)
    for shift, sum_ref in enumerate(sum_refs):
        i = (CHIPS - shift) % CHIPS
        main = sum_ref[8 * (i // 2) : 8 * (i // 2) + 8, :]
        rest = part_rests(sum_ref[HUB_ROWS:HUB_PACKED, :])[i // 2]
        rows = jnp.concatenate([main, rest], axis=1)
        hubs += pltpu.roll(rows, HUBS_EACH, 0) if i % 2 else rows
    hub_ref[...] = hubs
    unused, core = position()
    holder = (core == LOSS_AT * CORES // STACK_ROWS) & (lax.axis_index("dev") == LOSS_AT % (STACK_ROWS // CORES) // PIECE)
    rest = piece[0:1] - piece[0:1].astype(BF16).astype(F32)
    row = iota(piece.shape, 0)
    piece = jnp.where((row == 2) & holder, rest, piece).astype(BF16)
    for n in range(PEERS):
        out_ref[n] = piece


def return_hubs(base_ref, hub_ref, wanted_ref, weights_ref, out_ref):
    nodes = out_ref.shape[0]
    high, low = split(nn(hub_ref[...].astype(BF16), weights_ref[2 * SELF_AT :, :]))
    owner = one_hot(wanted_ref[CAPACITY:FORWARD_ROWS, 0:1] == iota((8, nodes), 1))
    out_ref[...] = base_ref[...] + tn(owner, high) + tn(owner, low)


def weight_outputs(samples_all, mine_ref, theirs_ref, first_self_ref, first_mean_ref, self_ref, mean_ref, loss_ref, stack_ref):
    unused, core = position()
    half = STACK_ROWS // CORES
    for n in range(PEERS):
        mine = mine_ref[n].astype(F32)
        theirs = theirs_ref[n].astype(F32)
        lanes = slice(TILE * (n // 8), TILE * (n // 8 + 1))
        at = PIECE * (n % 8)
        stack_ref[at : at + PIECE, lanes] = jnp.where(core == 0, mine, theirs)
        stack_ref[half + at : half + at + PIECE, lanes] = jnp.where(core == 0, theirs, mine)
    classes = self_ref.shape[0]
    first_self_ref[...] = stack_ref[0:TILE, :]
    first_mean_ref[...] = stack_ref[TILE : 2 * TILE, :]
    self_ref[...] = stack_ref[SELF_AT : SELF_AT + classes, :]
    mean_ref[...] = stack_ref[MEAN_AT : MEAN_AT + classes, :]
    parts = stack_ref[LOSS_AT : LOSS_AT + 8, 0:1]
    loss_ref[...] = (parts[0:1] + parts[1:2] + parts[2:3]) / samples_all


def shape(dims, dtype):
    return jax.ShapeDtypeStruct(dims, dtype)


def swap(values):
    return lax.all_to_all(values, "dev", split_axis=0, concat_axis=0, tiled=True)


def to_core(values):
    return lax.ppermute(values, "grp", [(i, i ^ 1) for i in range(CHIPS * CORES)])


def to_chips(values):
    every = CHIPS * CORES
    return [
        lax.ppermute(values, "grp", [(i, (i + CORES * shift) % every) for i in range(every)])
        for shift in range(1, CHIPS)
    ]


def on_device(
    features,
    hub_list,
    send_list,
    send_count,
    tile_dst,
    tile_src,
    tile_count,
    tile_adj,
    sample_ids,
    labels,
    first_self,
    first_mean,
    second_self,
    second_mean,
):
    nodes, inputs = features.shape
    width, classes = second_self.shape
    hubs = CHIPS * CORES * PEERS * HUBS_EACH
    edges = PEERS * CAPACITY
    table = nodes + hubs + edges
    padded = 2 * TILE
    samples_all = float(sample_ids.shape[1] * CHIPS * CORES * PEERS)

    slots = PEERS * FORWARD_ROWS

    def gather_hubs(arrived, beside):
        own = kernel_call(group_hubs, shape((GROUP_HUBS, inputs), BF16))(arrived)
        blocks = kernel_call(
            join_blocks,
            shape((CHIPS * GROUP_HUBS, inputs), BF16),
            in_specs=[VM] * CHIPS + [ANY] * len(beside),
        )(own, *to_chips(own), *beside)
        return blocks, to_core(blocks)

    rows = kernel_call(
        send_features,
        shape((slots, inputs), BF16),
        [
            pltpu.VMEM((slots, nodes), BF16),
            pltpu.VMEM((nodes, inputs), BF16),
            pltpu.VMEM(send_list.shape[1:], I32),
            pltpu.VMEM(send_count.shape, I32),
            pltpu.SMEM(hub_list.shape, I32),
            pltpu.SemaphoreType.DMA((4,)),
        ],
        [HBM] * 4,
    )(*(pltpu.with_memory_space_constraint(operand, pltpu.HBM) for operand in (features, send_list, send_count, hub_list)))
    feature_arrived = swap(rows.reshape(PEERS, FORWARD_ROWS, inputs))
    raw = (second_self.T, second_mean.T)
    operands = (
        tile_adj, tile_dst, tile_src, tile_count, send_list[0], send_count, hub_list,
        sample_ids, labels.reshape(1, nodes), first_self, first_mean, *raw,
    )
    dense, numbers, weights, wanted, picks = kernel_call(
        build_dense,
        (
            shape((nodes, table), BF16),
            shape((nodes, TILE), F32),
            shape((3 * padded, width), BF16),
            shape((FORWARD_ROWS, PEERS), I32),
            shape((slots, nodes), BF16),
        ),
        [
            pltpu.VMEM(tile_adj.shape, BF16),
            pltpu.SMEM(tile_dst.shape, I32),
            pltpu.SMEM(tile_src.shape, I32),
            pltpu.SMEM(tile_count.shape, I32),
            pltpu.VMEM(send_list.shape[1:], I32),
            pltpu.VMEM(send_count.shape, I32),
            pltpu.SMEM(hub_list.shape, I32),
            pltpu.VMEM(sample_ids.shape, I32),
            pltpu.VMEM((1, nodes), I32),
            pltpu.VMEM(raw[0].shape, BF16),
            pltpu.VMEM(raw[1].shape, BF16),
            pltpu.SemaphoreType.DMA((len(operands),)),
        ],
        [HBM] * len(operands) + [ANY],
        flops=2 * nodes * table * TILE,
        moved=8 * MIB,
    )(
        *(
            operand if operand is tile_count else pltpu.with_memory_space_constraint(operand, pltpu.HBM)
            for operand in operands
        ),
        feature_arrived,
    )
    feature_hubs = gather_hubs(feature_arrived, [numbers])
    part = kernel_call(
        early_means,
        shape((nodes, inputs), F32),
        [pltpu.VMEM((table, inputs), BF16)],
        flops=2 * nodes * table * inputs,
        moved=4 * MIB,
    )(features, feature_arrived, dense, feature_hubs[0])
    mean_rows, rows = kernel_call(
        first_means, (shape((nodes, inputs), BF16), shape((slots, inputs), BF16))
    )(part, dense, numbers, picks, feature_hubs[1])
    mean_arrived = swap(rows.reshape(PEERS, FORWARD_ROWS, inputs))

    hidden, early_turned, early_source, part, own_logits = kernel_call(
        early_part,
        (
            shape((nodes, width), BF16),
            shape((2 * inputs, nodes + edges), BF16),
            shape((nodes + edges, width), BF16),
            shape((nodes, width), F32),
            shape((nodes, padded), F32),
        ),
        [pltpu.VMEM((nodes + edges, 2 * inputs), BF16)],
        limit=8,
        flops=6 * nodes * edges * width,
        moved=8 * MIB,
    )(features, feature_arrived, mean_rows, mean_arrived, dense, weights)
    turned = kernel_call(
        build_turned,
        shape((table, nodes), BF16),
        [
            pltpu.VMEM(tile_adj.shape, BF16),
            pltpu.SMEM(tile_dst.shape, I32),
            pltpu.SMEM(tile_src.shape, I32),
            pltpu.SemaphoreType.DMA((3,)),
        ],
        [HBM, HBM, HBM, SM, ANY],
        moved=4 * MIB,
    )(
        *(pltpu.with_memory_space_constraint(operand, pltpu.HBM) for operand in (tile_adj, tile_dst, tile_src)),
        tile_count,
        mean_arrived,
    )
    mean_hubs = gather_hubs(mean_arrived, [own_logits, turned])
    half = CHIPS * GROUP_HUBS
    own_turned, own_source, part = kernel_call(
        own_hub_part,
        (
            shape((2 * inputs, half), BF16),
            shape((half, width), BF16),
            shape((nodes, width), F32),
        ),
        [pltpu.VMEM((nodes, half), BF16)],
        limit=6,
        flops=4 * nodes * half * width,
        moved=4 * MIB,
    )(dense, weights, part, feature_hubs[0], mean_hubs[0])
    base, edge_rows, mine, theirs = kernel_call(
        functools.partial(main_part, samples_all, classes),
        (
            shape((nodes, width), F32),
            shape((PEERS, EDGE_ROWS, TILE), BF16),
            shape((PEERS, SUM_ROWS, TILE), BF16),
            shape((PEERS, SUM_ROWS, TILE), BF16),
        ),
        [
            pltpu.VMEM((2 * inputs, half), BF16),
            pltpu.VMEM((half, width), BF16),
            pltpu.VMEM((nodes, half), BF16),
            pltpu.VMEM((half, nodes), BF16),
            pltpu.VMEM((nodes, padded), BF16),
            pltpu.VMEM((table, width), BF16),
            pltpu.VMEM((STACK_ROWS, width), F32),
            pltpu.VMEM((CORES, PEERS, HUB_PACKED - HUB_ROWS, TILE), F32),
        ],
        limit=20,
    )(
        early_turned, early_source, own_logits, own_turned, own_source, part,
        dense, turned, numbers, weights, feature_hubs[1], mean_hubs[1],
    )
    rows = kernel_call(sum_cores, shape((PEERS, BACK_ROWS, TILE), BF16))(mine, to_core(theirs), edge_rows)
    arrived = swap(rows)
    sums = kernel_call(sum_peers, shape((SUM_ROWS, TILE), F32))(arrived)
    base = kernel_call(
        return_edges,
        shape((nodes, width), F32),
        [pltpu.VMEM((slots, padded), BF16), pltpu.VMEM((slots, nodes), BF16)],
        limit=6,
        flops=2 * nodes * (edges * padded + width * padded),
        moved=4 * MIB,
    )(base, arrived, wanted, weights)
    pieces, own_hubs = kernel_call(
        sum_chips,
        (shape((PEERS, PIECE, TILE), BF16), shape((8, padded), F32)),
        in_specs=[VM] * CHIPS + [ANY],
    )(sums, *to_chips(sums), base)
    pieces = swap(pieces)
    grad_hidden = kernel_call(
        return_hubs,
        shape((nodes, width), F32),
        flops=4 * nodes * padded * width,
        moved=4 * MIB,
    )(base, own_hubs, wanted, weights)
    first_self_sum, first_mean_sum, self_sum, mean_sum, loss = kernel_call(
        functools.partial(weight_outputs, samples_all),
        (
            shape(first_self.shape, F32),
            shape(first_mean.shape, F32),
            shape((classes, width), F32),
            shape((classes, width), F32),
            shape((1, 1), F32),
        ),
        [pltpu.VMEM((STACK_ROWS, width), F32)],
    )(pieces, to_core(pieces))
    return hidden, grad_hidden, loss[0, 0], first_self_sum, first_mean_sum, self_sum.T, mean_sum.T


def solution(mesh):
    both = ("grp", "dev")
    placed = (
        P(both, None),
        P(both, None),
        P(both, None, None),
        P(both, None),
        P(both, None),
        P(both, None),
        P(both),
        P(both, None, None),
        P(both, None),
        P(both),
        P(),
        P(),
        P(),
        P(),
    )
    return jax.shard_map(
        on_device,
        mesh=mesh,
        in_specs=placed,
        out_specs=(P(both, None), P(both, None), P(), P(), P(), P(), P()),
        check_vma=False,
    )
```

```python
import functools

import jax
import jax.numpy as jnp
from jax import lax
from jax.experimental import pallas as pl
from jax.experimental.pallas import tpu as pltpu
from jax.sharding import PartitionSpec as P

F32 = jnp.float32
BF16 = jnp.bfloat16
I32 = jnp.int32
MIB = 1 << 20
TILE = 128
HALF = 64
PEERS = 32
CHIPS = 4
CORES = 2
HUBS_EACH = 4
CAPACITY = 32
GROUP_HUBS = PEERS * HUBS_EACH
FORWARD_ROWS = CAPACITY + 8
PEER_HUBS = CORES * CHIPS * HUBS_EACH
EDGE_ROWS = CAPACITY + CAPACITY // 2
HUB_ROWS = CHIPS * HUBS_EACH
HUB_PACKED = HUB_ROWS + HUB_ROWS // 2
STACK_ROWS = 640
SELF_AT = 256
LOSS_AT = 440
MEAN_AT = 448
CLASS_ROWS = 176
PIECE = STACK_ROWS // CORES * 4 // PEERS
SUM_ROWS = HUB_PACKED + PIECE
BACK_ROWS = EDGE_ROWS + SUM_ROWS

VM = pl.BlockSpec(memory_space=pltpu.VMEM)
SM = pl.BlockSpec(memory_space=pltpu.SMEM)
ANY = pl.BlockSpec(memory_space=pl.ANY)
HBM = pl.BlockSpec(memory_space=pltpu.HBM)


def nn(left, right):
    return jnp.dot(left, right, preferred_element_type=F32)


def nt(left, right):
    return lax.dot_general(left, right, (((1,), (1,)), ((), ())), preferred_element_type=F32)


def tn(left, right):
    return lax.dot_general(left, right, (((0,), (0,)), ((), ())), preferred_element_type=F32)


def split(values):
    high = values.astype(BF16)
    low = (values - high.astype(F32)).astype(BF16)
    return high, low


def one_hot(hit):
    return jnp.where(hit, 1.0, 0.0).astype(BF16)


def iota(dims, axis):
    return lax.broadcasted_iota(I32, dims, axis)


def kernel_call(body, outs, scratch=(), in_specs=None, limit=5, flops=0, moved=0):
    placed = {} if in_specs is None else {"in_specs": in_specs}
    return pl.pallas_call(
        body,
        out_shape=outs,
        **placed,
        scratch_shapes=list(scratch),
        compiler_params=pltpu.CompilerParams(vmem_limit_bytes=limit * MIB),
        cost_estimate=pl.CostEstimate(flops=flops, bytes_accessed=moved, transcendentals=0),
    )


def position():
    group = lax.axis_index("grp")
    return group // CORES, group % CORES


def fetch(pairs, sems):
    loads = [pltpu.make_async_copy(source, target, sems.at[i]) for i, (source, target) in enumerate(pairs)]
    for load in loads:
        load.start()
    return loads


def wanted_rows(send, counts, hub_ref):
    send = jnp.transpose(send)
    send = jnp.where(iota(send.shape, 0) < counts, send, -1)
    row = iota((FORWARD_ROWS - CAPACITY, PEERS), 0)
    hubs = jnp.full(row.shape, -1, I32)
    for k in range(HUBS_EACH):
        hubs = jnp.where(row == k, hub_ref[0, k], hubs)
    return jnp.concatenate([send, hubs], axis=0)


def pick_matrix(wanted, pick_ref):
    lane = iota((2 * FORWARD_ROWS, pick_ref.shape[1]), 1)
    for n in range(0, PEERS, 2):
        pair = jnp.concatenate([wanted[:, n : n + 1], wanted[:, n + 1 : n + 2]], axis=0)
        pick_ref[n * FORWARD_ROWS : (n + 2) * FORWARD_ROWS, :] = one_hot(pair == lane)


def send_features(
    features_any, send_any, count_any, hub_any, out_ref, pick_ref, features_ref, send_ref, count_ref, hub_ref, sems
):
    loads = fetch(
        (
            (send_any.at[0], send_ref),
            (count_any, count_ref),
            (hub_any, hub_ref),
            (features_any, features_ref),
        ),
        sems,
    )
    for load in loads[:-1]:
        load.wait()
    pick_matrix(wanted_rows(send_ref[...], count_ref[...], hub_ref), pick_ref)
    loads[-1].wait()
    out_ref[...] = nn(pick_ref[...], features_ref[...]).astype(BF16)


def build_dense(*refs):
    count = 13
    sources, refs = refs[:count], refs[count + 1 :]
    dense_ref, numbers_ref, weights_ref, wanted_ref, pick_ref, *places, sems = refs
    (
        adj_ref, dst_ref, src_ref, live_ref, send_ref, count_ref, hub_ref,
        sample_ref, label_ref, raw_self_ref, raw_mean_ref,
    ) = places
    targets = (
        adj_ref, dst_ref, src_ref, live_ref, send_ref, count_ref, hub_ref, sample_ref, label_ref,
        weights_ref.at[pl.ds(0, TILE)], weights_ref.at[pl.ds(TILE, TILE)], raw_self_ref, raw_mean_ref,
    )
    loads = fetch(zip(sources, targets), sems)
    dense_ref[...] = jnp.zeros_like(dense_ref)
    weights_ref[SELF_AT:, :] = jnp.zeros((weights_ref.shape[0] - SELF_AT, weights_ref.shape[1]), BF16)
    for load in loads:
        load.wait()

    def add(t, carry):
        rows = pl.ds(pl.multiple_of(dst_ref[0, t] * TILE, TILE), TILE)
        columns = pl.ds(pl.multiple_of(src_ref[0, t] * TILE, TILE), TILE)
        dense_ref[rows, columns] += adj_ref[t]
        return carry

    lax.fori_loop(0, live_ref[0], add, 0)
    classes = raw_self_ref.shape[0]
    weights_ref[SELF_AT : SELF_AT + classes, :] = raw_self_ref[...]
    weights_ref[2 * SELF_AT : 2 * SELF_AT + classes, :] = raw_mean_ref[...]
    wanted = wanted_rows(send_ref[...], count_ref[...], hub_ref)
    wanted_ref[...] = wanted
    pick_matrix(wanted, pick_ref)
    nodes = dense_ref.shape[0]
    node = iota((nodes, sample_ref.shape[1]), 0)
    times = jnp.sum(jnp.where(node == sample_ref[...], 1.0, 0.0), axis=1, keepdims=True)
    label = jnp.transpose(jnp.broadcast_to(label_ref[...], (8, nodes)))[:, 0:1]
    degree = jnp.maximum(nn(dense_ref[...], jnp.ones((dense_ref.shape[1], TILE), BF16)), 1.0)
    lane = iota(degree.shape, 1)
    numbers_ref[...] = jnp.where(lane == 0, degree, jnp.where(lane == 1, times, label.astype(F32)))


def group_hubs(arrived_ref, out_ref):
    low = iota((8, TILE), 0) < HUBS_EACH
    rows = []
    for n in range(0, PEERS, 2):
        first = arrived_ref[n, CAPACITY:FORWARD_ROWS, :].astype(F32)
        second = arrived_ref[n + 1, CAPACITY:FORWARD_ROWS, :].astype(F32)
        rows.append(jnp.where(low, first, pltpu.roll(second, HUBS_EACH, 0)))
    out_ref[...] = jnp.concatenate(rows, axis=0).astype(BF16)


def join_blocks(*refs):
    out_ref = refs[-1]
    for i in range(CHIPS):
        out_ref[i * GROUP_HUBS : (i + 1) * GROUP_HUBS, :] = refs[i][...]


def place_hubs(table_ref, start, hub_refs, lanes):
    chip, core = position()
    for there, hub_ref in zip((core, 1 - core), hub_refs):
        for i in range(CHIPS):
            other = (chip + CHIPS - i) % CHIPS
            at = start + (other * CORES + there) * GROUP_HUBS
            block = hub_ref[i * GROUP_HUBS : (i + 1) * GROUP_HUBS, :]
            table_ref[pl.ds(pl.multiple_of(at, GROUP_HUBS), GROUP_HUBS), lanes] = block


def early_means(features_ref, arrived_ref, dense_ref, own_hub_ref, part_ref, table_ref):
    nodes = features_ref.shape[0]
    edge_at = nodes + CORES * CHIPS * GROUP_HUBS
    table_ref[0:nodes, :] = features_ref[...]
    table_ref[nodes:edge_at, :] = jnp.zeros((edge_at - nodes, TILE), BF16)
    place_hubs(table_ref, nodes, (own_hub_ref,), slice(0, TILE))
    for n in range(PEERS):
        at = edge_at + n * CAPACITY
        table_ref[at : at + CAPACITY, :] = arrived_ref[n, 0:CAPACITY, :]
    part_ref[...] = nn(dense_ref[...], table_ref[...])


def first_means(part_ref, dense_ref, numbers_ref, pick_ref, other_hub_ref, mean_ref, out_ref):
    nodes = part_ref.shape[0]
    chip, core = position()
    total = part_ref[...]
    for i in range(CHIPS):
        other = (chip + CHIPS - i) % CHIPS
        at = nodes + (other * CORES + 1 - core) * GROUP_HUBS
        columns = dense_ref[:, pl.ds(pl.multiple_of(at, GROUP_HUBS), GROUP_HUBS)]
        total += nn(columns, other_hub_ref[i * GROUP_HUBS : (i + 1) * GROUP_HUBS, :])
    mean = (total / numbers_ref[:, 0:1]).astype(BF16)
    mean_ref[...] = mean
    out_ref[...] = nn(pick_ref[...], mean).astype(BF16)


def join_rests(first, second):
    return first + pltpu.roll(second, HALF, 1)


def part_rests(packed):
    low = iota(packed.shape, 1) < HALF
    return jnp.where(low, packed, 0.0), jnp.where(low, pltpu.roll(packed, HALF, 1), 0.0)


def early_part(
    features_ref, feature_arrived_ref, mean_ref, arrived_ref, dense_ref, weights_ref,
    hidden_ref, turned_ref, source_ref, part_ref, logits_ref, table_ref,
):
    nodes, width = hidden_ref.shape
    edges = PEERS * CAPACITY
    edge_at = dense_ref.shape[1] - edges
    table_ref[0:nodes, 0:TILE] = features_ref[...]
    table_ref[0:nodes, TILE:] = mean_ref[...]
    for n in range(PEERS):
        at = nodes + n * CAPACITY
        table_ref[at : at + CAPACITY, 0:TILE] = feature_arrived_ref[n, 0:CAPACITY, :]
        table_ref[at : at + CAPACITY, TILE:] = arrived_ref[n, 0:CAPACITY, :]
    for at in range(0, nodes + edges, nodes):
        rows = slice(at, at + nodes)
        linear = nn(table_ref[rows, :], weights_ref[0:SELF_AT, :])
        source_ref[rows, :] = jnp.maximum(linear, 0.0).astype(BF16)
        turned_ref[:, rows] = jnp.transpose(table_ref[rows, :])
    hidden = source_ref[0:nodes, :]
    hidden_ref[...] = hidden
    part_ref[...] = nn(dense_ref[:, 0:nodes], hidden) + nn(dense_ref[:, edge_at:], source_ref[nodes:, :])
    logits_ref[...] = nt(hidden, weights_ref[SELF_AT : 2 * SELF_AT, :])


def hub_part(
    dense_ref, weights_ref, features, means, others, turned_ref, source_ref, columns_ref
):
    nodes = dense_ref.shape[0]
    chip, core = position()
    there = 1 - core if others else core
    table = jnp.concatenate([features, means], axis=1)
    turned_ref[...] = jnp.transpose(table)
    source_ref[...] = jnp.maximum(nn(table, weights_ref[0:SELF_AT, :]), 0.0).astype(BF16)
    for i in range(CHIPS):
        other = (chip + CHIPS - i) % CHIPS
        at = pl.multiple_of(nodes + (other * CORES + there) * GROUP_HUBS, GROUP_HUBS)
        columns_ref[:, i * GROUP_HUBS : (i + 1) * GROUP_HUBS] = dense_ref[:, pl.ds(at, GROUP_HUBS)]
    return nn(columns_ref[...], source_ref[...])


def own_hub_part(
    dense_ref, weights_ref, part_ref, feature_ref, mean_ref, turned_ref, source_ref, columns_ref, out_ref
):
    total = hub_part(
        dense_ref, weights_ref, feature_ref[...], mean_ref[...], False, turned_ref, source_ref, columns_ref
    )
    out_ref[...] = part_ref[...] + total


def main_part(
    samples_all, classes,
    early_turned_ref, early_source_ref, logits_ref, own_turned_ref, own_source_ref, own_columns_ref, part_ref,
    dense_ref, numbers_ref, weights_ref, feature_ref, mean_ref,
    base_ref, edge_ref, mine_ref, theirs_ref,
    other_turned_ref, other_source_ref, other_columns_ref, scaled_ref, masked_ref, stack_ref, rest_ref,
):
    nodes, width = base_ref.shape
    padded = SELF_AT
    self_rows = slice(SELF_AT, 2 * SELF_AT)
    mean_rows = slice(2 * SELF_AT, 3 * SELF_AT)
    edge_at = dense_ref.shape[1] - PEERS * CAPACITY
    total = hub_part(
        dense_ref, weights_ref, feature_ref[...], mean_ref[...], True,
        other_turned_ref, other_source_ref, other_columns_ref,
    )
    hidden = early_source_ref[0:nodes, :]
    degree = numbers_ref[:, 0:1]
    times = numbers_ref[:, 1:2]
    label = numbers_ref[:, 2:3].astype(I32)
    mean = ((part_ref[...] + total) / degree).astype(BF16)
    logits = logits_ref[...] + nt(mean, weights_ref[mean_rows, :])

    lane = iota((nodes, padded), 1)
    real = lane < classes
    onehot = jnp.where(lane == label, 1.0, 0.0)
    top = jnp.max(jnp.where(real, logits, -jnp.inf), axis=1, keepdims=True)
    shifted = logits - top
    powers = jnp.where(real, jnp.exp(shifted), 0.0)
    total = jnp.sum(powers, axis=1, keepdims=True)
    chosen = jnp.sum(onehot * shifted, axis=1, keepdims=True)
    loss = jnp.sum(times * (jnp.log(total) - chosen), axis=0, keepdims=True)
    upstream = times * ((powers / total - onehot) / samples_all)
    upstream = upstream.astype(BF16)
    scaled_ref[...] = jnp.transpose((upstream.astype(F32) / degree).astype(BF16))

    def back(columns):
        found = nn(scaled_ref[...], columns)
        found = jnp.transpose(found.astype(BF16))
        return found, nn(found, weights_ref[mean_rows, :])

    def mask(at, source, grad):
        masked_ref[at : at + nodes, :] = jnp.where(source > 0, grad, 0.0).astype(BF16)

    low = iota((8, padded), 0) < HUBS_EACH
    hub_at = nodes + PEERS * CAPACITY
    for i, (columns_ref, source_ref, out_ref) in enumerate(
        ((own_columns_ref, own_source_ref, mine_ref), (other_columns_ref, other_source_ref, theirs_ref))
    ):
        found, spread = back(columns_ref[...])
        mask(hub_at + i * nodes, source_ref[...], spread)
        found = found.astype(F32)
        for n in range(0, PEERS, 2):
            first, second = [], []
            for pair in range(CHIPS // 2):
                at = 2 * pair * GROUP_HUBS + n * HUBS_EACH
                even = found[at : at + 8]
                odd = found[at + GROUP_HUBS : at + GROUP_HUBS + 8]
                first.append(jnp.where(low, even, pltpu.roll(odd, HUBS_EACH, 0)))
                second.append(jnp.where(low, pltpu.roll(even, HUBS_EACH, 0), odd))
            for member, blocks in ((n, first), (n + 1, second)):
                rows = jnp.concatenate([block[:, 0:TILE] for block in blocks], axis=0)
                out_ref[member, 0:HUB_ROWS, :] = rows.astype(BF16)
                rest_ref[i, member] = join_rests(blocks[0][:, TILE:], blocks[1][:, TILE:])

    unused, spread = back(dense_ref[:, 0:nodes])
    base = nn(upstream, weights_ref[self_rows, :]) + spread
    base_ref[...] = base
    mask(0, hidden, base)
    each = nodes // CAPACITY
    for i in range(PEERS // each):
        found, spread = back(dense_ref[:, edge_at + i * nodes : edge_at + (i + 1) * nodes])
        at = (i + 1) * nodes
        mask(at, early_source_ref[at : at + nodes, :], spread)
        for p in range(each):
            at = p * CAPACITY
            rest = found[at : at + CAPACITY, TILE:].astype(F32)
            edge_ref[i * each + p, 0:CAPACITY, :] = found[at : at + CAPACITY, 0:TILE]
            edge_ref[i * each + p, CAPACITY:EDGE_ROWS, :] = join_rests(
                rest[0 : CAPACITY // 2], rest[CAPACITY // 2 :]
            ).astype(BF16)

    stack_ref[SELF_AT:, :] = jnp.zeros((STACK_ROWS - SELF_AT, width), F32)
    upstream_turned = jnp.transpose(upstream)
    stack_ref[SELF_AT : SELF_AT + CLASS_ROWS, :] = nn(upstream_turned, hidden)[0:CLASS_ROWS]
    stack_ref[MEAN_AT : MEAN_AT + CLASS_ROWS, :] = nn(upstream_turned, mean)[0:CLASS_ROWS]
    loss_high = loss.astype(BF16).astype(F32)
    place = iota((8, width), 0)
    marks = jnp.where(place == 0, loss_high, 0.0)
    stack_ref[LOSS_AT : LOSS_AT + 8, :] = jnp.where(place == 1, loss - loss_high, marks)
    stack_ref[0:SELF_AT, :] = (
        nn(early_turned_ref[...], masked_ref[0:hub_at, :])
        + nn(own_turned_ref[...], masked_ref[hub_at : hub_at + nodes, :])
        + nn(other_turned_ref[...], masked_ref[hub_at + nodes :, :])
    )
    unused, core = position()
    for i, (there, out_ref) in enumerate(((core, mine_ref), (1 - core, theirs_ref))):
        for n in range(PEERS):
            at = there * (STACK_ROWS // CORES) + PIECE * (n % 8)
            lanes = slice(TILE * (n // 8), TILE * (n // 8 + 1))
            piece = stack_ref[pl.ds(pl.multiple_of(at, 8), PIECE), lanes]
            rows = jnp.concatenate([rest_ref[i, n], piece], axis=0)
            out_ref[n, HUB_ROWS:SUM_ROWS, :] = rows.astype(BF16)


def sum_cores(mine_ref, arrived_ref, edge_ref, out_ref):
    out_ref[:, 0:EDGE_ROWS, :] = edge_ref[...]
    total = mine_ref[...].astype(F32) + arrived_ref[...].astype(F32)
    out_ref[:, EDGE_ROWS:BACK_ROWS, :] = total.astype(BF16)


def sum_peers(arrived_ref, out_ref):
    total = arrived_ref[0, EDGE_ROWS:BACK_ROWS, :].astype(F32)
    for n in range(1, PEERS):
        total += arrived_ref[n, EDGE_ROWS:BACK_ROWS, :].astype(F32)
    out_ref[...] = total


def return_edges(base_ref, arrived_ref, wanted_ref, weights_ref, out_ref, found_ref, pick_ref):
    pick_matrix(wanted_ref[...], pick_ref)
    found_ref[...] = jnp.zeros_like(found_ref)
    for n in range(PEERS):
        at = n * FORWARD_ROWS
        first, second = part_rests(arrived_ref[n, CAPACITY:EDGE_ROWS, :].astype(F32))
        rest = jnp.concatenate([first, second], axis=0).astype(BF16)
        found_ref[at : at + CAPACITY, 0:TILE] = arrived_ref[n, 0:CAPACITY, :]
        found_ref[at : at + CAPACITY, TILE:] = rest
    rows = tn(pick_ref[...], found_ref[...])
    out_ref[...] = base_ref[...] + nn(rows.astype(BF16), weights_ref[2 * SELF_AT :, :])


def sum_chips(*refs):
    sum_refs, out_ref, hub_ref = refs[:CHIPS], refs[-2], refs[-1]
    parts = [sum_ref[HUB_PACKED:SUM_ROWS, :] for sum_ref in sum_refs]
    piece = (parts[0] + parts[2]) + (parts[1] + parts[3])
    hubs = jnp.zeros((8, 2 * TILE), F32)
    for shift, sum_ref in enumerate(sum_refs):
        i = (CHIPS - shift) % CHIPS
        main = sum_ref[8 * (i // 2) : 8 * (i // 2) + 8, :]
        rest = part_rests(sum_ref[HUB_ROWS:HUB_PACKED, :])[i // 2]
        rows = jnp.concatenate([main, rest], axis=1)
        hubs += pltpu.roll(rows, HUBS_EACH, 0) if i % 2 else rows
    hub_ref[...] = hubs
    unused, core = position()
    holder = (core == LOSS_AT * CORES // STACK_ROWS) & (lax.axis_index("dev") == LOSS_AT % (STACK_ROWS // CORES) // PIECE)
    rest = piece[0:1] - piece[0:1].astype(BF16).astype(F32)
    row = iota(piece.shape, 0)
    piece = jnp.where((row == 2) & holder, rest, piece).astype(BF16)
    for n in range(PEERS):
        out_ref[n] = piece


def return_hubs(base_ref, hub_ref, wanted_ref, weights_ref, out_ref):
    nodes = out_ref.shape[0]
    high, low = split(nn(hub_ref[...].astype(BF16), weights_ref[2 * SELF_AT :, :]))
    owner = one_hot(wanted_ref[CAPACITY:FORWARD_ROWS, 0:1] == iota((8, nodes), 1))
    out_ref[...] = base_ref[...] + tn(owner, high) + tn(owner, low)


def weight_outputs(samples_all, mine_ref, theirs_ref, first_self_ref, first_mean_ref, self_ref, mean_ref, loss_ref):
    unused, core = position()
    half = STACK_ROWS // CORES
    classes = self_ref.shape[0]
    spans = (
        (0, TILE, first_self_ref),
        (TILE, 2 * TILE, first_mean_ref),
        (SELF_AT, SELF_AT + classes, self_ref),
        (MEAN_AT, MEAN_AT + classes, mean_ref),
    )
    for n in range(PEERS):
        mine = mine_ref[n].astype(F32)
        theirs = theirs_ref[n].astype(F32)
        lanes = slice(TILE * (n // 8), TILE * (n // 8 + 1))
        for at, piece in (
            (PIECE * (n % 8), jnp.where(core == 0, mine, theirs)),
            (half + PIECE * (n % 8), jnp.where(core == 0, theirs, mine)),
        ):
            for start, end, out_ref in spans:
                low, high = max(start, at), min(end, at + PIECE)
                if low < high:
                    out_ref[low - start : high - start, lanes] = piece[low - at : high - at]
            if at == LOSS_AT and lanes.start == 0:
                loss_ref[...] = (piece[0:1, 0:1] + piece[1:2, 0:1] + piece[2:3, 0:1]) / samples_all


def shape(dims, dtype):
    return jax.ShapeDtypeStruct(dims, dtype)


def swap(values):
    return lax.all_to_all(values, "dev", split_axis=0, concat_axis=0, tiled=True)


def to_core(values):
    return lax.ppermute(values, "grp", [(i, i ^ 1) for i in range(CHIPS * CORES)])


def to_chips(values):
    every = CHIPS * CORES
    return [
        lax.ppermute(values, "grp", [(i, (i + CORES * shift) % every) for i in range(every)])
        for shift in range(1, CHIPS)
    ]


def on_device(
    features,
    hub_list,
    send_list,
    send_count,
    tile_dst,
    tile_src,
    tile_count,
    tile_adj,
    sample_ids,
    labels,
    first_self,
    first_mean,
    second_self,
    second_mean,
):
    nodes, inputs = features.shape
    width, classes = second_self.shape
    hubs = CHIPS * CORES * PEERS * HUBS_EACH
    edges = PEERS * CAPACITY
    table = nodes + hubs + edges
    padded = 2 * TILE
    samples_all = float(sample_ids.shape[1] * CHIPS * CORES * PEERS)

    slots = PEERS * FORWARD_ROWS

    def gather_hubs(arrived, beside):
        own = kernel_call(group_hubs, shape((GROUP_HUBS, inputs), BF16))(arrived)
        blocks = kernel_call(
            join_blocks,
            shape((CHIPS * GROUP_HUBS, inputs), BF16),
            in_specs=[VM] * CHIPS + [ANY] * len(beside),
        )(own, *to_chips(own), *beside)
        return blocks, to_core(blocks)

    rows = kernel_call(
        send_features,
        shape((slots, inputs), BF16),
        [
            pltpu.VMEM((slots, nodes), BF16),
            pltpu.VMEM((nodes, inputs), BF16),
            pltpu.VMEM(send_list.shape[1:], I32),
            pltpu.VMEM(send_count.shape, I32),
            pltpu.SMEM(hub_list.shape, I32),
            pltpu.SemaphoreType.DMA((4,)),
        ],
        [HBM] * 4,
    )(*(pltpu.with_memory_space_constraint(operand, pltpu.HBM) for operand in (features, send_list, send_count, hub_list)))
    feature_arrived = swap(rows.reshape(PEERS, FORWARD_ROWS, inputs))
    raw = (second_self.T, second_mean.T)
    operands = (
        tile_adj, tile_dst, tile_src, tile_count, send_list[0], send_count, hub_list,
        sample_ids, labels.reshape(1, nodes), first_self, first_mean, *raw,
    )
    dense, numbers, weights, wanted, picks = kernel_call(
        build_dense,
        (
            shape((nodes, table), BF16),
            shape((nodes, TILE), F32),
            shape((3 * padded, width), BF16),
            shape((FORWARD_ROWS, PEERS), I32),
            shape((slots, nodes), BF16),
        ),
        [
            pltpu.VMEM(tile_adj.shape, BF16),
            pltpu.SMEM(tile_dst.shape, I32),
            pltpu.SMEM(tile_src.shape, I32),
            pltpu.SMEM(tile_count.shape, I32),
            pltpu.VMEM(send_list.shape[1:], I32),
            pltpu.VMEM(send_count.shape, I32),
            pltpu.SMEM(hub_list.shape, I32),
            pltpu.VMEM(sample_ids.shape, I32),
            pltpu.VMEM((1, nodes), I32),
            pltpu.VMEM(raw[0].shape, BF16),
            pltpu.VMEM(raw[1].shape, BF16),
            pltpu.SemaphoreType.DMA((len(operands),)),
        ],
        [HBM] * len(operands) + [ANY],
        flops=2 * nodes * table * TILE,
        moved=8 * MIB,
    )(
        *(
            operand if operand is tile_count else pltpu.with_memory_space_constraint(operand, pltpu.HBM)
            for operand in operands
        ),
        feature_arrived,
    )
    feature_hubs = gather_hubs(feature_arrived, [numbers])
    part = kernel_call(
        early_means,
        shape((nodes, inputs), F32),
        [pltpu.VMEM((table, inputs), BF16)],
        flops=2 * nodes * table * inputs,
        moved=4 * MIB,
    )(features, feature_arrived, dense, feature_hubs[0])
    mean_rows, rows = kernel_call(
        first_means, (shape((nodes, inputs), BF16), shape((slots, inputs), BF16))
    )(part, dense, numbers, picks, feature_hubs[1])
    mean_arrived = swap(rows.reshape(PEERS, FORWARD_ROWS, inputs))

    hidden, early_turned, early_source, part, own_logits = kernel_call(
        early_part,
        (
            shape((nodes, width), BF16),
            shape((2 * inputs, nodes + edges), BF16),
            shape((nodes + edges, width), BF16),
            shape((nodes, width), F32),
            shape((nodes, padded), F32),
        ),
        [pltpu.VMEM((nodes + edges, 2 * inputs), BF16)],
        limit=8,
        flops=6 * nodes * edges * width,
        moved=8 * MIB,
    )(features, feature_arrived, mean_rows, mean_arrived, dense, weights)
    mean_hubs = gather_hubs(mean_arrived, [own_logits])
    half = CHIPS * GROUP_HUBS
    own_turned, own_source, own_columns, part = kernel_call(
        own_hub_part,
        (
            shape((2 * inputs, half), BF16),
            shape((half, width), BF16),
            shape((nodes, half), BF16),
            shape((nodes, width), F32),
        ),
        limit=6,
        flops=4 * nodes * half * width,
        moved=4 * MIB,
    )(dense, weights, part, feature_hubs[0], mean_hubs[0])
    base, edge_rows, mine, theirs = kernel_call(
        functools.partial(main_part, samples_all, classes),
        (
            shape((nodes, width), F32),
            shape((PEERS, EDGE_ROWS, TILE), BF16),
            shape((PEERS, SUM_ROWS, TILE), BF16),
            shape((PEERS, SUM_ROWS, TILE), BF16),
        ),
        [
            pltpu.VMEM((2 * inputs, half), BF16),
            pltpu.VMEM((half, width), BF16),
            pltpu.VMEM((nodes, half), BF16),
            pltpu.VMEM((padded, nodes), BF16),
            pltpu.VMEM((table, width), BF16),
            pltpu.VMEM((STACK_ROWS, width), F32),
            pltpu.VMEM((CORES, PEERS, HUB_PACKED - HUB_ROWS, TILE), F32),
        ],
        limit=20,
    )(
        early_turned, early_source, own_logits, own_turned, own_source, own_columns, part,
        dense, numbers, weights, feature_hubs[1], mean_hubs[1],
    )
    rows = kernel_call(sum_cores, shape((PEERS, BACK_ROWS, TILE), BF16))(mine, to_core(theirs), edge_rows)
    arrived = swap(rows)
    sums = kernel_call(sum_peers, shape((SUM_ROWS, TILE), F32))(arrived)
    base = kernel_call(
        return_edges,
        shape((nodes, width), F32),
        [pltpu.VMEM((slots, padded), BF16), pltpu.VMEM((slots, nodes), BF16)],
        limit=6,
        flops=2 * nodes * (edges * padded + width * padded),
        moved=4 * MIB,
    )(base, arrived, wanted, weights)
    pieces, own_hubs = kernel_call(
        sum_chips,
        (shape((PEERS, PIECE, TILE), BF16), shape((8, padded), F32)),
        in_specs=[VM] * CHIPS + [ANY],
    )(sums, *to_chips(sums), base)
    pieces = swap(pieces)
    grad_hidden = kernel_call(
        return_hubs,
        shape((nodes, width), F32),
        flops=4 * nodes * padded * width,
        moved=4 * MIB,
    )(base, own_hubs, wanted, weights)
    first_self_sum, first_mean_sum, self_sum, mean_sum, loss = kernel_call(
        functools.partial(weight_outputs, samples_all),
        (
            shape(first_self.shape, F32),
            shape(first_mean.shape, F32),
            shape((classes, width), F32),
            shape((classes, width), F32),
            shape((1, 1), F32),
        ),
    )(pieces, to_core(pieces))
    return hidden, grad_hidden, loss[0, 0], first_self_sum, first_mean_sum, self_sum.T, mean_sum.T


def solution(mesh):
    both = ("grp", "dev")
    placed = (
        P(both, None),
        P(both, None),
        P(both, None, None),
        P(both, None),
        P(both, None),
        P(both, None),
        P(both),
        P(both, None, None),
        P(both, None),
        P(both),
        P(),
        P(),
        P(),
        P(),
    )
    return jax.shard_map(
        on_device,
        mesh=mesh,
        in_specs=placed,
        out_specs=(P(both, None), P(both, None), P(), P(), P(), P(), P()),
        check_vma=False,
    )
```

```python
import functools

import jax
import jax.numpy as jnp
from jax import lax
from jax.experimental import pallas as pl
from jax.experimental.pallas import tpu as pltpu
from jax.sharding import PartitionSpec as P

F32 = jnp.float32
BF16 = jnp.bfloat16
I32 = jnp.int32
MIB = 1 << 20
TILE = 128
HALF = 64
PEERS = 32
CHIPS = 4
CORES = 2
HUBS_EACH = 4
CAPACITY = 32
GROUP_HUBS = PEERS * HUBS_EACH
FORWARD_ROWS = CAPACITY + 8
PEER_HUBS = CORES * CHIPS * HUBS_EACH
EDGE_ROWS = CAPACITY + CAPACITY // 2
HUB_ROWS = 2 * HUBS_EACH
CHIP_HUBS = PEERS * HUB_ROWS
STACK_ROWS = 640
SELF_AT = 256
LOSS_AT = 440
MEAN_AT = 448
CLASS_ROWS = 176
PIECE = STACK_ROWS // CORES * 4 // PEERS
BACK_ROWS = EDGE_ROWS + PIECE
CORE_ROWS = CHIPS * CHIP_HUBS + PEERS * PIECE
CHIP_ROWS = CHIP_HUBS + 2 * PIECE
LAST_ROWS = HUB_ROWS + PIECE

VM = pl.BlockSpec(memory_space=pltpu.VMEM)
SM = pl.BlockSpec(memory_space=pltpu.SMEM)
ANY = pl.BlockSpec(memory_space=pl.ANY)
HBM = pl.BlockSpec(memory_space=pltpu.HBM)


def nn(left, right):
    return jnp.dot(left, right, preferred_element_type=F32)


def nt(left, right):
    return lax.dot_general(left, right, (((1,), (1,)), ((), ())), preferred_element_type=F32)


def tn(left, right):
    return lax.dot_general(left, right, (((0,), (0,)), ((), ())), preferred_element_type=F32)


def split(values):
    high = values.astype(BF16)
    low = (values - high.astype(F32)).astype(BF16)
    return high, low


def one_hot(hit):
    return jnp.where(hit, 1.0, 0.0).astype(BF16)


def iota(dims, axis):
    return lax.broadcasted_iota(I32, dims, axis)


def kernel_call(body, outs, scratch=(), in_specs=None, limit=5, flops=0, moved=0):
    placed = {} if in_specs is None else {"in_specs": in_specs}
    return pl.pallas_call(
        body,
        out_shape=outs,
        **placed,
        scratch_shapes=list(scratch),
        compiler_params=pltpu.CompilerParams(vmem_limit_bytes=limit * MIB),
        cost_estimate=pl.CostEstimate(flops=flops, bytes_accessed=moved, transcendentals=0),
    )


def position():
    group = lax.axis_index("grp")
    return group // CORES, group % CORES


def fetch(pairs, sems):
    loads = [pltpu.make_async_copy(source, target, sems.at[i]) for i, (source, target) in enumerate(pairs)]
    for load in loads:
        load.start()
    return loads


def wanted_rows(send, counts, hub_ref):
    send = jnp.transpose(send)
    send = jnp.where(iota(send.shape, 0) < counts, send, -1)
    row = iota((FORWARD_ROWS - CAPACITY, PEERS), 0)
    hubs = jnp.full(row.shape, -1, I32)
    for k in range(HUBS_EACH):
        hubs = jnp.where(row == k, hub_ref[0, k], hubs)
    return jnp.concatenate([send, hubs], axis=0)


def pick_matrix(wanted, pick_ref):
    lane = iota((2 * FORWARD_ROWS, pick_ref.shape[1]), 1)
    for n in range(0, PEERS, 2):
        pair = jnp.concatenate([wanted[:, n : n + 1], wanted[:, n + 1 : n + 2]], axis=0)
        pick_ref[n * FORWARD_ROWS : (n + 2) * FORWARD_ROWS, :] = one_hot(pair == lane)


def send_features(
    features_any, send_any, count_any, hub_any, out_ref, pick_ref, features_ref, send_ref, count_ref, hub_ref, sems
):
    loads = fetch(
        (
            (send_any.at[0], send_ref),
            (count_any, count_ref),
            (hub_any, hub_ref),
            (features_any, features_ref),
        ),
        sems,
    )
    for load in loads[:-1]:
        load.wait()
    pick_matrix(wanted_rows(send_ref[...], count_ref[...], hub_ref), pick_ref)
    loads[-1].wait()
    out_ref[...] = nn(pick_ref[...], features_ref[...]).astype(BF16)


def build_dense(*refs):
    count = 13
    sources, refs = refs[:count], refs[count + 1 :]
    dense_ref, numbers_ref, weights_ref, wanted_ref, pick_ref, *places, sems = refs
    (
        adj_ref, dst_ref, src_ref, live_ref, send_ref, count_ref, hub_ref,
        sample_ref, label_ref, raw_self_ref, raw_mean_ref,
    ) = places
    targets = (
        adj_ref, dst_ref, src_ref, live_ref, send_ref, count_ref, hub_ref, sample_ref, label_ref,
        weights_ref.at[pl.ds(0, TILE)], weights_ref.at[pl.ds(TILE, TILE)], raw_self_ref, raw_mean_ref,
    )
    loads = fetch(zip(sources, targets), sems)
    dense_ref[...] = jnp.zeros_like(dense_ref)
    weights_ref[SELF_AT:, :] = jnp.zeros((weights_ref.shape[0] - SELF_AT, weights_ref.shape[1]), BF16)
    for load in loads:
        load.wait()

    def add(t, carry):
        rows = pl.ds(pl.multiple_of(dst_ref[0, t] * TILE, TILE), TILE)
        columns = pl.ds(pl.multiple_of(src_ref[0, t] * TILE, TILE), TILE)
        dense_ref[rows, columns] += adj_ref[t]
        return carry

    lax.fori_loop(0, live_ref[0], add, 0)
    classes = raw_self_ref.shape[0]
    weights_ref[SELF_AT : SELF_AT + classes, :] = raw_self_ref[...]
    weights_ref[2 * SELF_AT : 2 * SELF_AT + classes, :] = raw_mean_ref[...]
    wanted = wanted_rows(send_ref[...], count_ref[...], hub_ref)
    wanted_ref[...] = wanted
    pick_matrix(wanted, pick_ref)
    nodes = dense_ref.shape[0]
    node = iota((nodes, sample_ref.shape[1]), 0)
    times = jnp.sum(jnp.where(node == sample_ref[...], 1.0, 0.0), axis=1, keepdims=True)
    label = jnp.transpose(jnp.broadcast_to(label_ref[...], (8, nodes)))[:, 0:1]
    degree = jnp.maximum(nn(dense_ref[...], jnp.ones((dense_ref.shape[1], TILE), BF16)), 1.0)
    lane = iota(degree.shape, 1)
    numbers_ref[...] = jnp.where(lane == 0, degree, jnp.where(lane == 1, times, label.astype(F32)))


def group_hubs(arrived_ref, out_ref):
    low = iota((8, TILE), 0) < HUBS_EACH
    rows = []
    for n in range(0, PEERS, 2):
        first = arrived_ref[n, CAPACITY:FORWARD_ROWS, :].astype(F32)
        second = arrived_ref[n + 1, CAPACITY:FORWARD_ROWS, :].astype(F32)
        rows.append(jnp.where(low, first, pltpu.roll(second, HUBS_EACH, 0)))
    out_ref[...] = jnp.concatenate(rows, axis=0).astype(BF16)


def join_blocks(*refs):
    out_ref = refs[-1]
    for i in range(CHIPS):
        out_ref[i * GROUP_HUBS : (i + 1) * GROUP_HUBS, :] = refs[i][...]


def place_hubs(table_ref, start, hub_refs, lanes):
    chip, core = position()
    for there, hub_ref in zip((core, 1 - core), hub_refs):
        for i in range(CHIPS):
            other = (chip + CHIPS - i) % CHIPS
            at = start + (other * CORES + there) * GROUP_HUBS
            block = hub_ref[i * GROUP_HUBS : (i + 1) * GROUP_HUBS, :]
            table_ref[pl.ds(pl.multiple_of(at, GROUP_HUBS), GROUP_HUBS), lanes] = block


def early_means(features_ref, arrived_ref, dense_ref, own_hub_ref, part_ref, table_ref):
    nodes = features_ref.shape[0]
    edge_at = nodes + CORES * CHIPS * GROUP_HUBS
    table_ref[0:nodes, :] = features_ref[...]
    table_ref[nodes:edge_at, :] = jnp.zeros((edge_at - nodes, TILE), BF16)
    place_hubs(table_ref, nodes, (own_hub_ref,), slice(0, TILE))
    for n in range(PEERS):
        at = edge_at + n * CAPACITY
        table_ref[at : at + CAPACITY, :] = arrived_ref[n, 0:CAPACITY, :]
    part_ref[...] = nn(dense_ref[...], table_ref[...])


def first_means(part_ref, dense_ref, numbers_ref, pick_ref, other_hub_ref, mean_ref, out_ref):
    nodes = part_ref.shape[0]
    chip, core = position()
    total = part_ref[...]
    for i in range(CHIPS):
        other = (chip + CHIPS - i) % CHIPS
        at = nodes + (other * CORES + 1 - core) * GROUP_HUBS
        columns = dense_ref[:, pl.ds(pl.multiple_of(at, GROUP_HUBS), GROUP_HUBS)]
        total += nn(columns, other_hub_ref[i * GROUP_HUBS : (i + 1) * GROUP_HUBS, :])
    mean = (total / numbers_ref[:, 0:1]).astype(BF16)
    mean_ref[...] = mean
    out_ref[...] = nn(pick_ref[...], mean).astype(BF16)


def join_rests(first, second):
    return first + pltpu.roll(second, HALF, 1)


def part_rests(packed):
    low = iota(packed.shape, 1) < HALF
    return jnp.where(low, packed, 0.0), jnp.where(low, pltpu.roll(packed, HALF, 1), 0.0)


def early_part(
    features_ref, feature_arrived_ref, mean_ref, arrived_ref, dense_ref, weights_ref,
    hidden_ref, turned_ref, source_ref, part_ref, logits_ref, table_ref,
):
    nodes, width = hidden_ref.shape
    edges = PEERS * CAPACITY
    edge_at = dense_ref.shape[1] - edges
    table_ref[0:nodes, 0:TILE] = features_ref[...]
    table_ref[0:nodes, TILE:] = mean_ref[...]
    for n in range(PEERS):
        at = nodes + n * CAPACITY
        table_ref[at : at + CAPACITY, 0:TILE] = feature_arrived_ref[n, 0:CAPACITY, :]
        table_ref[at : at + CAPACITY, TILE:] = arrived_ref[n, 0:CAPACITY, :]
    for at in range(0, nodes + edges, nodes):
        rows = slice(at, at + nodes)
        linear = nn(table_ref[rows, :], weights_ref[0:SELF_AT, :])
        source_ref[rows, :] = jnp.maximum(linear, 0.0).astype(BF16)
        turned_ref[:, rows] = jnp.transpose(table_ref[rows, :])
    hidden = source_ref[0:nodes, :]
    hidden_ref[...] = hidden
    part_ref[...] = nn(dense_ref[:, 0:nodes], hidden) + nn(dense_ref[:, edge_at:], source_ref[nodes:, :])
    logits_ref[...] = nt(hidden, weights_ref[SELF_AT : 2 * SELF_AT, :])


def hub_part(
    dense_ref, weights_ref, features, means, others, turned_ref, source_ref, columns_ref
):
    nodes = dense_ref.shape[0]
    chip, core = position()
    there = 1 - core if others else core
    table = jnp.concatenate([features, means], axis=1)
    turned_ref[...] = jnp.transpose(table)
    source_ref[...] = jnp.maximum(nn(table, weights_ref[0:SELF_AT, :]), 0.0).astype(BF16)
    for i in range(CHIPS):
        other = (chip + CHIPS - i) % CHIPS
        at = pl.multiple_of(nodes + (other * CORES + there) * GROUP_HUBS, GROUP_HUBS)
        columns_ref[:, i * GROUP_HUBS : (i + 1) * GROUP_HUBS] = dense_ref[:, pl.ds(at, GROUP_HUBS)]
    return nn(columns_ref[...], source_ref[...])


def own_hub_part(
    dense_ref, weights_ref, part_ref, feature_ref, mean_ref, turned_ref, source_ref, columns_ref, out_ref
):
    total = hub_part(
        dense_ref, weights_ref, feature_ref[...], mean_ref[...], False, turned_ref, source_ref, columns_ref
    )
    out_ref[...] = part_ref[...] + total


def main_part(
    samples_all, classes,
    early_turned_ref, early_source_ref, logits_ref, own_turned_ref, own_source_ref, own_columns_ref, part_ref,
    dense_ref, numbers_ref, weights_ref, feature_ref, mean_ref,
    base_ref, edge_ref, mine_ref, theirs_ref,
    other_turned_ref, other_source_ref, other_columns_ref, scaled_ref, masked_ref, stack_ref,
):
    nodes, width = base_ref.shape
    padded = SELF_AT
    self_rows = slice(SELF_AT, 2 * SELF_AT)
    mean_rows = slice(2 * SELF_AT, 3 * SELF_AT)
    edge_at = dense_ref.shape[1] - PEERS * CAPACITY
    total = hub_part(
        dense_ref, weights_ref, feature_ref[...], mean_ref[...], True,
        other_turned_ref, other_source_ref, other_columns_ref,
    )
    hidden = early_source_ref[0:nodes, :]
    degree = numbers_ref[:, 0:1]
    times = numbers_ref[:, 1:2]
    label = numbers_ref[:, 2:3].astype(I32)
    mean = ((part_ref[...] + total) / degree).astype(BF16)
    logits = logits_ref[...] + nt(mean, weights_ref[mean_rows, :])

    lane = iota((nodes, padded), 1)
    real = lane < classes
    onehot = jnp.where(lane == label, 1.0, 0.0)
    top = jnp.max(jnp.where(real, logits, -jnp.inf), axis=1, keepdims=True)
    shifted = logits - top
    powers = jnp.where(real, jnp.exp(shifted), 0.0)
    total = jnp.sum(powers, axis=1, keepdims=True)
    chosen = jnp.sum(onehot * shifted, axis=1, keepdims=True)
    loss = jnp.sum(times * (jnp.log(total) - chosen), axis=0, keepdims=True)
    upstream = times * ((powers / total - onehot) / samples_all)
    upstream = upstream.astype(BF16)
    scaled_ref[...] = jnp.transpose((upstream.astype(F32) / degree).astype(BF16))

    def back(columns):
        found = nn(scaled_ref[...], columns)
        found = jnp.transpose(found.astype(BF16))
        return found, nn(found, weights_ref[mean_rows, :])

    def mask(at, source, grad):
        masked_ref[at : at + nodes, :] = jnp.where(source > 0, grad, 0.0).astype(BF16)

    low = iota((8, TILE), 0) < HUBS_EACH
    hub_at = nodes + PEERS * CAPACITY
    for i, (columns_ref, source_ref, out_ref) in enumerate(
        ((own_columns_ref, own_source_ref, mine_ref), (other_columns_ref, other_source_ref, theirs_ref))
    ):
        found, spread = back(columns_ref[...])
        mask(hub_at + i * nodes, source_ref[...], spread)
        found = found.astype(F32)
        for block in range(CHIPS):
            for n in range(0, PEERS, 2):
                at = block * GROUP_HUBS + n * HUBS_EACH
                mains = found[at : at + 8, 0:TILE]
                rests = found[at : at + 8, TILE:]
                pair = (
                    jnp.where(low, mains, pltpu.roll(rests, HUBS_EACH, 0)),
                    jnp.where(low, pltpu.roll(mains, HUBS_EACH, 0), rests),
                )
                at = block * CHIP_HUBS + n * HUB_ROWS
                out_ref[at : at + 2 * HUB_ROWS, :] = jnp.concatenate(pair, axis=0).astype(BF16)

    unused, spread = back(dense_ref[:, 0:nodes])
    base = nn(upstream, weights_ref[self_rows, :]) + spread
    base_ref[...] = base
    mask(0, hidden, base)
    each = nodes // CAPACITY
    for i in range(PEERS // each):
        found, spread = back(dense_ref[:, edge_at + i * nodes : edge_at + (i + 1) * nodes])
        at = (i + 1) * nodes
        mask(at, early_source_ref[at : at + nodes, :], spread)
        for p in range(each):
            at = p * CAPACITY
            rest = found[at : at + CAPACITY, TILE:].astype(F32)
            edge_ref[i * each + p, 0:CAPACITY, :] = found[at : at + CAPACITY, 0:TILE]
            edge_ref[i * each + p, CAPACITY:EDGE_ROWS, :] = join_rests(
                rest[0 : CAPACITY // 2], rest[CAPACITY // 2 :]
            ).astype(BF16)

    stack_ref[SELF_AT:, :] = jnp.zeros((STACK_ROWS - SELF_AT, width), F32)
    upstream_turned = jnp.transpose(upstream)
    stack_ref[SELF_AT : SELF_AT + CLASS_ROWS, :] = nn(upstream_turned, hidden)[0:CLASS_ROWS]
    stack_ref[MEAN_AT : MEAN_AT + CLASS_ROWS, :] = nn(upstream_turned, mean)[0:CLASS_ROWS]
    loss_high = loss.astype(BF16).astype(F32)
    place = iota((8, width), 0)
    marks = jnp.where(place == 0, loss_high, 0.0)
    stack_ref[LOSS_AT : LOSS_AT + 8, :] = jnp.where(place == 1, loss - loss_high, marks)
    stack_ref[0:SELF_AT, :] = (
        nn(early_turned_ref[...], masked_ref[0:hub_at, :])
        + nn(own_turned_ref[...], masked_ref[hub_at : hub_at + nodes, :])
        + nn(other_turned_ref[...], masked_ref[hub_at + nodes :, :])
    )
    unused, core = position()
    for there, out_ref in ((core, mine_ref), (1 - core, theirs_ref)):
        for n in range(0, PEERS, 2):
            at = there * (STACK_ROWS // CORES) + PIECE * (n % 8)
            lanes = slice(TILE * (n // 8), TILE * (n // 8 + 1))
            rows = stack_ref[pl.ds(pl.multiple_of(at, 16), 2 * PIECE), lanes]
            at = CHIPS * CHIP_HUBS + n * PIECE
            out_ref[at : at + 2 * PIECE, :] = rows.astype(BF16)


def sum_cores(mine_ref, arrived_ref, edge_ref, out_ref, *hub_refs):
    out_ref[:, 0:EDGE_ROWS, :] = edge_ref[...]
    total = mine_ref[...].astype(F32) + arrived_ref[...].astype(F32)
    for block, hub_ref in enumerate(hub_refs):
        hub_ref[...] = total[block * CHIP_HUBS : (block + 1) * CHIP_HUBS].astype(BF16)
    for n in range(PEERS):
        at = CHIPS * CHIP_HUBS + n * PIECE
        out_ref[n, EDGE_ROWS:BACK_ROWS, :] = total[at : at + PIECE].astype(BF16)


def sum_peers(arrived_ref, *refs):
    hub_refs, (sum_ref, *out_refs) = refs[: CHIPS - 1], refs[CHIPS - 1 :]
    total = arrived_ref[0, EDGE_ROWS:BACK_ROWS, :].astype(F32)
    for n in range(1, PEERS):
        total += arrived_ref[n, EDGE_ROWS:BACK_ROWS, :].astype(F32)
    high = total.astype(BF16).astype(F32)
    low = (total - high).astype(BF16).astype(F32)
    sum_ref[...] = high + low
    parts = jnp.concatenate([high, low], axis=0).astype(BF16)
    for hub_ref, out_ref in zip(hub_refs, out_refs):
        out_ref[0:CHIP_HUBS, :] = hub_ref[...]
        out_ref[CHIP_HUBS:CHIP_ROWS, :] = parts


def return_edges(base_ref, arrived_ref, wanted_ref, weights_ref, out_ref, found_ref, pick_ref):
    pick_matrix(wanted_ref[...], pick_ref)
    found_ref[...] = jnp.zeros_like(found_ref)
    for n in range(PEERS):
        at = n * FORWARD_ROWS
        first, second = part_rests(arrived_ref[n, CAPACITY:EDGE_ROWS, :].astype(F32))
        rest = jnp.concatenate([first, second], axis=0).astype(BF16)
        found_ref[at : at + CAPACITY, 0:TILE] = arrived_ref[n, 0:CAPACITY, :]
        found_ref[at : at + CAPACITY, TILE:] = rest
    rows = tn(pick_ref[...], found_ref[...])
    out_ref[...] = base_ref[...] + nn(rows.astype(BF16), weights_ref[2 * SELF_AT :, :])


def sum_chips(sum_ref, own_ref, *refs):
    sent_refs, out_ref = refs[: CHIPS - 1], refs[-1]
    hubs = own_ref[...].astype(F32)
    pieces = [sum_ref[...]]
    for sent_ref in sent_refs:
        rows = sent_ref[...].astype(F32)
        hubs += rows[0:CHIP_HUBS]
        pieces.append(rows[CHIP_HUBS : CHIP_HUBS + PIECE] + rows[CHIP_HUBS + PIECE : CHIP_ROWS])
    piece = (pieces[0] + pieces[2]) + (pieces[1] + pieces[3])
    unused, core = position()
    holder = (core == LOSS_AT * CORES // STACK_ROWS) & (lax.axis_index("dev") == LOSS_AT % (STACK_ROWS // CORES) // PIECE)
    rest = piece[0:1] - piece[0:1].astype(BF16).astype(F32)
    row = iota(piece.shape, 0)
    piece = jnp.where((row == 2) & holder, rest, piece)
    tail = piece[8:PIECE].astype(BF16)
    for n in range(PEERS):
        head = jnp.concatenate([hubs[n * HUB_ROWS : (n + 1) * HUB_ROWS], piece[0:8]], axis=0)
        out_ref[n, 0:16, :] = head.astype(BF16)
        out_ref[n, 16:LAST_ROWS, :] = tail


def return_hubs(base_ref, arrived_ref, wanted_ref, weights_ref, out_ref):
    nodes = out_ref.shape[0]
    hubs = arrived_ref[0, 0:16, :].astype(F32)
    for n in range(1, PEERS):
        hubs += arrived_ref[n, 0:16, :].astype(F32)
    hubs = hubs[0:HUB_ROWS]
    hubs = jnp.concatenate([hubs, pltpu.roll(hubs, HUBS_EACH, 0)], axis=1)
    high, low = split(nn(hubs.astype(BF16), weights_ref[2 * SELF_AT :, :]))
    owner = one_hot(wanted_ref[CAPACITY:FORWARD_ROWS, 0:1] == iota((HUB_ROWS, nodes), 1))
    out_ref[...] = base_ref[...] + tn(owner, high) + tn(owner, low)


def weight_outputs(samples_all, mine_ref, theirs_ref, first_self_ref, first_mean_ref, self_ref, mean_ref, loss_ref):
    unused, core = position()
    half = STACK_ROWS // CORES
    classes = self_ref.shape[0]
    spans = (
        (0, TILE, first_self_ref),
        (TILE, 2 * TILE, first_mean_ref),
        (SELF_AT, SELF_AT + classes, self_ref),
        (MEAN_AT, MEAN_AT + classes, mean_ref),
    )
    for n in range(PEERS):
        mine = mine_ref[n].astype(F32)[HUB_ROWS:]
        theirs = theirs_ref[n].astype(F32)[HUB_ROWS:]
        lanes = slice(TILE * (n // 8), TILE * (n // 8 + 1))
        for at, piece in (
            (PIECE * (n % 8), jnp.where(core == 0, mine, theirs)),
            (half + PIECE * (n % 8), jnp.where(core == 0, theirs, mine)),
        ):
            for start, end, out_ref in spans:
                low, high = max(start, at), min(end, at + PIECE)
                if low < high:
                    out_ref[low - start : high - start, lanes] = piece[low - at : high - at]
            if at == LOSS_AT and lanes.start == 0:
                loss_ref[...] = (piece[0:1, 0:1] + piece[1:2, 0:1] + piece[2:3, 0:1]) / samples_all


def shape(dims, dtype):
    return jax.ShapeDtypeStruct(dims, dtype)


def swap(values):
    return lax.all_to_all(values, "dev", split_axis=0, concat_axis=0, tiled=True)


def to_core(values):
    return lax.ppermute(values, "grp", [(i, i ^ 1) for i in range(CHIPS * CORES)])


def along_x(values, shift):
    every = CHIPS * CORES
    return lax.ppermute(values, "grp", [(i, (i + CORES * shift) % every) for i in range(every)])


def to_chips(values):
    return [along_x(values, shift) for shift in range(1, CHIPS)]


def on_device(
    features,
    hub_list,
    send_list,
    send_count,
    tile_dst,
    tile_src,
    tile_count,
    tile_adj,
    sample_ids,
    labels,
    first_self,
    first_mean,
    second_self,
    second_mean,
):
    nodes, inputs = features.shape
    width, classes = second_self.shape
    hubs = CHIPS * CORES * PEERS * HUBS_EACH
    edges = PEERS * CAPACITY
    table = nodes + hubs + edges
    padded = 2 * TILE
    samples_all = float(sample_ids.shape[1] * CHIPS * CORES * PEERS)

    slots = PEERS * FORWARD_ROWS

    def gather_hubs(arrived, beside):
        own = kernel_call(group_hubs, shape((GROUP_HUBS, inputs), BF16))(arrived)
        blocks = kernel_call(
            join_blocks,
            shape((CHIPS * GROUP_HUBS, inputs), BF16),
            in_specs=[VM] * CHIPS + [ANY] * len(beside),
        )(own, *to_chips(own), *beside)
        return blocks, to_core(blocks)

    rows = kernel_call(
        send_features,
        shape((slots, inputs), BF16),
        [
            pltpu.VMEM((slots, nodes), BF16),
            pltpu.VMEM((nodes, inputs), BF16),
            pltpu.VMEM(send_list.shape[1:], I32),
            pltpu.VMEM(send_count.shape, I32),
            pltpu.SMEM(hub_list.shape, I32),
            pltpu.SemaphoreType.DMA((4,)),
        ],
        [HBM] * 4,
    )(*(pltpu.with_memory_space_constraint(operand, pltpu.HBM) for operand in (features, send_list, send_count, hub_list)))
    feature_arrived = swap(rows.reshape(PEERS, FORWARD_ROWS, inputs))
    raw = (second_self.T, second_mean.T)
    operands = (
        tile_adj, tile_dst, tile_src, tile_count, send_list[0], send_count, hub_list,
        sample_ids, labels.reshape(1, nodes), first_self, first_mean, *raw,
    )
    dense, numbers, weights, wanted, picks = kernel_call(
        build_dense,
        (
            shape((nodes, table), BF16),
            shape((nodes, TILE), F32),
            shape((3 * padded, width), BF16),
            shape((FORWARD_ROWS, PEERS), I32),
            shape((slots, nodes), BF16),
        ),
        [
            pltpu.VMEM(tile_adj.shape, BF16),
            pltpu.SMEM(tile_dst.shape, I32),
            pltpu.SMEM(tile_src.shape, I32),
            pltpu.SMEM(tile_count.shape, I32),
            pltpu.VMEM(send_list.shape[1:], I32),
            pltpu.VMEM(send_count.shape, I32),
            pltpu.SMEM(hub_list.shape, I32),
            pltpu.VMEM(sample_ids.shape, I32),
            pltpu.VMEM((1, nodes), I32),
            pltpu.VMEM(raw[0].shape, BF16),
            pltpu.VMEM(raw[1].shape, BF16),
            pltpu.SemaphoreType.DMA((len(operands),)),
        ],
        [HBM] * len(operands) + [ANY],
        flops=2 * nodes * table * TILE,
        moved=8 * MIB,
    )(
        *(
            operand if operand is tile_count else pltpu.with_memory_space_constraint(operand, pltpu.HBM)
            for operand in operands
        ),
        feature_arrived,
    )
    feature_hubs = gather_hubs(feature_arrived, [numbers])
    part = kernel_call(
        early_means,
        shape((nodes, inputs), F32),
        [pltpu.VMEM((table, inputs), BF16)],
        flops=2 * nodes * table * inputs,
        moved=4 * MIB,
    )(features, feature_arrived, dense, feature_hubs[0])
    mean_rows, rows = kernel_call(
        first_means, (shape((nodes, inputs), BF16), shape((slots, inputs), BF16))
    )(part, dense, numbers, picks, feature_hubs[1])
    mean_arrived = swap(rows.reshape(PEERS, FORWARD_ROWS, inputs))

    hidden, early_turned, early_source, part, own_logits = kernel_call(
        early_part,
        (
            shape((nodes, width), BF16),
            shape((2 * inputs, nodes + edges), BF16),
            shape((nodes + edges, width), BF16),
            shape((nodes, width), F32),
            shape((nodes, padded), F32),
        ),
        [pltpu.VMEM((nodes + edges, 2 * inputs), BF16)],
        limit=8,
        flops=6 * nodes * edges * width,
        moved=8 * MIB,
    )(features, feature_arrived, mean_rows, mean_arrived, dense, weights)
    mean_hubs = gather_hubs(mean_arrived, [own_logits])
    half = CHIPS * GROUP_HUBS
    own_turned, own_source, own_columns, part = kernel_call(
        own_hub_part,
        (
            shape((2 * inputs, half), BF16),
            shape((half, width), BF16),
            shape((nodes, half), BF16),
            shape((nodes, width), F32),
        ),
        limit=6,
        flops=4 * nodes * half * width,
        moved=4 * MIB,
    )(dense, weights, part, feature_hubs[0], mean_hubs[0])
    base, edge_rows, mine, theirs = kernel_call(
        functools.partial(main_part, samples_all, classes),
        (
            shape((nodes, width), F32),
            shape((PEERS, EDGE_ROWS, TILE), BF16),
            shape((CORE_ROWS, TILE), BF16),
            shape((CORE_ROWS, TILE), BF16),
        ),
        [
            pltpu.VMEM((2 * inputs, half), BF16),
            pltpu.VMEM((half, width), BF16),
            pltpu.VMEM((nodes, half), BF16),
            pltpu.VMEM((padded, nodes), BF16),
            pltpu.VMEM((table, width), BF16),
            pltpu.VMEM((STACK_ROWS, width), F32),
        ],
        limit=20,
    )(
        early_turned, early_source, own_logits, own_turned, own_source, own_columns, part,
        dense, numbers, weights, feature_hubs[1], mean_hubs[1],
    )
    rows, *blocks = kernel_call(
        sum_cores, (shape((PEERS, BACK_ROWS, TILE), BF16),) + (shape((CHIP_HUBS, TILE), BF16),) * CHIPS
    )(mine, to_core(theirs), edge_rows)
    arrived = swap(rows)
    sums, *sent = kernel_call(
        sum_peers, (shape((PIECE, TILE), F32),) + (shape((CHIP_ROWS, TILE), BF16),) * (CHIPS - 1)
    )(arrived, *blocks[1:])
    sent = [along_x(block, -1 - i) for i, block in enumerate(sent)]
    base = kernel_call(
        return_edges,
        shape((nodes, width), F32),
        [pltpu.VMEM((slots, padded), BF16), pltpu.VMEM((slots, nodes), BF16)],
        limit=6,
        flops=2 * nodes * (edges * padded + width * padded),
        moved=4 * MIB,
    )(base, arrived, wanted, weights)
    pieces = kernel_call(
        sum_chips,
        shape((PEERS, LAST_ROWS, TILE), BF16),
        in_specs=[VM] * (CHIPS + 1) + [ANY],
    )(sums, blocks[0], *sent, base)
    pieces = swap(pieces)
    grad_hidden = kernel_call(
        return_hubs,
        shape((nodes, width), F32),
        flops=4 * nodes * padded * width,
        moved=4 * MIB,
    )(base, pieces, wanted, weights)
    first_self_sum, first_mean_sum, self_sum, mean_sum, loss = kernel_call(
        functools.partial(weight_outputs, samples_all),
        (
            shape(first_self.shape, F32),
            shape(first_mean.shape, F32),
            shape((classes, width), F32),
            shape((classes, width), F32),
            shape((1, 1), F32),
        ),
    )(pieces, to_core(pieces))
    return hidden, grad_hidden, loss[0, 0], first_self_sum, first_mean_sum, self_sum.T, mean_sum.T


def solution(mesh):
    both = ("grp", "dev")
    placed = (
        P(both, None),
        P(both, None),
        P(both, None, None),
        P(both, None),
        P(both, None),
        P(both, None),
        P(both),
        P(both, None, None),
        P(both, None),
        P(both),
        P(),
        P(),
        P(),
        P(),
    )
    return jax.shard_map(
        on_device,
        mesh=mesh,
        in_specs=placed,
        out_specs=(P(both, None), P(both, None), P(), P(), P(), P(), P()),
        check_vma=False,
    )
```

```python
import functools

import jax
import jax.numpy as jnp
from jax import lax
from jax.experimental import pallas as pl
from jax.experimental.pallas import tpu as pltpu
from jax.sharding import PartitionSpec as P

F32 = jnp.float32
BF16 = jnp.bfloat16
I32 = jnp.int32
MIB = 1 << 20
TILE = 128
HALF = 64
PEERS = 32
CHIPS = 4
CORES = 2
HUBS_EACH = 4
CAPACITY = 32
GROUP_HUBS = PEERS * HUBS_EACH
FORWARD_ROWS = CAPACITY + 8
PEER_HUBS = CORES * CHIPS * HUBS_EACH
EDGE_ROWS = CAPACITY + CAPACITY // 2
HUB_ROWS = 2 * HUBS_EACH
CHIP_HUBS = PEERS * HUB_ROWS
STACK_ROWS = 640
SELF_AT = 256
LOSS_AT = 440
MEAN_AT = 448
CLASS_ROWS = 176
PIECE = STACK_ROWS // CORES * 4 // PEERS
BACK_ROWS = EDGE_ROWS + PIECE
CORE_ROWS = CHIPS * CHIP_HUBS + PEERS * PIECE
CHIP_ROWS = CHIP_HUBS + 2 * PIECE
LAST_ROWS = HUB_ROWS + PIECE

VM = pl.BlockSpec(memory_space=pltpu.VMEM)
SM = pl.BlockSpec(memory_space=pltpu.SMEM)
ANY = pl.BlockSpec(memory_space=pl.ANY)
HBM = pl.BlockSpec(memory_space=pltpu.HBM)


def nn(left, right):
    return jnp.dot(left, right, preferred_element_type=F32)


def nt(left, right):
    return lax.dot_general(left, right, (((1,), (1,)), ((), ())), preferred_element_type=F32)


def tn(left, right):
    return lax.dot_general(left, right, (((0,), (0,)), ((), ())), preferred_element_type=F32)


def split(values):
    high = values.astype(BF16)
    low = (values - high.astype(F32)).astype(BF16)
    return high, low


def one_hot(hit):
    return jnp.where(hit, 1.0, 0.0).astype(BF16)


def iota(dims, axis):
    return lax.broadcasted_iota(I32, dims, axis)


def kernel_call(body, outs, scratch=(), in_specs=None, limit=5, flops=0, moved=0):
    placed = {} if in_specs is None else {"in_specs": in_specs}
    return pl.pallas_call(
        body,
        out_shape=outs,
        **placed,
        scratch_shapes=list(scratch),
        compiler_params=pltpu.CompilerParams(vmem_limit_bytes=limit * MIB),
        cost_estimate=pl.CostEstimate(flops=flops, bytes_accessed=moved, transcendentals=0),
    )


def position():
    group = lax.axis_index("grp")
    return group // CORES, group % CORES


def fetch(pairs, sems):
    loads = [pltpu.make_async_copy(source, target, sems.at[i]) for i, (source, target) in enumerate(pairs)]
    for load in loads:
        load.start()
    return loads


def wanted_rows(send, counts, hub_ref):
    send = jnp.transpose(send)
    send = jnp.where(iota(send.shape, 0) < counts, send, -1)
    row = iota((FORWARD_ROWS - CAPACITY, PEERS), 0)
    hubs = jnp.full(row.shape, -1, I32)
    for k in range(HUBS_EACH):
        hubs = jnp.where(row == k, hub_ref[0, k], hubs)
    return jnp.concatenate([send, hubs], axis=0)


def pick_matrix(wanted, pick_ref):
    lane = iota((2 * FORWARD_ROWS, pick_ref.shape[1]), 1)
    for n in range(0, PEERS, 2):
        pair = jnp.concatenate([wanted[:, n : n + 1], wanted[:, n + 1 : n + 2]], axis=0)
        pick_ref[n * FORWARD_ROWS : (n + 2) * FORWARD_ROWS, :] = one_hot(pair == lane)


def send_features(
    features_any, send_any, count_any, hub_any, out_ref, features_ref, send_ref, count_ref, hub_ref, sems
):
    loads = fetch(
        (
            (send_any.at[0], send_ref),
            (count_any, count_ref),
            (hub_any, hub_ref),
            (features_any, features_ref),
        ),
        sems,
    )
    for load in loads[:-1]:
        load.wait()
    wanted = wanted_rows(send_ref[...], count_ref[...], hub_ref)
    loads[-1].wait()
    features = features_ref[...]
    lane = iota((8 * FORWARD_ROWS, features.shape[0]), 1)
    for n in range(0, PEERS, 8):
        rows = jnp.concatenate([wanted[:, i : i + 1] for i in range(n, n + 8)], axis=0)
        out_ref[n * FORWARD_ROWS : (n + 8) * FORWARD_ROWS, :] = nn(one_hot(rows == lane), features).astype(BF16)


def build_dense(*refs):
    count = 13
    sources, refs = refs[:count], refs[count + 1 :]
    dense_ref, numbers_ref, weights_ref, wanted_ref, pick_ref, *places, sems = refs
    (
        adj_ref, dst_ref, src_ref, live_ref, send_ref, count_ref, hub_ref,
        sample_ref, label_ref, raw_self_ref, raw_mean_ref,
    ) = places
    targets = (
        adj_ref, dst_ref, src_ref, live_ref, send_ref, count_ref, hub_ref, sample_ref, label_ref,
        weights_ref.at[pl.ds(0, TILE)], weights_ref.at[pl.ds(TILE, TILE)], raw_self_ref, raw_mean_ref,
    )
    loads = fetch(zip(sources, targets), sems)
    dense_ref[...] = jnp.zeros_like(dense_ref)
    weights_ref[SELF_AT:, :] = jnp.zeros((weights_ref.shape[0] - SELF_AT, weights_ref.shape[1]), BF16)
    for load in loads:
        load.wait()

    def add(t, carry):
        rows = pl.ds(pl.multiple_of(dst_ref[0, t] * TILE, TILE), TILE)
        columns = pl.ds(pl.multiple_of(src_ref[0, t] * TILE, TILE), TILE)
        dense_ref[rows, columns] += adj_ref[t]
        return carry

    lax.fori_loop(0, live_ref[0], add, 0)
    classes = raw_self_ref.shape[0]
    weights_ref[SELF_AT : SELF_AT + classes, :] = raw_self_ref[...]
    weights_ref[2 * SELF_AT : 2 * SELF_AT + classes, :] = raw_mean_ref[...]
    wanted = wanted_rows(send_ref[...], count_ref[...], hub_ref)
    wanted_ref[...] = wanted
    pick_matrix(wanted, pick_ref)
    nodes = dense_ref.shape[0]
    node = iota((nodes, sample_ref.shape[1]), 0)
    times = jnp.sum(jnp.where(node == sample_ref[...], 1.0, 0.0), axis=1, keepdims=True)
    label = jnp.transpose(jnp.broadcast_to(label_ref[...], (8, nodes)))[:, 0:1]
    degree = jnp.maximum(nn(dense_ref[...], jnp.ones((dense_ref.shape[1], TILE), BF16)), 1.0)
    lane = iota(degree.shape, 1)
    numbers_ref[...] = jnp.where(lane == 0, degree, jnp.where(lane == 1, times, label.astype(F32)))


def group_hubs(arrived_ref, out_ref):
    low = iota((8, TILE), 0) < HUBS_EACH
    rows = []
    for n in range(0, PEERS, 2):
        first = arrived_ref[n, CAPACITY:FORWARD_ROWS, :].astype(F32)
        second = arrived_ref[n + 1, CAPACITY:FORWARD_ROWS, :].astype(F32)
        rows.append(jnp.where(low, first, pltpu.roll(second, HUBS_EACH, 0)))
    out_ref[...] = jnp.concatenate(rows, axis=0).astype(BF16)


def join_blocks(*refs):
    out_ref = refs[-1]
    for i in range(CHIPS):
        out_ref[i * GROUP_HUBS : (i + 1) * GROUP_HUBS, :] = refs[i][...]


def place_hubs(table_ref, start, hub_refs, lanes):
    chip, core = position()
    for there, hub_ref in zip((core, 1 - core), hub_refs):
        for i in range(CHIPS):
            other = (chip + CHIPS - i) % CHIPS
            at = start + (other * CORES + there) * GROUP_HUBS
            block = hub_ref[i * GROUP_HUBS : (i + 1) * GROUP_HUBS, :]
            table_ref[pl.ds(pl.multiple_of(at, GROUP_HUBS), GROUP_HUBS), lanes] = block


def early_means(features_ref, arrived_ref, dense_ref, own_hub_ref, part_ref, table_ref):
    nodes = features_ref.shape[0]
    edge_at = nodes + CORES * CHIPS * GROUP_HUBS
    table_ref[0:nodes, :] = features_ref[...]
    table_ref[nodes:edge_at, :] = jnp.zeros((edge_at - nodes, TILE), BF16)
    place_hubs(table_ref, nodes, (own_hub_ref,), slice(0, TILE))
    for n in range(PEERS):
        at = edge_at + n * CAPACITY
        table_ref[at : at + CAPACITY, :] = arrived_ref[n, 0:CAPACITY, :]
    part_ref[...] = nn(dense_ref[...], table_ref[...])


def first_means(part_ref, dense_ref, numbers_ref, pick_ref, other_hub_ref, mean_ref, out_ref):
    nodes = part_ref.shape[0]
    chip, core = position()
    total = part_ref[...]
    for i in range(CHIPS):
        other = (chip + CHIPS - i) % CHIPS
        at = nodes + (other * CORES + 1 - core) * GROUP_HUBS
        columns = dense_ref[:, pl.ds(pl.multiple_of(at, GROUP_HUBS), GROUP_HUBS)]
        total += nn(columns, other_hub_ref[i * GROUP_HUBS : (i + 1) * GROUP_HUBS, :])
    mean = (total / numbers_ref[:, 0:1]).astype(BF16)
    mean_ref[...] = mean
    out_ref[...] = nn(pick_ref[...], mean).astype(BF16)


def join_rests(first, second):
    return first + pltpu.roll(second, HALF, 1)


def part_rests(packed):
    low = iota(packed.shape, 1) < HALF
    return jnp.where(low, packed, 0.0), jnp.where(low, pltpu.roll(packed, HALF, 1), 0.0)


def early_part(
    features_ref, feature_arrived_ref, mean_ref, arrived_ref, dense_ref, weights_ref,
    hidden_ref, turned_ref, source_ref, part_ref, logits_ref, table_ref,
):
    nodes, width = hidden_ref.shape
    edges = PEERS * CAPACITY
    edge_at = dense_ref.shape[1] - edges
    table_ref[0:nodes, 0:TILE] = features_ref[...]
    table_ref[0:nodes, TILE:] = mean_ref[...]
    for n in range(PEERS):
        at = nodes + n * CAPACITY
        table_ref[at : at + CAPACITY, 0:TILE] = feature_arrived_ref[n, 0:CAPACITY, :]
        table_ref[at : at + CAPACITY, TILE:] = arrived_ref[n, 0:CAPACITY, :]
    for at in range(0, nodes + edges, nodes):
        rows = slice(at, at + nodes)
        linear = nn(table_ref[rows, :], weights_ref[0:SELF_AT, :])
        source_ref[rows, :] = jnp.maximum(linear, 0.0).astype(BF16)
        turned_ref[:, rows] = jnp.transpose(table_ref[rows, :])
    hidden = source_ref[0:nodes, :]
    hidden_ref[...] = hidden
    part_ref[...] = nn(dense_ref[:, 0:nodes], hidden) + nn(dense_ref[:, edge_at:], source_ref[nodes:, :])
    logits_ref[...] = nt(hidden, weights_ref[SELF_AT : 2 * SELF_AT, :])


def hub_part(
    dense_ref, weights_ref, features, means, others, turned_ref, source_ref, columns_ref
):
    nodes = dense_ref.shape[0]
    chip, core = position()
    there = 1 - core if others else core
    table = jnp.concatenate([features, means], axis=1)
    turned_ref[...] = jnp.transpose(table)
    source_ref[...] = jnp.maximum(nn(table, weights_ref[0:SELF_AT, :]), 0.0).astype(BF16)
    for i in range(CHIPS):
        other = (chip + CHIPS - i) % CHIPS
        at = pl.multiple_of(nodes + (other * CORES + there) * GROUP_HUBS, GROUP_HUBS)
        columns_ref[:, i * GROUP_HUBS : (i + 1) * GROUP_HUBS] = dense_ref[:, pl.ds(at, GROUP_HUBS)]
    return nn(columns_ref[...], source_ref[...])


def own_hub_part(
    dense_ref, weights_ref, part_ref, feature_ref, mean_ref, turned_ref, source_ref, columns_ref, out_ref
):
    total = hub_part(
        dense_ref, weights_ref, feature_ref[...], mean_ref[...], False, turned_ref, source_ref, columns_ref
    )
    out_ref[...] = part_ref[...] + total


def main_part(
    samples_all, classes,
    early_turned_ref, early_source_ref, logits_ref, own_turned_ref, own_source_ref, own_columns_ref, part_ref,
    dense_ref, numbers_ref, weights_ref, feature_ref, mean_ref,
    base_ref, edge_ref, mine_ref, theirs_ref,
    other_turned_ref, other_source_ref, other_columns_ref, scaled_ref, masked_ref, stack_ref,
):
    nodes, width = base_ref.shape
    padded = SELF_AT
    self_rows = slice(SELF_AT, 2 * SELF_AT)
    mean_rows = slice(2 * SELF_AT, 3 * SELF_AT)
    edge_at = dense_ref.shape[1] - PEERS * CAPACITY
    total = hub_part(
        dense_ref, weights_ref, feature_ref[...], mean_ref[...], True,
        other_turned_ref, other_source_ref, other_columns_ref,
    )
    hidden = early_source_ref[0:nodes, :]
    degree = numbers_ref[:, 0:1]
    times = numbers_ref[:, 1:2]
    label = numbers_ref[:, 2:3].astype(I32)
    mean = ((part_ref[...] + total) / degree).astype(BF16)
    logits = logits_ref[...] + nt(mean, weights_ref[mean_rows, :])

    lane = iota((nodes, padded), 1)
    real = lane < classes
    onehot = jnp.where(lane == label, 1.0, 0.0)
    top = jnp.max(jnp.where(real, logits, -jnp.inf), axis=1, keepdims=True)
    shifted = logits - top
    powers = jnp.where(real, jnp.exp(shifted), 0.0)
    total = jnp.sum(powers, axis=1, keepdims=True)
    chosen = jnp.sum(onehot * shifted, axis=1, keepdims=True)
    loss = jnp.sum(times * (jnp.log(total) - chosen), axis=0, keepdims=True)
    upstream = times * ((powers / total - onehot) / samples_all)
    upstream = upstream.astype(BF16)
    scaled_ref[...] = (upstream.astype(F32) / degree).astype(BF16)

    def back(columns):
        found = tn(columns, scaled_ref[...])
        return found, nn(found.astype(BF16), weights_ref[mean_rows, :])

    def mask(at, source, grad):
        masked_ref[at : at + nodes, :] = jnp.where(source > 0, grad, 0.0).astype(BF16)

    low = iota((8, TILE), 0) < HUBS_EACH
    hub_at = nodes + PEERS * CAPACITY
    for i, (columns_ref, source_ref, out_ref) in enumerate(
        ((own_columns_ref, own_source_ref, mine_ref), (other_columns_ref, other_source_ref, theirs_ref))
    ):
        found, spread = back(columns_ref[...])
        mask(hub_at + i * nodes, source_ref[...], spread)
        for block in range(CHIPS):
            for n in range(0, PEERS, 2):
                at = block * GROUP_HUBS + n * HUBS_EACH
                mains = found[at : at + 8, 0:TILE]
                rests = found[at : at + 8, TILE:]
                pair = (
                    jnp.where(low, mains, pltpu.roll(rests, HUBS_EACH, 0)),
                    jnp.where(low, pltpu.roll(mains, HUBS_EACH, 0), rests),
                )
                at = block * CHIP_HUBS + n * HUB_ROWS
                out_ref[at : at + 2 * HUB_ROWS, :] = jnp.concatenate(pair, axis=0).astype(BF16)

    unused, spread = back(dense_ref[:, 0:nodes])
    base = nn(upstream, weights_ref[self_rows, :]) + spread
    base_ref[...] = base
    mask(0, hidden, base)
    each = nodes // CAPACITY
    for i in range(PEERS // each):
        found, spread = back(dense_ref[:, edge_at + i * nodes : edge_at + (i + 1) * nodes])
        at = (i + 1) * nodes
        mask(at, early_source_ref[at : at + nodes, :], spread)
        for p in range(each):
            at = p * CAPACITY
            rest = found[at : at + CAPACITY, TILE:]
            edge_ref[i * each + p, 0:CAPACITY, :] = found[at : at + CAPACITY, 0:TILE].astype(BF16)
            edge_ref[i * each + p, CAPACITY:EDGE_ROWS, :] = join_rests(
                rest[0 : CAPACITY // 2], rest[CAPACITY // 2 :]
            ).astype(BF16)

    stack_ref[SELF_AT:, :] = jnp.zeros((STACK_ROWS - SELF_AT, width), F32)
    upstream_turned = jnp.transpose(upstream)
    stack_ref[SELF_AT : SELF_AT + CLASS_ROWS, :] = nn(upstream_turned, hidden)[0:CLASS_ROWS]
    stack_ref[MEAN_AT : MEAN_AT + CLASS_ROWS, :] = nn(upstream_turned, mean)[0:CLASS_ROWS]
    loss_high = loss.astype(BF16).astype(F32)
    place = iota((8, width), 0)
    marks = jnp.where(place == 0, loss_high, 0.0)
    stack_ref[LOSS_AT : LOSS_AT + 8, :] = jnp.where(place == 1, loss - loss_high, marks)
    stack_ref[0:SELF_AT, :] = (
        nn(early_turned_ref[...], masked_ref[0:hub_at, :])
        + nn(own_turned_ref[...], masked_ref[hub_at : hub_at + nodes, :])
        + nn(other_turned_ref[...], masked_ref[hub_at + nodes :, :])
    )
    unused, core = position()
    for there, out_ref in ((core, mine_ref), (1 - core, theirs_ref)):
        for n in range(0, PEERS, 2):
            at = there * (STACK_ROWS // CORES) + PIECE * (n % 8)
            lanes = slice(TILE * (n // 8), TILE * (n // 8 + 1))
            rows = stack_ref[pl.ds(pl.multiple_of(at, 16), 2 * PIECE), lanes]
            at = CHIPS * CHIP_HUBS + n * PIECE
            out_ref[at : at + 2 * PIECE, :] = rows.astype(BF16)


def sum_cores(mine_ref, arrived_ref, edge_ref, out_ref, *hub_refs):
    out_ref[:, 0:EDGE_ROWS, :] = edge_ref[...]
    total = mine_ref[...].astype(F32) + arrived_ref[...].astype(F32)
    for block, hub_ref in enumerate(hub_refs):
        hub_ref[...] = total[block * CHIP_HUBS : (block + 1) * CHIP_HUBS].astype(BF16)
    for n in range(PEERS):
        at = CHIPS * CHIP_HUBS + n * PIECE
        out_ref[n, EDGE_ROWS:BACK_ROWS, :] = total[at : at + PIECE].astype(BF16)


def sum_peers(arrived_ref, *refs):
    hub_refs, (sum_ref, *out_refs) = refs[: CHIPS - 1], refs[CHIPS - 1 :]
    total = arrived_ref[0, EDGE_ROWS:BACK_ROWS, :].astype(F32)
    for n in range(1, PEERS):
        total += arrived_ref[n, EDGE_ROWS:BACK_ROWS, :].astype(F32)
    high = total.astype(BF16).astype(F32)
    low = (total - high).astype(BF16).astype(F32)
    sum_ref[...] = high + low
    parts = jnp.concatenate([high, low], axis=0).astype(BF16)
    for hub_ref, out_ref in zip(hub_refs, out_refs):
        out_ref[0:CHIP_HUBS, :] = hub_ref[...]
        out_ref[CHIP_HUBS:CHIP_ROWS, :] = parts


def return_edges(base_ref, arrived_ref, wanted_ref, weights_ref, out_ref, found_ref, pick_ref):
    pick_matrix(wanted_ref[...], pick_ref)
    found_ref[...] = jnp.zeros_like(found_ref)
    for n in range(PEERS):
        at = n * FORWARD_ROWS
        first, second = part_rests(arrived_ref[n, CAPACITY:EDGE_ROWS, :].astype(F32))
        rest = jnp.concatenate([first, second], axis=0).astype(BF16)
        found_ref[at : at + CAPACITY, 0:TILE] = arrived_ref[n, 0:CAPACITY, :]
        found_ref[at : at + CAPACITY, TILE:] = rest
    rows = tn(pick_ref[...], found_ref[...])
    out_ref[...] = base_ref[...] + nn(rows.astype(BF16), weights_ref[2 * SELF_AT :, :])


def sum_chips(sum_ref, own_ref, *refs):
    sent_refs, out_ref = refs[: CHIPS - 1], refs[-1]
    hubs = own_ref[...].astype(F32)
    pieces = [sum_ref[...]]
    for sent_ref in sent_refs:
        rows = sent_ref[...].astype(F32)
        hubs += rows[0:CHIP_HUBS]
        pieces.append(rows[CHIP_HUBS : CHIP_HUBS + PIECE] + rows[CHIP_HUBS + PIECE : CHIP_ROWS])
    piece = (pieces[0] + pieces[2]) + (pieces[1] + pieces[3])
    unused, core = position()
    holder = (core == LOSS_AT * CORES // STACK_ROWS) & (lax.axis_index("dev") == LOSS_AT % (STACK_ROWS // CORES) // PIECE)
    rest = piece[0:1] - piece[0:1].astype(BF16).astype(F32)
    row = iota(piece.shape, 0)
    piece = jnp.where((row == 2) & holder, rest, piece)
    tail = piece[8:PIECE].astype(BF16)
    for n in range(PEERS):
        head = jnp.concatenate([hubs[n * HUB_ROWS : (n + 1) * HUB_ROWS], piece[0:8]], axis=0)
        out_ref[n, 0:16, :] = head.astype(BF16)
        out_ref[n, 16:LAST_ROWS, :] = tail


def return_hubs(base_ref, arrived_ref, wanted_ref, weights_ref, out_ref):
    nodes = out_ref.shape[0]
    hubs = arrived_ref[0, 0:16, :].astype(F32)
    for n in range(1, PEERS):
        hubs += arrived_ref[n, 0:16, :].astype(F32)
    hubs = hubs[0:HUB_ROWS]
    hubs = jnp.concatenate([hubs, pltpu.roll(hubs, HUBS_EACH, 0)], axis=1)
    high, low = split(nn(hubs.astype(BF16), weights_ref[2 * SELF_AT :, :]))
    owner = one_hot(wanted_ref[CAPACITY:FORWARD_ROWS, 0:1] == iota((HUB_ROWS, nodes), 1))
    out_ref[...] = base_ref[...] + tn(owner, high) + tn(owner, low)


def weight_outputs(samples_all, mine_ref, theirs_ref, first_self_ref, first_mean_ref, self_ref, mean_ref, loss_ref):
    unused, core = position()
    half = STACK_ROWS // CORES
    classes = self_ref.shape[0]
    spans = (
        (0, TILE, first_self_ref),
        (TILE, 2 * TILE, first_mean_ref),
        (SELF_AT, SELF_AT + classes, self_ref),
        (MEAN_AT, MEAN_AT + classes, mean_ref),
    )
    for n in range(PEERS):
        mine = mine_ref[n].astype(F32)[HUB_ROWS:]
        theirs = theirs_ref[n].astype(F32)[HUB_ROWS:]
        lanes = slice(TILE * (n // 8), TILE * (n // 8 + 1))
        for at, piece in (
            (PIECE * (n % 8), jnp.where(core == 0, mine, theirs)),
            (half + PIECE * (n % 8), jnp.where(core == 0, theirs, mine)),
        ):
            for start, end, out_ref in spans:
                low, high = max(start, at), min(end, at + PIECE)
                if low < high:
                    out_ref[low - start : high - start, lanes] = piece[low - at : high - at]
            if at == LOSS_AT and lanes.start == 0:
                loss_ref[...] = (piece[0:1, 0:1] + piece[1:2, 0:1] + piece[2:3, 0:1]) / samples_all


def shape(dims, dtype):
    return jax.ShapeDtypeStruct(dims, dtype)


def swap(values):
    return lax.all_to_all(values, "dev", split_axis=0, concat_axis=0, tiled=True)


def to_core(values):
    return lax.ppermute(values, "grp", [(i, i ^ 1) for i in range(CHIPS * CORES)])


def along_x(values, shift):
    every = CHIPS * CORES
    return lax.ppermute(values, "grp", [(i, (i + CORES * shift) % every) for i in range(every)])


def to_chips(values):
    return [along_x(values, shift) for shift in range(1, CHIPS)]


def on_device(
    features,
    hub_list,
    send_list,
    send_count,
    tile_dst,
    tile_src,
    tile_count,
    tile_adj,
    sample_ids,
    labels,
    first_self,
    first_mean,
    second_self,
    second_mean,
):
    nodes, inputs = features.shape
    width, classes = second_self.shape
    hubs = CHIPS * CORES * PEERS * HUBS_EACH
    edges = PEERS * CAPACITY
    table = nodes + hubs + edges
    padded = 2 * TILE
    samples_all = float(sample_ids.shape[1] * CHIPS * CORES * PEERS)

    slots = PEERS * FORWARD_ROWS

    def gather_hubs(arrived, beside):
        own = kernel_call(group_hubs, shape((GROUP_HUBS, inputs), BF16))(arrived)
        blocks = kernel_call(
            join_blocks,
            shape((CHIPS * GROUP_HUBS, inputs), BF16),
            in_specs=[VM] * CHIPS + [ANY] * len(beside),
        )(own, *to_chips(own), *beside)
        return blocks, to_core(blocks)

    rows = kernel_call(
        send_features,
        shape((slots, inputs), BF16),
        [
            pltpu.VMEM((nodes, inputs), BF16),
            pltpu.VMEM(send_list.shape[1:], I32),
            pltpu.VMEM(send_count.shape, I32),
            pltpu.SMEM(hub_list.shape, I32),
            pltpu.SemaphoreType.DMA((4,)),
        ],
        [HBM] * 4,
    )(*(pltpu.with_memory_space_constraint(operand, pltpu.HBM) for operand in (features, send_list, send_count, hub_list)))
    feature_arrived = swap(rows.reshape(PEERS, FORWARD_ROWS, inputs))
    raw = (second_self.T, second_mean.T)
    operands = (
        tile_adj, tile_dst, tile_src, tile_count, send_list[0], send_count, hub_list,
        sample_ids, labels.reshape(1, nodes), first_self, first_mean, *raw,
    )
    dense, numbers, weights, wanted, picks = kernel_call(
        build_dense,
        (
            shape((nodes, table), BF16),
            shape((nodes, TILE), F32),
            shape((3 * padded, width), BF16),
            shape((FORWARD_ROWS, PEERS), I32),
            shape((slots, nodes), BF16),
        ),
        [
            pltpu.VMEM(tile_adj.shape, BF16),
            pltpu.SMEM(tile_dst.shape, I32),
            pltpu.SMEM(tile_src.shape, I32),
            pltpu.SMEM(tile_count.shape, I32),
            pltpu.VMEM(send_list.shape[1:], I32),
            pltpu.VMEM(send_count.shape, I32),
            pltpu.SMEM(hub_list.shape, I32),
            pltpu.VMEM(sample_ids.shape, I32),
            pltpu.VMEM((1, nodes), I32),
            pltpu.VMEM(raw[0].shape, BF16),
            pltpu.VMEM(raw[1].shape, BF16),
            pltpu.SemaphoreType.DMA((len(operands),)),
        ],
        [HBM] * len(operands) + [ANY],
        flops=2 * nodes * table * TILE,
        moved=8 * MIB,
    )(
        *(
            operand if operand is tile_count else pltpu.with_memory_space_constraint(operand, pltpu.HBM)
            for operand in operands
        ),
        feature_arrived,
    )
    feature_hubs = gather_hubs(feature_arrived, [numbers])
    part = kernel_call(
        early_means,
        shape((nodes, inputs), F32),
        [pltpu.VMEM((table, inputs), BF16)],
        flops=2 * nodes * table * inputs,
        moved=4 * MIB,
    )(features, feature_arrived, dense, feature_hubs[0])
    mean_rows, rows = kernel_call(
        first_means, (shape((nodes, inputs), BF16), shape((slots, inputs), BF16))
    )(part, dense, numbers, picks, feature_hubs[1])
    mean_arrived = swap(rows.reshape(PEERS, FORWARD_ROWS, inputs))

    hidden, early_turned, early_source, part, own_logits = kernel_call(
        early_part,
        (
            shape((nodes, width), BF16),
            shape((2 * inputs, nodes + edges), BF16),
            shape((nodes + edges, width), BF16),
            shape((nodes, width), F32),
            shape((nodes, padded), F32),
        ),
        [pltpu.VMEM((nodes + edges, 2 * inputs), BF16)],
        limit=8,
        flops=6 * nodes * edges * width,
        moved=8 * MIB,
    )(features, feature_arrived, mean_rows, mean_arrived, dense, weights)
    mean_hubs = gather_hubs(mean_arrived, [own_logits])
    half = CHIPS * GROUP_HUBS
    own_turned, own_source, own_columns, part = kernel_call(
        own_hub_part,
        (
            shape((2 * inputs, half), BF16),
            shape((half, width), BF16),
            shape((nodes, half), BF16),
            shape((nodes, width), F32),
        ),
        limit=6,
        flops=4 * nodes * half * width,
        moved=4 * MIB,
    )(dense, weights, part, feature_hubs[0], mean_hubs[0])
    base, edge_rows, mine, theirs = kernel_call(
        functools.partial(main_part, samples_all, classes),
        (
            shape((nodes, width), F32),
            shape((PEERS, EDGE_ROWS, TILE), BF16),
            shape((CORE_ROWS, TILE), BF16),
            shape((CORE_ROWS, TILE), BF16),
        ),
        [
            pltpu.VMEM((2 * inputs, half), BF16),
            pltpu.VMEM((half, width), BF16),
            pltpu.VMEM((nodes, half), BF16),
            pltpu.VMEM((nodes, padded), BF16),
            pltpu.VMEM((table, width), BF16),
            pltpu.VMEM((STACK_ROWS, width), F32),
        ],
        limit=20,
    )(
        early_turned, early_source, own_logits, own_turned, own_source, own_columns, part,
        dense, numbers, weights, feature_hubs[1], mean_hubs[1],
    )
    rows, *blocks = kernel_call(
        sum_cores, (shape((PEERS, BACK_ROWS, TILE), BF16),) + (shape((CHIP_HUBS, TILE), BF16),) * CHIPS
    )(mine, to_core(theirs), edge_rows)
    arrived = swap(rows)
    sums, *sent = kernel_call(
        sum_peers, (shape((PIECE, TILE), F32),) + (shape((CHIP_ROWS, TILE), BF16),) * (CHIPS - 1)
    )(arrived, *blocks[1:])
    sent = [along_x(block, -1 - i) for i, block in enumerate(sent)]
    base = kernel_call(
        return_edges,
        shape((nodes, width), F32),
        [pltpu.VMEM((slots, padded), BF16), pltpu.VMEM((slots, nodes), BF16)],
        limit=6,
        flops=2 * nodes * (edges * padded + width * padded),
        moved=4 * MIB,
    )(base, arrived, wanted, weights)
    pieces = kernel_call(
        sum_chips,
        shape((PEERS, LAST_ROWS, TILE), BF16),
        in_specs=[VM] * (CHIPS + 1) + [ANY],
    )(sums, blocks[0], *sent, base)
    pieces = swap(pieces)
    grad_hidden = kernel_call(
        return_hubs,
        shape((nodes, width), F32),
        flops=4 * nodes * padded * width,
        moved=4 * MIB,
    )(base, pieces, wanted, weights)
    first_self_sum, first_mean_sum, self_sum, mean_sum, loss = kernel_call(
        functools.partial(weight_outputs, samples_all),
        (
            shape(first_self.shape, F32),
            shape(first_mean.shape, F32),
            shape((classes, width), F32),
            shape((classes, width), F32),
            shape((1, 1), F32),
        ),
    )(pieces, to_core(pieces))
    return hidden, grad_hidden, loss[0, 0], first_self_sum, first_mean_sum, self_sum.T, mean_sum.T


def solution(mesh):
    both = ("grp", "dev")
    placed = (
        P(both, None),
        P(both, None),
        P(both, None, None),
        P(both, None),
        P(both, None),
        P(both, None),
        P(both),
        P(both, None, None),
        P(both, None),
        P(both),
        P(),
        P(),
        P(),
        P(),
    )
    return jax.shard_map(
        on_device,
        mesh=mesh,
        in_specs=placed,
        out_specs=(P(both, None), P(both, None), P(), P(), P(), P(), P()),
        check_vma=False,
    )
```

```python
import functools

import jax
import jax.numpy as jnp
from jax import lax
from jax.experimental import pallas as pl
from jax.experimental.pallas import tpu as pltpu
from jax.sharding import PartitionSpec as P

F32 = jnp.float32
BF16 = jnp.bfloat16
I32 = jnp.int32
MIB = 1 << 20
TILE = 128
HALF = 64
PEERS = 32
CHIPS = 4
CORES = 2
HUBS_EACH = 4
CAPACITY = 32
GROUP_HUBS = PEERS * HUBS_EACH
FORWARD_ROWS = CAPACITY + 8
PEER_HUBS = CORES * CHIPS * HUBS_EACH
EDGE_ROWS = CAPACITY + CAPACITY // 2
HUB_ROWS = 2 * HUBS_EACH
CHIP_HUBS = PEERS * HUB_ROWS
STACK_ROWS = 640
SELF_AT = 256
LOSS_AT = 440
MEAN_AT = 448
CLASS_ROWS = 176
PIECE = STACK_ROWS // CORES * 4 // PEERS
BACK_ROWS = EDGE_ROWS + PIECE
CORE_ROWS = CHIPS * CHIP_HUBS + PEERS * PIECE
CHIP_ROWS = CHIP_HUBS + 2 * PIECE
LAST_ROWS = HUB_ROWS + PIECE

VM = pl.BlockSpec(memory_space=pltpu.VMEM)
SM = pl.BlockSpec(memory_space=pltpu.SMEM)
ANY = pl.BlockSpec(memory_space=pl.ANY)
HBM = pl.BlockSpec(memory_space=pltpu.HBM)


def nn(left, right):
    return jnp.dot(left, right, preferred_element_type=F32)


def nt(left, right):
    return lax.dot_general(left, right, (((1,), (1,)), ((), ())), preferred_element_type=F32)


def tn(left, right):
    return lax.dot_general(left, right, (((0,), (0,)), ((), ())), preferred_element_type=F32)


def split(values):
    high = values.astype(BF16)
    low = (values - high.astype(F32)).astype(BF16)
    return high, low


def one_hot(hit):
    return jnp.where(hit, 1.0, 0.0).astype(BF16)


def iota(dims, axis):
    return lax.broadcasted_iota(I32, dims, axis)


def kernel_call(body, outs, scratch=(), in_specs=None, limit=5, flops=0, moved=0):
    placed = {} if in_specs is None else {"in_specs": in_specs}
    return pl.pallas_call(
        body,
        out_shape=outs,
        **placed,
        scratch_shapes=list(scratch),
        compiler_params=pltpu.CompilerParams(vmem_limit_bytes=limit * MIB),
        cost_estimate=pl.CostEstimate(flops=flops, bytes_accessed=moved, transcendentals=0),
    )


def position():
    group = lax.axis_index("grp")
    return group // CORES, group % CORES


def fetch(pairs, sems):
    loads = [pltpu.make_async_copy(source, target, sems.at[i]) for i, (source, target) in enumerate(pairs)]
    for load in loads:
        load.start()
    return loads


def wanted_rows(send, counts, hub_ref):
    send = jnp.transpose(send)
    send = jnp.where(iota(send.shape, 0) < counts, send, -1)
    row = iota((FORWARD_ROWS - CAPACITY, PEERS), 0)
    hubs = jnp.full(row.shape, -1, I32)
    for k in range(HUBS_EACH):
        hubs = jnp.where(row == k, hub_ref[0, k], hubs)
    return jnp.concatenate([send, hubs], axis=0)


def pick_matrix(wanted, pick_ref):
    lane = iota((2 * FORWARD_ROWS, pick_ref.shape[1]), 1)
    for n in range(0, PEERS, 2):
        pair = jnp.concatenate([wanted[:, n : n + 1], wanted[:, n + 1 : n + 2]], axis=0)
        pick_ref[n * FORWARD_ROWS : (n + 2) * FORWARD_ROWS, :] = one_hot(pair == lane)


def send_features(
    features_any, send_any, count_any, hub_any, out_ref, features_ref, send_ref, count_ref, hub_ref, sems
):
    loads = fetch(
        (
            (send_any.at[0], send_ref),
            (count_any, count_ref),
            (hub_any, hub_ref),
            (features_any, features_ref),
        ),
        sems,
    )
    for load in loads[:-1]:
        load.wait()
    wanted = wanted_rows(send_ref[...], count_ref[...], hub_ref)
    loads[-1].wait()
    features = features_ref[...]
    lane = iota((8 * FORWARD_ROWS, features.shape[0]), 1)
    for n in range(0, PEERS, 8):
        rows = jnp.concatenate([wanted[:, i : i + 1] for i in range(n, n + 8)], axis=0)
        out_ref[n * FORWARD_ROWS : (n + 8) * FORWARD_ROWS, :] = nn(one_hot(rows == lane), features).astype(BF16)


def build_dense(*refs):
    count = 11
    sources, refs = refs[:count], refs[count + 1 :]
    dense_ref, numbers_ref, weights_ref, wanted_ref, pick_ref, *places, sems = refs
    (
        adj_ref, dst_ref, src_ref, live_ref, send_ref, count_ref, hub_ref, raw_self_ref, raw_mean_ref,
    ) = places
    targets = (
        adj_ref, dst_ref, src_ref, live_ref, send_ref, count_ref, hub_ref,
        weights_ref.at[pl.ds(0, TILE)], weights_ref.at[pl.ds(TILE, TILE)], raw_self_ref, raw_mean_ref,
    )
    loads = fetch(zip(sources, targets), sems)
    dense_ref[...] = jnp.zeros_like(dense_ref)
    weights_ref[SELF_AT:, :] = jnp.zeros((weights_ref.shape[0] - SELF_AT, weights_ref.shape[1]), BF16)
    for load in loads:
        load.wait()

    def add(t, carry):
        rows = pl.ds(pl.multiple_of(dst_ref[0, t] * TILE, TILE), TILE)
        columns = pl.ds(pl.multiple_of(src_ref[0, t] * TILE, TILE), TILE)
        dense_ref[rows, columns] += adj_ref[t]
        return carry

    lax.fori_loop(0, live_ref[0], add, 0)
    classes = raw_self_ref.shape[0]
    weights_ref[SELF_AT : SELF_AT + classes, :] = raw_self_ref[...]
    weights_ref[2 * SELF_AT : 2 * SELF_AT + classes, :] = raw_mean_ref[...]
    wanted = wanted_rows(send_ref[...], count_ref[...], hub_ref)
    wanted_ref[...] = wanted
    pick_matrix(wanted, pick_ref)
    degree = jnp.maximum(nn(dense_ref[...], jnp.ones((dense_ref.shape[1], TILE), BF16)), 1.0)
    numbers_ref[...] = degree


def group_hubs(arrived_ref, out_ref):
    low = iota((8, TILE), 0) < HUBS_EACH
    rows = []
    for n in range(0, PEERS, 2):
        first = arrived_ref[n, CAPACITY:FORWARD_ROWS, :].astype(F32)
        second = arrived_ref[n + 1, CAPACITY:FORWARD_ROWS, :].astype(F32)
        rows.append(jnp.where(low, first, pltpu.roll(second, HUBS_EACH, 0)))
    out_ref[...] = jnp.concatenate(rows, axis=0).astype(BF16)


def join_blocks(*refs):
    out_ref = refs[-1]
    for i in range(CHIPS):
        out_ref[i * GROUP_HUBS : (i + 1) * GROUP_HUBS, :] = refs[i][...]


def place_hubs(table_ref, start, hub_refs, lanes):
    chip, core = position()
    for there, hub_ref in zip((core, 1 - core), hub_refs):
        for i in range(CHIPS):
            other = (chip + CHIPS - i) % CHIPS
            at = start + (other * CORES + there) * GROUP_HUBS
            block = hub_ref[i * GROUP_HUBS : (i + 1) * GROUP_HUBS, :]
            table_ref[pl.ds(pl.multiple_of(at, GROUP_HUBS), GROUP_HUBS), lanes] = block


def early_means(features_ref, arrived_ref, dense_ref, own_hub_ref, part_ref, table_ref):
    nodes = features_ref.shape[0]
    edge_at = nodes + CORES * CHIPS * GROUP_HUBS
    table_ref[0:nodes, :] = features_ref[...]
    table_ref[nodes:edge_at, :] = jnp.zeros((edge_at - nodes, TILE), BF16)
    place_hubs(table_ref, nodes, (own_hub_ref,), slice(0, TILE))
    for n in range(PEERS):
        at = edge_at + n * CAPACITY
        table_ref[at : at + CAPACITY, :] = arrived_ref[n, 0:CAPACITY, :]
    part_ref[...] = nn(dense_ref[...], table_ref[...])


def first_means(part_ref, dense_ref, numbers_ref, pick_ref, other_hub_ref, mean_ref, out_ref):
    nodes = part_ref.shape[0]
    chip, core = position()
    total = part_ref[...]
    for i in range(CHIPS):
        other = (chip + CHIPS - i) % CHIPS
        at = nodes + (other * CORES + 1 - core) * GROUP_HUBS
        columns = dense_ref[:, pl.ds(pl.multiple_of(at, GROUP_HUBS), GROUP_HUBS)]
        total += nn(columns, other_hub_ref[i * GROUP_HUBS : (i + 1) * GROUP_HUBS, :])
    mean = (total / numbers_ref[:, 0:1]).astype(BF16)
    mean_ref[...] = mean
    out_ref[...] = nn(pick_ref[...], mean).astype(BF16)


def join_rests(first, second):
    return first + pltpu.roll(second, HALF, 1)


def part_rests(packed):
    low = iota(packed.shape, 1) < HALF
    return jnp.where(low, packed, 0.0), jnp.where(low, pltpu.roll(packed, HALF, 1), 0.0)


def early_part(
    features_ref, feature_arrived_ref, mean_ref, arrived_ref, dense_ref, weights_ref,
    hidden_ref, turned_ref, source_ref, part_ref, logits_ref, table_ref,
):
    nodes, width = hidden_ref.shape
    edges = PEERS * CAPACITY
    edge_at = dense_ref.shape[1] - edges
    table_ref[0:nodes, 0:TILE] = features_ref[...]
    table_ref[0:nodes, TILE:] = mean_ref[...]
    for n in range(PEERS):
        at = nodes + n * CAPACITY
        table_ref[at : at + CAPACITY, 0:TILE] = feature_arrived_ref[n, 0:CAPACITY, :]
        table_ref[at : at + CAPACITY, TILE:] = arrived_ref[n, 0:CAPACITY, :]
    for at in range(0, nodes + edges, nodes):
        rows = slice(at, at + nodes)
        linear = nn(table_ref[rows, :], weights_ref[0:SELF_AT, :])
        source_ref[rows, :] = jnp.maximum(linear, 0.0).astype(BF16)
        turned_ref[:, rows] = jnp.transpose(table_ref[rows, :])
    hidden = source_ref[0:nodes, :]
    hidden_ref[...] = hidden
    part_ref[...] = nn(dense_ref[:, 0:nodes], hidden) + nn(dense_ref[:, edge_at:], source_ref[nodes:, :])
    logits_ref[...] = nt(hidden, weights_ref[SELF_AT : 2 * SELF_AT, :])


def hub_part(
    dense_ref, weights_ref, features, means, others, turned_ref, source_ref, columns_ref
):
    nodes = dense_ref.shape[0]
    chip, core = position()
    there = 1 - core if others else core
    table = jnp.concatenate([features, means], axis=1)
    turned_ref[...] = jnp.transpose(table)
    source_ref[...] = jnp.maximum(nn(table, weights_ref[0:SELF_AT, :]), 0.0).astype(BF16)
    for i in range(CHIPS):
        other = (chip + CHIPS - i) % CHIPS
        at = pl.multiple_of(nodes + (other * CORES + there) * GROUP_HUBS, GROUP_HUBS)
        columns_ref[:, i * GROUP_HUBS : (i + 1) * GROUP_HUBS] = dense_ref[:, pl.ds(at, GROUP_HUBS)]
    return nn(columns_ref[...], source_ref[...])


def own_hub_part(
    dense_ref, weights_ref, part_ref, feature_ref, mean_ref, sample_any, label_any,
    turned_ref, source_ref, columns_ref, out_ref, times_ref, sample_ref, label_ref, sems,
):
    loads = fetch(((sample_any, sample_ref), (label_any, label_ref)), sems)
    total = hub_part(
        dense_ref, weights_ref, feature_ref[...], mean_ref[...], False, turned_ref, source_ref, columns_ref
    )
    out_ref[...] = part_ref[...] + total
    for load in loads:
        load.wait()
    nodes = dense_ref.shape[0]
    node = iota((nodes, sample_ref.shape[1]), 0)
    times = jnp.sum(jnp.where(node == sample_ref[...], 1.0, 0.0), axis=1, keepdims=True)
    label = jnp.transpose(jnp.broadcast_to(label_ref[...], (8, nodes)))[:, 0:1]
    times_ref[...] = jnp.where(iota(times_ref.shape, 1) == 0, times, label.astype(F32))


def main_part(
    samples_all, classes,
    early_turned_ref, early_source_ref, logits_ref, own_turned_ref, own_source_ref, own_columns_ref, part_ref,
    dense_ref, numbers_ref, times_ref, weights_ref, feature_ref, mean_ref,
    base_ref, edge_ref, mine_ref, theirs_ref,
    other_turned_ref, other_source_ref, other_columns_ref, scaled_ref, masked_ref, stack_ref,
):
    nodes, width = base_ref.shape
    padded = SELF_AT
    self_rows = slice(SELF_AT, 2 * SELF_AT)
    mean_rows = slice(2 * SELF_AT, 3 * SELF_AT)
    edge_at = dense_ref.shape[1] - PEERS * CAPACITY
    total = hub_part(
        dense_ref, weights_ref, feature_ref[...], mean_ref[...], True,
        other_turned_ref, other_source_ref, other_columns_ref,
    )
    hidden = early_source_ref[0:nodes, :]
    degree = numbers_ref[:, 0:1]
    times = times_ref[:, 0:1]
    label = times_ref[:, 1:2].astype(I32)
    mean = ((part_ref[...] + total) / degree).astype(BF16)
    logits = logits_ref[...] + nt(mean, weights_ref[mean_rows, :])

    lane = iota((nodes, padded), 1)
    real = lane < classes
    onehot = jnp.where(lane == label, 1.0, 0.0)
    top = jnp.max(jnp.where(real, logits, -jnp.inf), axis=1, keepdims=True)
    shifted = logits - top
    powers = jnp.where(real, jnp.exp(shifted), 0.0)
    total = jnp.sum(powers, axis=1, keepdims=True)
    chosen = jnp.sum(onehot * shifted, axis=1, keepdims=True)
    loss = jnp.sum(times * (jnp.log(total) - chosen), axis=0, keepdims=True)
    upstream = times * ((powers / total - onehot) / samples_all)
    upstream = upstream.astype(BF16)
    scaled_ref[...] = (upstream.astype(F32) / degree).astype(BF16)

    def back(columns):
        found = tn(columns, scaled_ref[...])
        return found, nn(found.astype(BF16), weights_ref[mean_rows, :])

    def mask(at, source, grad):
        masked_ref[at : at + nodes, :] = jnp.where(source > 0, grad, 0.0).astype(BF16)

    low = iota((8, TILE), 0) < HUBS_EACH
    hub_at = nodes + PEERS * CAPACITY
    for i, (columns_ref, source_ref, out_ref) in enumerate(
        ((own_columns_ref, own_source_ref, mine_ref), (other_columns_ref, other_source_ref, theirs_ref))
    ):
        found, spread = back(columns_ref[...])
        mask(hub_at + i * nodes, source_ref[...], spread)
        for block in range(CHIPS):
            for n in range(0, PEERS, 2):
                at = block * GROUP_HUBS + n * HUBS_EACH
                mains = found[at : at + 8, 0:TILE]
                rests = found[at : at + 8, TILE:]
                pair = (
                    jnp.where(low, mains, pltpu.roll(rests, HUBS_EACH, 0)),
                    jnp.where(low, pltpu.roll(mains, HUBS_EACH, 0), rests),
                )
                at = block * CHIP_HUBS + n * HUB_ROWS
                out_ref[at : at + 2 * HUB_ROWS, :] = jnp.concatenate(pair, axis=0).astype(BF16)

    unused, spread = back(dense_ref[:, 0:nodes])
    base = nn(upstream, weights_ref[self_rows, :]) + spread
    base_ref[...] = base
    mask(0, hidden, base)
    each = nodes // CAPACITY
    for i in range(PEERS // each):
        found, spread = back(dense_ref[:, edge_at + i * nodes : edge_at + (i + 1) * nodes])
        at = (i + 1) * nodes
        mask(at, early_source_ref[at : at + nodes, :], spread)
        for p in range(each):
            at = p * CAPACITY
            rest = found[at : at + CAPACITY, TILE:]
            edge_ref[i * each + p, 0:CAPACITY, :] = found[at : at + CAPACITY, 0:TILE].astype(BF16)
            edge_ref[i * each + p, CAPACITY:EDGE_ROWS, :] = join_rests(
                rest[0 : CAPACITY // 2], rest[CAPACITY // 2 :]
            ).astype(BF16)

    stack_ref[SELF_AT:, :] = jnp.zeros((STACK_ROWS - SELF_AT, width), F32)
    upstream_turned = jnp.transpose(upstream)
    stack_ref[SELF_AT : SELF_AT + CLASS_ROWS, :] = nn(upstream_turned, hidden)[0:CLASS_ROWS]
    stack_ref[MEAN_AT : MEAN_AT + CLASS_ROWS, :] = nn(upstream_turned, mean)[0:CLASS_ROWS]
    loss_high = loss.astype(BF16).astype(F32)
    place = iota((8, width), 0)
    marks = jnp.where(place == 0, loss_high, 0.0)
    stack_ref[LOSS_AT : LOSS_AT + 8, :] = jnp.where(place == 1, loss - loss_high, marks)
    stack_ref[0:SELF_AT, :] = (
        nn(early_turned_ref[...], masked_ref[0:hub_at, :])
        + nn(own_turned_ref[...], masked_ref[hub_at : hub_at + nodes, :])
        + nn(other_turned_ref[...], masked_ref[hub_at + nodes :, :])
    )
    unused, core = position()
    for there, out_ref in ((core, mine_ref), (1 - core, theirs_ref)):
        for n in range(0, PEERS, 2):
            at = there * (STACK_ROWS // CORES) + PIECE * (n % 8)
            lanes = slice(TILE * (n // 8), TILE * (n // 8 + 1))
            rows = stack_ref[pl.ds(pl.multiple_of(at, 16), 2 * PIECE), lanes]
            at = CHIPS * CHIP_HUBS + n * PIECE
            out_ref[at : at + 2 * PIECE, :] = rows.astype(BF16)


def sum_cores(mine_ref, arrived_ref, edge_ref, out_ref, *hub_refs):
    out_ref[:, 0:EDGE_ROWS, :] = edge_ref[...]
    total = mine_ref[...].astype(F32) + arrived_ref[...].astype(F32)
    for block, hub_ref in enumerate(hub_refs):
        hub_ref[...] = total[block * CHIP_HUBS : (block + 1) * CHIP_HUBS].astype(BF16)
    for n in range(PEERS):
        at = CHIPS * CHIP_HUBS + n * PIECE
        out_ref[n, EDGE_ROWS:BACK_ROWS, :] = total[at : at + PIECE].astype(BF16)


def sum_peers(arrived_ref, *refs):
    hub_refs, (sum_ref, *out_refs) = refs[: CHIPS - 1], refs[CHIPS - 1 :]
    total = arrived_ref[0, EDGE_ROWS:BACK_ROWS, :].astype(F32)
    for n in range(1, PEERS):
        total += arrived_ref[n, EDGE_ROWS:BACK_ROWS, :].astype(F32)
    high = total.astype(BF16).astype(F32)
    low = (total - high).astype(BF16).astype(F32)
    sum_ref[...] = high + low
    parts = jnp.concatenate([high, low], axis=0).astype(BF16)
    for hub_ref, out_ref in zip(hub_refs, out_refs):
        out_ref[0:CHIP_HUBS, :] = hub_ref[...]
        out_ref[CHIP_HUBS:CHIP_ROWS, :] = parts


def return_edges(base_ref, arrived_ref, wanted_ref, weights_ref, out_ref, found_ref, pick_ref):
    pick_matrix(wanted_ref[...], pick_ref)
    found_ref[...] = jnp.zeros_like(found_ref)
    for n in range(PEERS):
        at = n * FORWARD_ROWS
        first, second = part_rests(arrived_ref[n, CAPACITY:EDGE_ROWS, :].astype(F32))
        rest = jnp.concatenate([first, second], axis=0).astype(BF16)
        found_ref[at : at + CAPACITY, 0:TILE] = arrived_ref[n, 0:CAPACITY, :]
        found_ref[at : at + CAPACITY, TILE:] = rest
    rows = tn(pick_ref[...], found_ref[...])
    out_ref[...] = base_ref[...] + nn(rows.astype(BF16), weights_ref[2 * SELF_AT :, :])


def sum_chips(sum_ref, own_ref, *refs):
    sent_refs, out_ref = refs[: CHIPS - 1], refs[-1]
    hubs = own_ref[...].astype(F32)
    pieces = [sum_ref[...]]
    for sent_ref in sent_refs:
        rows = sent_ref[...].astype(F32)
        hubs += rows[0:CHIP_HUBS]
        pieces.append(rows[CHIP_HUBS : CHIP_HUBS + PIECE] + rows[CHIP_HUBS + PIECE : CHIP_ROWS])
    piece = (pieces[0] + pieces[2]) + (pieces[1] + pieces[3])
    unused, core = position()
    holder = (core == LOSS_AT * CORES // STACK_ROWS) & (lax.axis_index("dev") == LOSS_AT % (STACK_ROWS // CORES) // PIECE)
    rest = piece[0:1] - piece[0:1].astype(BF16).astype(F32)
    row = iota(piece.shape, 0)
    piece = jnp.where((row == 2) & holder, rest, piece)
    tail = piece[8:PIECE].astype(BF16)
    for n in range(PEERS):
        head = jnp.concatenate([hubs[n * HUB_ROWS : (n + 1) * HUB_ROWS], piece[0:8]], axis=0)
        out_ref[n, 0:16, :] = head.astype(BF16)
        out_ref[n, 16:LAST_ROWS, :] = tail


def return_hubs(base_ref, arrived_ref, wanted_ref, weights_ref, out_ref):
    nodes = out_ref.shape[0]
    hubs = arrived_ref[0, 0:16, :].astype(F32)
    for n in range(1, PEERS):
        hubs += arrived_ref[n, 0:16, :].astype(F32)
    hubs = hubs[0:HUB_ROWS]
    hubs = jnp.concatenate([hubs, pltpu.roll(hubs, HUBS_EACH, 0)], axis=1)
    high, low = split(nn(hubs.astype(BF16), weights_ref[2 * SELF_AT :, :]))
    owner = one_hot(wanted_ref[CAPACITY:FORWARD_ROWS, 0:1] == iota((HUB_ROWS, nodes), 1))
    out_ref[...] = base_ref[...] + tn(owner, high) + tn(owner, low)


def weight_outputs(samples_all, mine_ref, theirs_ref, first_self_ref, first_mean_ref, self_ref, mean_ref, loss_ref):
    unused, core = position()
    half = STACK_ROWS // CORES
    classes = self_ref.shape[0]
    spans = (
        (0, TILE, first_self_ref),
        (TILE, 2 * TILE, first_mean_ref),
        (SELF_AT, SELF_AT + classes, self_ref),
        (MEAN_AT, MEAN_AT + classes, mean_ref),
    )
    for n in range(PEERS):
        mine = mine_ref[n].astype(F32)[HUB_ROWS:]
        theirs = theirs_ref[n].astype(F32)[HUB_ROWS:]
        lanes = slice(TILE * (n // 8), TILE * (n // 8 + 1))
        for at, piece in (
            (PIECE * (n % 8), jnp.where(core == 0, mine, theirs)),
            (half + PIECE * (n % 8), jnp.where(core == 0, theirs, mine)),
        ):
            for start, end, out_ref in spans:
                low, high = max(start, at), min(end, at + PIECE)
                if low < high:
                    out_ref[low - start : high - start, lanes] = piece[low - at : high - at]
            if at == LOSS_AT and lanes.start == 0:
                loss_ref[...] = (piece[0:1, 0:1] + piece[1:2, 0:1] + piece[2:3, 0:1]) / samples_all


def shape(dims, dtype):
    return jax.ShapeDtypeStruct(dims, dtype)


def swap(values):
    return lax.all_to_all(values, "dev", split_axis=0, concat_axis=0, tiled=True)


def to_core(values):
    return lax.ppermute(values, "grp", [(i, i ^ 1) for i in range(CHIPS * CORES)])


def along_x(values, shift):
    every = CHIPS * CORES
    return lax.ppermute(values, "grp", [(i, (i + CORES * shift) % every) for i in range(every)])


def to_chips(values):
    return [along_x(values, shift) for shift in range(1, CHIPS)]


def on_device(
    features,
    hub_list,
    send_list,
    send_count,
    tile_dst,
    tile_src,
    tile_count,
    tile_adj,
    sample_ids,
    labels,
    first_self,
    first_mean,
    second_self,
    second_mean,
):
    nodes, inputs = features.shape
    width, classes = second_self.shape
    hubs = CHIPS * CORES * PEERS * HUBS_EACH
    edges = PEERS * CAPACITY
    table = nodes + hubs + edges
    padded = 2 * TILE
    samples_all = float(sample_ids.shape[1] * CHIPS * CORES * PEERS)

    slots = PEERS * FORWARD_ROWS

    def gather_hubs(arrived, beside):
        own = kernel_call(group_hubs, shape((GROUP_HUBS, inputs), BF16))(arrived)
        blocks = kernel_call(
            join_blocks,
            shape((CHIPS * GROUP_HUBS, inputs), BF16),
            in_specs=[VM] * CHIPS + [ANY] * len(beside),
        )(own, *to_chips(own), *beside)
        return blocks, to_core(blocks)

    rows = kernel_call(
        send_features,
        shape((slots, inputs), BF16),
        [
            pltpu.VMEM((nodes, inputs), BF16),
            pltpu.VMEM(send_list.shape[1:], I32),
            pltpu.VMEM(send_count.shape, I32),
            pltpu.SMEM(hub_list.shape, I32),
            pltpu.SemaphoreType.DMA((4,)),
        ],
        [HBM] * 4,
    )(*(pltpu.with_memory_space_constraint(operand, pltpu.HBM) for operand in (features, send_list, send_count, hub_list)))
    feature_arrived = swap(rows.reshape(PEERS, FORWARD_ROWS, inputs))
    raw = (second_self.T, second_mean.T)
    operands = (
        tile_adj, tile_dst, tile_src, tile_count, send_list[0], send_count, hub_list,
        first_self, first_mean, *raw,
    )
    dense, numbers, weights, wanted, picks = kernel_call(
        build_dense,
        (
            shape((nodes, table), BF16),
            shape((nodes, TILE), F32),
            shape((3 * padded, width), BF16),
            shape((FORWARD_ROWS, PEERS), I32),
            shape((slots, nodes), BF16),
        ),
        [
            pltpu.VMEM(tile_adj.shape, BF16),
            pltpu.SMEM(tile_dst.shape, I32),
            pltpu.SMEM(tile_src.shape, I32),
            pltpu.SMEM(tile_count.shape, I32),
            pltpu.VMEM(send_list.shape[1:], I32),
            pltpu.VMEM(send_count.shape, I32),
            pltpu.SMEM(hub_list.shape, I32),
            pltpu.VMEM(raw[0].shape, BF16),
            pltpu.VMEM(raw[1].shape, BF16),
            pltpu.SemaphoreType.DMA((len(operands),)),
        ],
        [HBM] * len(operands) + [ANY],
        flops=2 * nodes * table * TILE,
        moved=8 * MIB,
    )(
        *(
            operand if operand is tile_count else pltpu.with_memory_space_constraint(operand, pltpu.HBM)
            for operand in operands
        ),
        feature_arrived,
    )
    feature_hubs = gather_hubs(feature_arrived, [numbers])
    part = kernel_call(
        early_means,
        shape((nodes, inputs), F32),
        [pltpu.VMEM((table, inputs), BF16)],
        flops=2 * nodes * table * inputs,
        moved=4 * MIB,
    )(features, feature_arrived, dense, feature_hubs[0])
    mean_rows, rows = kernel_call(
        first_means, (shape((nodes, inputs), BF16), shape((slots, inputs), BF16))
    )(part, dense, numbers, picks, feature_hubs[1])
    mean_arrived = swap(rows.reshape(PEERS, FORWARD_ROWS, inputs))

    hidden, early_turned, early_source, part, own_logits = kernel_call(
        early_part,
        (
            shape((nodes, width), BF16),
            shape((2 * inputs, nodes + edges), BF16),
            shape((nodes + edges, width), BF16),
            shape((nodes, width), F32),
            shape((nodes, padded), F32),
        ),
        [pltpu.VMEM((nodes + edges, 2 * inputs), BF16)],
        limit=8,
        flops=6 * nodes * edges * width,
        moved=8 * MIB,
    )(features, feature_arrived, mean_rows, mean_arrived, dense, weights)
    mean_hubs = gather_hubs(mean_arrived, [own_logits])
    half = CHIPS * GROUP_HUBS
    own_turned, own_source, own_columns, part, times = kernel_call(
        own_hub_part,
        (
            shape((2 * inputs, half), BF16),
            shape((half, width), BF16),
            shape((nodes, half), BF16),
            shape((nodes, width), F32),
            shape((nodes, TILE), F32),
        ),
        [
            pltpu.VMEM(sample_ids.shape, I32),
            pltpu.VMEM((1, nodes), I32),
            pltpu.SemaphoreType.DMA((2,)),
        ],
        [VM] * 5 + [HBM] * 2,
        limit=6,
        flops=4 * nodes * half * width,
        moved=4 * MIB,
    )(
        dense, weights, part, feature_hubs[0], mean_hubs[0],
        *(pltpu.with_memory_space_constraint(operand, pltpu.HBM) for operand in (sample_ids, labels.reshape(1, nodes))),
    )
    base, edge_rows, mine, theirs = kernel_call(
        functools.partial(main_part, samples_all, classes),
        (
            shape((nodes, width), F32),
            shape((PEERS, EDGE_ROWS, TILE), BF16),
            shape((CORE_ROWS, TILE), BF16),
            shape((CORE_ROWS, TILE), BF16),
        ),
        [
            pltpu.VMEM((2 * inputs, half), BF16),
            pltpu.VMEM((half, width), BF16),
            pltpu.VMEM((nodes, half), BF16),
            pltpu.VMEM((nodes, padded), BF16),
            pltpu.VMEM((table, width), BF16),
            pltpu.VMEM((STACK_ROWS, width), F32),
        ],
        limit=20,
    )(
        early_turned, early_source, own_logits, own_turned, own_source, own_columns, part,
        dense, numbers, times, weights, feature_hubs[1], mean_hubs[1],
    )
    rows, *blocks = kernel_call(
        sum_cores, (shape((PEERS, BACK_ROWS, TILE), BF16),) + (shape((CHIP_HUBS, TILE), BF16),) * CHIPS
    )(mine, to_core(theirs), edge_rows)
    arrived = swap(rows)
    sums, *sent = kernel_call(
        sum_peers, (shape((PIECE, TILE), F32),) + (shape((CHIP_ROWS, TILE), BF16),) * (CHIPS - 1)
    )(arrived, *blocks[1:])
    sent = [along_x(block, -1 - i) for i, block in enumerate(sent)]
    base = kernel_call(
        return_edges,
        shape((nodes, width), F32),
        [pltpu.VMEM((slots, padded), BF16), pltpu.VMEM((slots, nodes), BF16)],
        limit=6,
        flops=2 * nodes * (edges * padded + width * padded),
        moved=4 * MIB,
    )(base, arrived, wanted, weights)
    pieces = kernel_call(
        sum_chips,
        shape((PEERS, LAST_ROWS, TILE), BF16),
        in_specs=[VM] * (CHIPS + 1) + [ANY],
    )(sums, blocks[0], *sent, base)
    pieces = swap(pieces)
    grad_hidden = kernel_call(
        return_hubs,
        shape((nodes, width), F32),
        flops=4 * nodes * padded * width,
        moved=4 * MIB,
    )(base, pieces, wanted, weights)
    first_self_sum, first_mean_sum, self_sum, mean_sum, loss = kernel_call(
        functools.partial(weight_outputs, samples_all),
        (
            shape(first_self.shape, F32),
            shape(first_mean.shape, F32),
            shape((classes, width), F32),
            shape((classes, width), F32),
            shape((1, 1), F32),
        ),
    )(pieces, to_core(pieces))
    return hidden, grad_hidden, loss[0, 0], first_self_sum, first_mean_sum, self_sum.T, mean_sum.T


def solution(mesh):
    both = ("grp", "dev")
    placed = (
        P(both, None),
        P(both, None),
        P(both, None, None),
        P(both, None),
        P(both, None),
        P(both, None),
        P(both),
        P(both, None, None),
        P(both, None),
        P(both),
        P(),
        P(),
        P(),
        P(),
    )
    return jax.shard_map(
        on_device,
        mesh=mesh,
        in_specs=placed,
        out_specs=(P(both, None), P(both, None), P(), P(), P(), P(), P()),
        check_vma=False,
    )
```

```python
import functools

import jax
import jax.numpy as jnp
from jax import lax
from jax.experimental import pallas as pl
from jax.experimental.pallas import tpu as pltpu
from jax.sharding import PartitionSpec as P

F32 = jnp.float32
BF16 = jnp.bfloat16
I32 = jnp.int32
MIB = 1 << 20
TILE = 128
HALF = 64
PEERS = 32
CHIPS = 4
CORES = 2
HUBS_EACH = 4
CAPACITY = 32
GROUP_HUBS = PEERS * HUBS_EACH
FORWARD_ROWS = CAPACITY + 8
PEER_HUBS = CORES * CHIPS * HUBS_EACH
EDGE_ROWS = CAPACITY + CAPACITY // 2
HUB_ROWS = 2 * HUBS_EACH
CHIP_HUBS = PEERS * HUB_ROWS
STACK_ROWS = 640
SELF_AT = 256
LOSS_AT = 440
MEAN_AT = 448
CLASS_ROWS = 176
PIECE = STACK_ROWS // CORES * 4 // PEERS
BACK_ROWS = EDGE_ROWS + PIECE
CORE_ROWS = CHIPS * CHIP_HUBS + PEERS * PIECE
CHIP_ROWS = CHIP_HUBS + 2 * PIECE
LAST_ROWS = HUB_ROWS + PIECE

VM = pl.BlockSpec(memory_space=pltpu.VMEM)
SM = pl.BlockSpec(memory_space=pltpu.SMEM)
ANY = pl.BlockSpec(memory_space=pl.ANY)
HBM = pl.BlockSpec(memory_space=pltpu.HBM)


def nn(left, right):
    return jnp.dot(left, right, preferred_element_type=F32)


def nt(left, right):
    return lax.dot_general(left, right, (((1,), (1,)), ((), ())), preferred_element_type=F32)


def tn(left, right):
    return lax.dot_general(left, right, (((0,), (0,)), ((), ())), preferred_element_type=F32)


def split(values):
    high = values.astype(BF16)
    low = (values - high.astype(F32)).astype(BF16)
    return high, low


def one_hot(hit):
    return jnp.where(hit, 1.0, 0.0).astype(BF16)


def iota(dims, axis):
    return lax.broadcasted_iota(I32, dims, axis)


def kernel_call(body, outs, scratch=(), in_specs=None, limit=5, flops=0, moved=0):
    placed = {} if in_specs is None else {"in_specs": in_specs}
    return pl.pallas_call(
        body,
        out_shape=outs,
        **placed,
        scratch_shapes=list(scratch),
        compiler_params=pltpu.CompilerParams(vmem_limit_bytes=limit * MIB),
        cost_estimate=pl.CostEstimate(flops=flops, bytes_accessed=moved, transcendentals=0),
    )


def position():
    group = lax.axis_index("grp")
    return group // CORES, group % CORES


def fetch(pairs, sems):
    loads = [pltpu.make_async_copy(source, target, sems.at[i]) for i, (source, target) in enumerate(pairs)]
    for load in loads:
        load.start()
    return loads


def wanted_rows(send, counts, hub_ref):
    send = jnp.transpose(send)
    send = jnp.where(iota(send.shape, 0) < counts, send, -1)
    row = iota((FORWARD_ROWS - CAPACITY, PEERS), 0)
    hubs = jnp.full(row.shape, -1, I32)
    for k in range(HUBS_EACH):
        hubs = jnp.where(row == k, hub_ref[0, k], hubs)
    return jnp.concatenate([send, hubs], axis=0)


def pick_matrix(wanted, pick_ref):
    lane = iota((2 * FORWARD_ROWS, pick_ref.shape[1]), 1)
    for n in range(0, PEERS, 2):
        pair = jnp.concatenate([wanted[:, n : n + 1], wanted[:, n + 1 : n + 2]], axis=0)
        pick_ref[n * FORWARD_ROWS : (n + 2) * FORWARD_ROWS, :] = one_hot(pair == lane)


def send_features(
    features_any, send_any, count_any, hub_any, out_ref, features_ref, send_ref, count_ref, hub_ref, sems
):
    loads = fetch(
        (
            (send_any.at[0], send_ref),
            (count_any, count_ref),
            (hub_any, hub_ref),
            (features_any, features_ref),
        ),
        sems,
    )
    for load in loads[:-1]:
        load.wait()
    wanted = wanted_rows(send_ref[...], count_ref[...], hub_ref)
    loads[-1].wait()
    features = features_ref[...]
    lane = iota((8 * FORWARD_ROWS, features.shape[0]), 1)
    for n in range(0, PEERS, 8):
        rows = jnp.concatenate([wanted[:, i : i + 1] for i in range(n, n + 8)], axis=0)
        out_ref[n * FORWARD_ROWS : (n + 8) * FORWARD_ROWS, :] = nn(one_hot(rows == lane), features).astype(BF16)


def build_dense(*refs):
    count = 11
    sources, refs = refs[:count], refs[count + 1 :]
    dense_ref, numbers_ref, weights_ref, wanted_ref, pick_ref, *places, sems = refs
    (
        adj_ref, dst_ref, src_ref, live_ref, send_ref, count_ref, hub_ref, raw_self_ref, raw_mean_ref,
    ) = places
    targets = (
        adj_ref, dst_ref, src_ref, live_ref, send_ref, count_ref, hub_ref,
        weights_ref.at[pl.ds(0, TILE)], weights_ref.at[pl.ds(TILE, TILE)], raw_self_ref, raw_mean_ref,
    )
    loads = fetch(zip(sources, targets), sems)
    dense_ref[...] = jnp.zeros_like(dense_ref)
    weights_ref[SELF_AT:, :] = jnp.zeros((weights_ref.shape[0] - SELF_AT, weights_ref.shape[1]), BF16)
    for load in loads:
        load.wait()

    def add(t, carry):
        rows = pl.ds(pl.multiple_of(dst_ref[0, t] * TILE, TILE), TILE)
        columns = pl.ds(pl.multiple_of(src_ref[0, t] * TILE, TILE), TILE)
        dense_ref[rows, columns] += adj_ref[t]
        return carry

    lax.fori_loop(0, live_ref[0], add, 0)
    classes = raw_self_ref.shape[0]
    weights_ref[SELF_AT : SELF_AT + classes, :] = raw_self_ref[...]
    weights_ref[2 * SELF_AT : 2 * SELF_AT + classes, :] = raw_mean_ref[...]
    wanted = wanted_rows(send_ref[...], count_ref[...], hub_ref)
    wanted_ref[...] = wanted
    pick_matrix(wanted, pick_ref)
    degree = jnp.maximum(nn(dense_ref[...], jnp.ones((dense_ref.shape[1], TILE), BF16)), 1.0)
    numbers_ref[...] = degree


def group_hubs(arrived_ref, out_ref):
    low = iota((8, TILE), 0) < HUBS_EACH
    rows = []
    for n in range(0, PEERS, 2):
        first = arrived_ref[n, CAPACITY:FORWARD_ROWS, :].astype(F32)
        second = arrived_ref[n + 1, CAPACITY:FORWARD_ROWS, :].astype(F32)
        rows.append(jnp.where(low, first, pltpu.roll(second, HUBS_EACH, 0)))
    out_ref[...] = jnp.concatenate(rows, axis=0).astype(BF16)


def join_blocks(*refs):
    out_ref = refs[-1]
    for i in range(CHIPS):
        out_ref[i * GROUP_HUBS : (i + 1) * GROUP_HUBS, :] = refs[i][...]


def place_hubs(table_ref, start, hub_refs, lanes):
    chip, core = position()
    for there, hub_ref in zip((core, 1 - core), hub_refs):
        for i in range(CHIPS):
            other = (chip + CHIPS - i) % CHIPS
            at = start + (other * CORES + there) * GROUP_HUBS
            block = hub_ref[i * GROUP_HUBS : (i + 1) * GROUP_HUBS, :]
            table_ref[pl.ds(pl.multiple_of(at, GROUP_HUBS), GROUP_HUBS), lanes] = block


def early_means(features_ref, arrived_ref, dense_ref, own_hub_ref, part_ref, table_ref):
    nodes = features_ref.shape[0]
    edge_at = nodes + CORES * CHIPS * GROUP_HUBS
    table_ref[0:nodes, :] = features_ref[...]
    table_ref[nodes:edge_at, :] = jnp.zeros((edge_at - nodes, TILE), BF16)
    place_hubs(table_ref, nodes, (own_hub_ref,), slice(0, TILE))
    for n in range(PEERS):
        at = edge_at + n * CAPACITY
        table_ref[at : at + CAPACITY, :] = arrived_ref[n, 0:CAPACITY, :]
    part_ref[...] = nn(dense_ref[...], table_ref[...])


def first_means(part_ref, dense_ref, numbers_ref, pick_ref, other_hub_ref, mean_ref, out_ref):
    nodes = part_ref.shape[0]
    chip, core = position()
    total = part_ref[...]
    for i in range(CHIPS):
        other = (chip + CHIPS - i) % CHIPS
        at = nodes + (other * CORES + 1 - core) * GROUP_HUBS
        columns = dense_ref[:, pl.ds(pl.multiple_of(at, GROUP_HUBS), GROUP_HUBS)]
        total += nn(columns, other_hub_ref[i * GROUP_HUBS : (i + 1) * GROUP_HUBS, :])
    mean = (total / numbers_ref[:, 0:1]).astype(BF16)
    mean_ref[...] = mean
    out_ref[...] = nn(pick_ref[...], mean).astype(BF16)


def join_rests(first, second):
    return first + pltpu.roll(second, HALF, 1)


def part_rests(packed):
    low = iota(packed.shape, 1) < HALF
    return jnp.where(low, packed, 0.0), jnp.where(low, pltpu.roll(packed, HALF, 1), 0.0)


def early_part(
    features_ref, feature_arrived_ref, mean_ref, arrived_ref, dense_ref, weights_ref, sample_any, label_any,
    hidden_ref, turned_ref, source_ref, part_ref, logits_ref, times_ref, table_ref, sample_ref, label_ref, sems,
):
    loads = fetch(((sample_any, sample_ref), (label_any, label_ref)), sems)
    nodes, width = hidden_ref.shape
    edges = PEERS * CAPACITY
    edge_at = dense_ref.shape[1] - edges
    table_ref[0:nodes, 0:TILE] = features_ref[...]
    table_ref[0:nodes, TILE:] = mean_ref[...]
    for n in range(PEERS):
        at = nodes + n * CAPACITY
        table_ref[at : at + CAPACITY, 0:TILE] = feature_arrived_ref[n, 0:CAPACITY, :]
        table_ref[at : at + CAPACITY, TILE:] = arrived_ref[n, 0:CAPACITY, :]
    for at in range(0, nodes + edges, nodes):
        rows = slice(at, at + nodes)
        linear = nn(table_ref[rows, :], weights_ref[0:SELF_AT, :])
        source_ref[rows, :] = jnp.maximum(linear, 0.0).astype(BF16)
        turned_ref[:, rows] = jnp.transpose(table_ref[rows, :])
    hidden = source_ref[0:nodes, :]
    hidden_ref[...] = hidden
    part_ref[...] = nn(dense_ref[:, 0:nodes], hidden) + nn(dense_ref[:, edge_at:], source_ref[nodes:, :])
    logits_ref[...] = nt(hidden, weights_ref[SELF_AT : 2 * SELF_AT, :])
    for load in loads:
        load.wait()
    node = iota((nodes, sample_ref.shape[1]), 0)
    times = jnp.sum(jnp.where(node == sample_ref[...], 1.0, 0.0), axis=1, keepdims=True)
    label = jnp.transpose(jnp.broadcast_to(label_ref[...], (8, nodes)))[:, 0:1]
    times_ref[...] = jnp.where(iota(times_ref.shape, 1) == 0, times, label.astype(F32))


def hub_part(
    dense_ref, weights_ref, features, means, others, turned_ref, source_ref, columns_ref
):
    nodes = dense_ref.shape[0]
    chip, core = position()
    there = 1 - core if others else core
    table = jnp.concatenate([features, means], axis=1)
    turned_ref[...] = jnp.transpose(table)
    source_ref[...] = jnp.maximum(nn(table, weights_ref[0:SELF_AT, :]), 0.0).astype(BF16)
    for i in range(CHIPS):
        other = (chip + CHIPS - i) % CHIPS
        at = pl.multiple_of(nodes + (other * CORES + there) * GROUP_HUBS, GROUP_HUBS)
        columns_ref[:, i * GROUP_HUBS : (i + 1) * GROUP_HUBS] = dense_ref[:, pl.ds(at, GROUP_HUBS)]
    return nn(columns_ref[...], source_ref[...])


def own_hub_part(
    dense_ref, weights_ref, part_ref, feature_ref, mean_ref, turned_ref, source_ref, columns_ref, out_ref
):
    total = hub_part(
        dense_ref, weights_ref, feature_ref[...], mean_ref[...], False, turned_ref, source_ref, columns_ref
    )
    out_ref[...] = part_ref[...] + total


def main_part(
    samples_all, classes,
    early_turned_ref, early_source_ref, logits_ref, own_turned_ref, own_source_ref, own_columns_ref, part_ref,
    dense_ref, numbers_ref, times_ref, weights_ref, feature_ref, mean_ref,
    base_ref, edge_ref, mine_ref, theirs_ref,
    other_turned_ref, other_source_ref, other_columns_ref, scaled_ref, masked_ref, stack_ref,
):
    nodes, width = base_ref.shape
    padded = SELF_AT
    self_rows = slice(SELF_AT, 2 * SELF_AT)
    mean_rows = slice(2 * SELF_AT, 3 * SELF_AT)
    edge_at = dense_ref.shape[1] - PEERS * CAPACITY
    total = hub_part(
        dense_ref, weights_ref, feature_ref[...], mean_ref[...], True,
        other_turned_ref, other_source_ref, other_columns_ref,
    )
    hidden = early_source_ref[0:nodes, :]
    degree = numbers_ref[:, 0:1]
    times = times_ref[:, 0:1]
    label = times_ref[:, 1:2].astype(I32)
    mean = ((part_ref[...] + total) / degree).astype(BF16)
    logits = logits_ref[...] + nt(mean, weights_ref[mean_rows, :])

    lane = iota((nodes, padded), 1)
    real = lane < classes
    onehot = jnp.where(lane == label, 1.0, 0.0)
    top = jnp.max(jnp.where(real, logits, -jnp.inf), axis=1, keepdims=True)
    shifted = logits - top
    powers = jnp.where(real, jnp.exp(shifted), 0.0)
    total = jnp.sum(powers, axis=1, keepdims=True)
    chosen = jnp.sum(onehot * shifted, axis=1, keepdims=True)
    loss = jnp.sum(times * (jnp.log(total) - chosen), axis=0, keepdims=True)
    upstream = times * ((powers / total - onehot) / samples_all)
    upstream = upstream.astype(BF16)
    scaled_ref[...] = (upstream.astype(F32) / degree).astype(BF16)

    def back(columns):
        found = tn(columns, scaled_ref[...])
        return found, nn(found.astype(BF16), weights_ref[mean_rows, :])

    def mask(at, source, grad):
        masked_ref[at : at + nodes, :] = jnp.where(source > 0, grad, 0.0).astype(BF16)

    low = iota((8, TILE), 0) < HUBS_EACH
    hub_at = nodes + PEERS * CAPACITY
    for i, (columns_ref, source_ref, out_ref) in enumerate(
        ((own_columns_ref, own_source_ref, mine_ref), (other_columns_ref, other_source_ref, theirs_ref))
    ):
        found, spread = back(columns_ref[...])
        mask(hub_at + i * nodes, source_ref[...], spread)
        for block in range(CHIPS):
            for n in range(0, PEERS, 2):
                at = block * GROUP_HUBS + n * HUBS_EACH
                mains = found[at : at + 8, 0:TILE]
                rests = found[at : at + 8, TILE:]
                pair = (
                    jnp.where(low, mains, pltpu.roll(rests, HUBS_EACH, 0)),
                    jnp.where(low, pltpu.roll(mains, HUBS_EACH, 0), rests),
                )
                at = block * CHIP_HUBS + n * HUB_ROWS
                out_ref[at : at + 2 * HUB_ROWS, :] = jnp.concatenate(pair, axis=0).astype(BF16)

    unused, spread = back(dense_ref[:, 0:nodes])
    base = nn(upstream, weights_ref[self_rows, :]) + spread
    base_ref[...] = base
    mask(0, hidden, base)
    each = nodes // CAPACITY
    for i in range(PEERS // each):
        found, spread = back(dense_ref[:, edge_at + i * nodes : edge_at + (i + 1) * nodes])
        at = (i + 1) * nodes
        mask(at, early_source_ref[at : at + nodes, :], spread)
        for p in range(each):
            at = p * CAPACITY
            rest = found[at : at + CAPACITY, TILE:]
            edge_ref[i * each + p, 0:CAPACITY, :] = found[at : at + CAPACITY, 0:TILE].astype(BF16)
            edge_ref[i * each + p, CAPACITY:EDGE_ROWS, :] = join_rests(
                rest[0 : CAPACITY // 2], rest[CAPACITY // 2 :]
            ).astype(BF16)

    stack_ref[SELF_AT:, :] = jnp.zeros((STACK_ROWS - SELF_AT, width), F32)
    upstream_turned = jnp.transpose(upstream)
    stack_ref[SELF_AT : SELF_AT + CLASS_ROWS, :] = nn(upstream_turned, hidden)[0:CLASS_ROWS]
    stack_ref[MEAN_AT : MEAN_AT + CLASS_ROWS, :] = nn(upstream_turned, mean)[0:CLASS_ROWS]
    loss_high = loss.astype(BF16).astype(F32)
    place = iota((8, width), 0)
    marks = jnp.where(place == 0, loss_high, 0.0)
    stack_ref[LOSS_AT : LOSS_AT + 8, :] = jnp.where(place == 1, loss - loss_high, marks)
    stack_ref[0:SELF_AT, :] = (
        nn(early_turned_ref[...], masked_ref[0:hub_at, :])
        + nn(own_turned_ref[...], masked_ref[hub_at : hub_at + nodes, :])
        + nn(other_turned_ref[...], masked_ref[hub_at + nodes :, :])
    )
    unused, core = position()
    for there, out_ref in ((core, mine_ref), (1 - core, theirs_ref)):
        for n in range(0, PEERS, 2):
            at = there * (STACK_ROWS // CORES) + PIECE * (n % 8)
            lanes = slice(TILE * (n // 8), TILE * (n // 8 + 1))
            rows = stack_ref[pl.ds(pl.multiple_of(at, 16), 2 * PIECE), lanes]
            at = CHIPS * CHIP_HUBS + n * PIECE
            out_ref[at : at + 2 * PIECE, :] = rows.astype(BF16)


def sum_cores(mine_ref, arrived_ref, edge_ref, out_ref, *hub_refs):
    out_ref[:, 0:EDGE_ROWS, :] = edge_ref[...]
    total = mine_ref[...].astype(F32) + arrived_ref[...].astype(F32)
    for block, hub_ref in enumerate(hub_refs):
        hub_ref[...] = total[block * CHIP_HUBS : (block + 1) * CHIP_HUBS].astype(BF16)
    for n in range(PEERS):
        at = CHIPS * CHIP_HUBS + n * PIECE
        out_ref[n, EDGE_ROWS:BACK_ROWS, :] = total[at : at + PIECE].astype(BF16)


def sum_peers(arrived_ref, *refs):
    hub_refs, (sum_ref, *out_refs) = refs[: CHIPS - 1], refs[CHIPS - 1 :]
    total = arrived_ref[0, EDGE_ROWS:BACK_ROWS, :].astype(F32)
    for n in range(1, PEERS):
        total += arrived_ref[n, EDGE_ROWS:BACK_ROWS, :].astype(F32)
    high = total.astype(BF16).astype(F32)
    low = (total - high).astype(BF16).astype(F32)
    sum_ref[...] = high + low
    parts = jnp.concatenate([high, low], axis=0).astype(BF16)
    for hub_ref, out_ref in zip(hub_refs, out_refs):
        out_ref[0:CHIP_HUBS, :] = hub_ref[...]
        out_ref[CHIP_HUBS:CHIP_ROWS, :] = parts


def return_edges(base_ref, arrived_ref, wanted_ref, weights_ref, out_ref, found_ref, pick_ref):
    pick_matrix(wanted_ref[...], pick_ref)
    found_ref[...] = jnp.zeros_like(found_ref)
    for n in range(PEERS):
        at = n * FORWARD_ROWS
        first, second = part_rests(arrived_ref[n, CAPACITY:EDGE_ROWS, :].astype(F32))
        rest = jnp.concatenate([first, second], axis=0).astype(BF16)
        found_ref[at : at + CAPACITY, 0:TILE] = arrived_ref[n, 0:CAPACITY, :]
        found_ref[at : at + CAPACITY, TILE:] = rest
    rows = tn(pick_ref[...], found_ref[...])
    out_ref[...] = base_ref[...] + nn(rows.astype(BF16), weights_ref[2 * SELF_AT :, :])


def sum_chips(sum_ref, own_ref, *refs):
    sent_refs, out_ref = refs[: CHIPS - 1], refs[-1]
    hubs = own_ref[...].astype(F32)
    pieces = [sum_ref[...]]
    for sent_ref in sent_refs:
        rows = sent_ref[...].astype(F32)
        hubs += rows[0:CHIP_HUBS]
        pieces.append(rows[CHIP_HUBS : CHIP_HUBS + PIECE] + rows[CHIP_HUBS + PIECE : CHIP_ROWS])
    piece = (pieces[0] + pieces[2]) + (pieces[1] + pieces[3])
    unused, core = position()
    holder = (core == LOSS_AT * CORES // STACK_ROWS) & (lax.axis_index("dev") == LOSS_AT % (STACK_ROWS // CORES) // PIECE)
    rest = piece[0:1] - piece[0:1].astype(BF16).astype(F32)
    row = iota(piece.shape, 0)
    piece = jnp.where((row == 2) & holder, rest, piece)
    tail = piece[8:PIECE].astype(BF16)
    for n in range(PEERS):
        head = jnp.concatenate([hubs[n * HUB_ROWS : (n + 1) * HUB_ROWS], piece[0:8]], axis=0)
        out_ref[n, 0:16, :] = head.astype(BF16)
        out_ref[n, 16:LAST_ROWS, :] = tail


def return_hubs(base_ref, arrived_ref, wanted_ref, weights_ref, out_ref):
    nodes = out_ref.shape[0]
    hubs = arrived_ref[0, 0:16, :].astype(F32)
    for n in range(1, PEERS):
        hubs += arrived_ref[n, 0:16, :].astype(F32)
    hubs = hubs[0:HUB_ROWS]
    hubs = jnp.concatenate([hubs, pltpu.roll(hubs, HUBS_EACH, 0)], axis=1)
    high, low = split(nn(hubs.astype(BF16), weights_ref[2 * SELF_AT :, :]))
    owner = one_hot(wanted_ref[CAPACITY:FORWARD_ROWS, 0:1] == iota((HUB_ROWS, nodes), 1))
    out_ref[...] = base_ref[...] + tn(owner, high) + tn(owner, low)


def weight_outputs(samples_all, mine_ref, theirs_ref, first_self_ref, first_mean_ref, self_ref, mean_ref, loss_ref):
    unused, core = position()
    half = STACK_ROWS // CORES
    classes = self_ref.shape[0]
    spans = (
        (0, TILE, first_self_ref),
        (TILE, 2 * TILE, first_mean_ref),
        (SELF_AT, SELF_AT + classes, self_ref),
        (MEAN_AT, MEAN_AT + classes, mean_ref),
    )
    for n in range(PEERS):
        mine = mine_ref[n].astype(F32)[HUB_ROWS:]
        theirs = theirs_ref[n].astype(F32)[HUB_ROWS:]
        lanes = slice(TILE * (n // 8), TILE * (n // 8 + 1))
        for at, piece in (
            (PIECE * (n % 8), jnp.where(core == 0, mine, theirs)),
            (half + PIECE * (n % 8), jnp.where(core == 0, theirs, mine)),
        ):
            for start, end, out_ref in spans:
                low, high = max(start, at), min(end, at + PIECE)
                if low < high:
                    out_ref[low - start : high - start, lanes] = piece[low - at : high - at]
            if at == LOSS_AT and lanes.start == 0:
                loss_ref[...] = (piece[0:1, 0:1] + piece[1:2, 0:1] + piece[2:3, 0:1]) / samples_all


def shape(dims, dtype):
    return jax.ShapeDtypeStruct(dims, dtype)


def swap(values):
    return lax.all_to_all(values, "dev", split_axis=0, concat_axis=0, tiled=True)


def to_core(values):
    return lax.ppermute(values, "grp", [(i, i ^ 1) for i in range(CHIPS * CORES)])


def along_x(values, shift):
    every = CHIPS * CORES
    return lax.ppermute(values, "grp", [(i, (i + CORES * shift) % every) for i in range(every)])


def to_chips(values):
    return [along_x(values, shift) for shift in range(1, CHIPS)]


def on_device(
    features,
    hub_list,
    send_list,
    send_count,
    tile_dst,
    tile_src,
    tile_count,
    tile_adj,
    sample_ids,
    labels,
    first_self,
    first_mean,
    second_self,
    second_mean,
):
    nodes, inputs = features.shape
    width, classes = second_self.shape
    hubs = CHIPS * CORES * PEERS * HUBS_EACH
    edges = PEERS * CAPACITY
    table = nodes + hubs + edges
    padded = 2 * TILE
    samples_all = float(sample_ids.shape[1] * CHIPS * CORES * PEERS)

    slots = PEERS * FORWARD_ROWS

    def gather_hubs(arrived, beside):
        own = kernel_call(group_hubs, shape((GROUP_HUBS, inputs), BF16))(arrived)
        blocks = kernel_call(
            join_blocks,
            shape((CHIPS * GROUP_HUBS, inputs), BF16),
            in_specs=[VM] * CHIPS + [ANY] * len(beside),
        )(own, *to_chips(own), *beside)
        return blocks, to_core(blocks)

    rows = kernel_call(
        send_features,
        shape((slots, inputs), BF16),
        [
            pltpu.VMEM((nodes, inputs), BF16),
            pltpu.VMEM(send_list.shape[1:], I32),
            pltpu.VMEM(send_count.shape, I32),
            pltpu.SMEM(hub_list.shape, I32),
            pltpu.SemaphoreType.DMA((4,)),
        ],
        [HBM] * 4,
    )(*(pltpu.with_memory_space_constraint(operand, pltpu.HBM) for operand in (features, send_list, send_count, hub_list)))
    feature_arrived = swap(rows.reshape(PEERS, FORWARD_ROWS, inputs))
    raw = (second_self.T, second_mean.T)
    operands = (
        tile_adj, tile_dst, tile_src, tile_count, send_list[0], send_count, hub_list,
        first_self, first_mean, *raw,
    )
    dense, numbers, weights, wanted, picks = kernel_call(
        build_dense,
        (
            shape((nodes, table), BF16),
            shape((nodes, TILE), F32),
            shape((3 * padded, width), BF16),
            shape((FORWARD_ROWS, PEERS), I32),
            shape((slots, nodes), BF16),
        ),
        [
            pltpu.VMEM(tile_adj.shape, BF16),
            pltpu.SMEM(tile_dst.shape, I32),
            pltpu.SMEM(tile_src.shape, I32),
            pltpu.SMEM(tile_count.shape, I32),
            pltpu.VMEM(send_list.shape[1:], I32),
            pltpu.VMEM(send_count.shape, I32),
            pltpu.SMEM(hub_list.shape, I32),
            pltpu.VMEM(raw[0].shape, BF16),
            pltpu.VMEM(raw[1].shape, BF16),
            pltpu.SemaphoreType.DMA((len(operands),)),
        ],
        [HBM] * len(operands) + [ANY],
        flops=2 * nodes * table * TILE,
        moved=8 * MIB,
    )(
        *(
            operand if operand is tile_count else pltpu.with_memory_space_constraint(operand, pltpu.HBM)
            for operand in operands
        ),
        feature_arrived,
    )
    feature_hubs = gather_hubs(feature_arrived, [numbers])
    part = kernel_call(
        early_means,
        shape((nodes, inputs), F32),
        [pltpu.VMEM((table, inputs), BF16)],
        flops=2 * nodes * table * inputs,
        moved=4 * MIB,
    )(features, feature_arrived, dense, feature_hubs[0])
    mean_rows, rows = kernel_call(
        first_means, (shape((nodes, inputs), BF16), shape((slots, inputs), BF16))
    )(part, dense, numbers, picks, feature_hubs[1])
    mean_arrived = swap(rows.reshape(PEERS, FORWARD_ROWS, inputs))

    hidden, early_turned, early_source, part, own_logits, times = kernel_call(
        early_part,
        (
            shape((nodes, width), BF16),
            shape((2 * inputs, nodes + edges), BF16),
            shape((nodes + edges, width), BF16),
            shape((nodes, width), F32),
            shape((nodes, padded), F32),
            shape((nodes, TILE), F32),
        ),
        [
            pltpu.VMEM((nodes + edges, 2 * inputs), BF16),
            pltpu.VMEM(sample_ids.shape, I32),
            pltpu.VMEM((1, nodes), I32),
            pltpu.SemaphoreType.DMA((2,)),
        ],
        [VM] * 6 + [HBM] * 2,
        limit=8,
        flops=6 * nodes * edges * width,
        moved=8 * MIB,
    )(
        features, feature_arrived, mean_rows, mean_arrived, dense, weights,
        *(pltpu.with_memory_space_constraint(operand, pltpu.HBM) for operand in (sample_ids, labels.reshape(1, nodes))),
    )
    mean_hubs = gather_hubs(mean_arrived, [own_logits])
    half = CHIPS * GROUP_HUBS
    own_turned, own_source, own_columns, part = kernel_call(
        own_hub_part,
        (
            shape((2 * inputs, half), BF16),
            shape((half, width), BF16),
            shape((nodes, half), BF16),
            shape((nodes, width), F32),
        ),
        limit=6,
        flops=4 * nodes * half * width,
        moved=4 * MIB,
    )(dense, weights, part, feature_hubs[0], mean_hubs[0])
    base, edge_rows, mine, theirs = kernel_call(
        functools.partial(main_part, samples_all, classes),
        (
            shape((nodes, width), F32),
            shape((PEERS, EDGE_ROWS, TILE), BF16),
            shape((CORE_ROWS, TILE), BF16),
            shape((CORE_ROWS, TILE), BF16),
        ),
        [
            pltpu.VMEM((2 * inputs, half), BF16),
            pltpu.VMEM((half, width), BF16),
            pltpu.VMEM((nodes, half), BF16),
            pltpu.VMEM((nodes, padded), BF16),
            pltpu.VMEM((table, width), BF16),
            pltpu.VMEM((STACK_ROWS, width), F32),
        ],
        limit=20,
    )(
        early_turned, early_source, own_logits, own_turned, own_source, own_columns, part,
        dense, numbers, times, weights, feature_hubs[1], mean_hubs[1],
    )
    rows, *blocks = kernel_call(
        sum_cores, (shape((PEERS, BACK_ROWS, TILE), BF16),) + (shape((CHIP_HUBS, TILE), BF16),) * CHIPS
    )(mine, to_core(theirs), edge_rows)
    arrived = swap(rows)
    sums, *sent = kernel_call(
        sum_peers, (shape((PIECE, TILE), F32),) + (shape((CHIP_ROWS, TILE), BF16),) * (CHIPS - 1)
    )(arrived, *blocks[1:])
    sent = [along_x(block, -1 - i) for i, block in enumerate(sent)]
    base = kernel_call(
        return_edges,
        shape((nodes, width), F32),
        [pltpu.VMEM((slots, padded), BF16), pltpu.VMEM((slots, nodes), BF16)],
        limit=6,
        flops=2 * nodes * (edges * padded + width * padded),
        moved=4 * MIB,
    )(base, arrived, wanted, weights)
    pieces = kernel_call(
        sum_chips,
        shape((PEERS, LAST_ROWS, TILE), BF16),
        in_specs=[VM] * (CHIPS + 1) + [ANY],
    )(sums, blocks[0], *sent, base)
    pieces = swap(pieces)
    grad_hidden = kernel_call(
        return_hubs,
        shape((nodes, width), F32),
        flops=4 * nodes * padded * width,
        moved=4 * MIB,
    )(base, pieces, wanted, weights)
    first_self_sum, first_mean_sum, self_sum, mean_sum, loss = kernel_call(
        functools.partial(weight_outputs, samples_all),
        (
            shape(first_self.shape, F32),
            shape(first_mean.shape, F32),
            shape((classes, width), F32),
            shape((classes, width), F32),
            shape((1, 1), F32),
        ),
    )(pieces, to_core(pieces))
    return hidden, grad_hidden, loss[0, 0], first_self_sum, first_mean_sum, self_sum.T, mean_sum.T


def solution(mesh):
    both = ("grp", "dev")
    placed = (
        P(both, None),
        P(both, None),
        P(both, None, None),
        P(both, None),
        P(both, None),
        P(both, None),
        P(both),
        P(both, None, None),
        P(both, None),
        P(both),
        P(),
        P(),
        P(),
        P(),
    )
    return jax.shard_map(
        on_device,
        mesh=mesh,
        in_specs=placed,
        out_specs=(P(both, None), P(both, None), P(), P(), P(), P(), P()),
        check_vma=False,
    )
```
